512 devices in a mesh: dp: 32 (over x_hi, z, core), graph: 16 (over y, x_lo).
Axes of the slice: x: 4 (x_hi: 2, x_lo: 2; x = x_hi * 2 + x_lo), y: 8, z: 8, core: 2. Of those that a mesh axis runs over, the one named last changes fastest.
Arguments:
- embeddings: bfloat16 [32, 64, 49, 128], P('dp', 'graph'), may hold values from -6 to 6
- atom_counts: int32 [32], P('dp'), may hold values from 32 to 64, as said below
- edge_counts: int32 [32, 16], P('dp', 'graph'), may hold values from 1 to 128, 1024 in all within a row
- source: int32 [32, 2048], P('dp', 'graph'), may hold values from 0 to 63, as said below
- target: int32 [32, 2048], P('dp', 'graph'), may hold values from 0 to 63, as said below
- wigner: bfloat16 [32, 29, 49, 2048], P('dp', None, None, 'graph'), may hold values from -4 to 4, as said below
- cotangent: float32 [32, 64, 49, 128], P('dp', 'graph'), may hold values from -6 to 6
- w_zero: bfloat16 [896, 896], P('graph', 'dp'), may hold values from -0.1875 to 0.1875
- w_one_real: bfloat16 [768, 768], P('graph', 'dp'), may hold values from -0.15625 to 0.15625
- w_one_imag: bfloat16 [768, 768], P('graph', 'dp'), may hold values from -0.15625 to 0.15625
- w_two_real: bfloat16 [640, 640], P('graph', 'dp'), may hold values from -0.15625 to 0.15625
- w_two_imag: bfloat16 [640, 640], P('graph', 'dp'), may hold values from -0.15625 to 0.15625
- attention: bfloat16 [128, 8], replicated, may hold values from -1 to 1
Outputs:
- node_update: bfloat16 [32, 64, 49, 128], P('dp', 'graph')
- grad_nodes: bfloat16 [32, 64, 49, 128], P('dp', 'graph')
- grad_w_zero: float32 [896, 896], P('graph', 'dp')
- grad_attention: float32 [128, 8], replicated
The draws below stay inside these ranges and needn't reach their ends.
Inputs may be any that keep to these rules, and one draw needn't show every extreme that they name: Atoms 0 to atom_counts[b] - 1 of batch b are real; the first batch fills all 64 rows and the second holds the fewest allowed. `source`: below the batch's atom count; never equal to the slot's target. `target`: below the batch's atom count; never equal to the slot's source. `wigner`: entry [k, j, e] is zero unless reduced row k and coefficient j have the same degree l.
All inputs are finite; a program needn't handle non-finite values. No bound on the sum of `edge_counts` on one device may be relied on, other than what follows from the above.
Results may differ from the reference program's by a relative error of at most 0.039.
Values may be sent and summed in bfloat16 or wider, within the bound.
No kernel may reach another device: no remote copies, remote signals or barrier semaphores. Data moves between devices by JAX's collectives and lax.ppermute only.
A program may use at most 64 MiB of HBM per device.

```python
import math
import jax
import jax.numpy as jnp
import numpy as np
from jax import lax

C = 128
HEADS = 8
LMAX = 6
EDGE_DEV = 128
COEF = 49
REDUCED = 29
HEAD_DIM = 16
D0 = 896
D1 = 768
D2 = 640
BATCHES = 32
NODES = 64
EDGES = 2048
N_GRAPH = 16


def degree_mask():
    row_degree = list(range(LMAX + 1)) + list(range(1, LMAX + 1)) * 2 + list(range(2, LMAX + 1)) * 2
    col_degree = [l for l in range(LMAX + 1) for _ in range(2 * l + 1)]
    block_mask = np.array([[1.0 / np.sqrt(2 * b + 1) if a == b else 0.0 for b in col_degree] for a in row_degree], np.float32)
    return jnp.asarray(block_mask)


def atom_table(key):
    missing = jax.random.randint(jax.random.fold_in(key, 5), (BATCHES,), 0, NODES // 2 + 1)
    batch_ids = jnp.arange(BATCHES)
    counts = jnp.where(batch_ids == 0, NODES, NODES - missing)
    counts = jnp.where(batch_ids == 1, NODES - NODES // 2, counts)
    return counts.astype(jnp.int32)


def source_table(key):
    atoms_here = atom_table(key)
    random_bits = jax.random.randint(jax.random.fold_in(key, 21), (BATCHES, EDGES), 0, 1 << 20)
    return (random_bits % atoms_here[:, None]).astype(jnp.int32)


def draw_atom_counts(key, part):
    return atom_table(key)


def draw_source(key, part):
    return source_table(key)


def draw_target(key, part):
    atoms_here = atom_table(key)
    sources = source_table(key)
    key = jax.random.fold_in(key, 22)
    random_bits = jax.random.randint(key, (BATCHES, EDGES), 0, 1 << 20)
    offset_by = 1 + random_bits % (atoms_here[:, None] - 1)
    return ((sources + offset_by) % atoms_here[:, None]).astype(jnp.int32)


def draw_wigner(key, part):
    key = jax.random.fold_in(key, 11)
    shape = (BATCHES, REDUCED, COEF, EDGES)
    entries = jnp.clip(jax.random.normal(key, shape, jnp.float32), -4.0, 4.0)
    return (entries * degree_mask()[None, :, :, None]).astype(jnp.bfloat16)


def block_scale(stream_key, extent, cuts, low, top_value):
    loudness, own = 1.0, jax.random.fold_in(stream_key, 6)
    for position, blocks in cuts:
        heights = jnp.exp(jax.random.uniform(jax.random.fold_in(own, position), (blocks,), jnp.float32, low / len(cuts), top_value / len(cuts)))
        loudness = loudness * jnp.repeat(heights, extent[position] // blocks).reshape([-1 if axis == position else 1 for axis in range(len(extent))])
    return loudness


def split_up(count, total, bound, skew):
    weights = [(1 << 20) // math.isqrt(grade ** skew) + 1 for grade in range(2, count + 1)]
    spare, given = total - bound - (count - 1), [1] * (count - 1)
    while spare > 0:
        movable = [i for i in range(count - 1) if given[i] < bound]
        mass, budget = sum([weights[i] for i in movable]), spare
        for i in movable:
            addition = min(bound - given[i], max(1, budget * weights[i] // mass), spare)
            given[i] = given[i] + addition
            spare = spare - addition
    return np.array([bound] + given)


def ragged(key, count, total, most, slope):
    if count == 2:
        one = jax.random.randint(key, (), max(1, total - most), min(most, total - 1) + 1)
        return jnp.stack([one, total - one])
    tallies = jnp.asarray(split_up(count, total, most, slope), jnp.int32)
    twos = (count - 1) // 2
    giver, taker = tallies[1:1 + 2 * twos:2], tallies[2:2 + 2 * twos:2]
    margin = jnp.minimum(giver - 1, most - taker)
    passed = jax.random.randint(jax.random.fold_in(key, 1), (twos,), 0, 1 << 20) % (margin + 1)
    tallies = tallies.at[1:1 + 2 * twos:2].set(giver - passed).at[2:2 + 2 * twos:2].set(taker + passed)
    return tallies[jax.random.permutation(jax.random.fold_in(key, 2), count)]


def noise(own_key, dims, deviation, reach, split=(), kind=jnp.bfloat16):
    values = jax.random.normal(own_key, dims, jnp.float32) * deviation
    if len(split) > 0:
        values = block_scale(own_key, dims, split, -0.22, 0.18) * values
    return jnp.clip(values, min=-reach, max=reach).astype(kind)


def setup_inputs(seed: int = 0) -> dict:
    keys = jax.random.split(jax.random.key(seed), 14)
    return {
        "embeddings": noise(keys[0], (BATCHES, NODES, COEF, C), 1.0, 6.0, ((0, 32), (1, 16))),
        "atom_counts": draw_atom_counts(jax.random.fold_in(keys[13], 71), 0),
        "edge_counts": jax.vmap(lambda own: ragged(own, N_GRAPH, EDGES // 2, EDGE_DEV, 2))(jax.random.split(keys[2], BATCHES)).reshape((BATCHES, N_GRAPH)).astype(jnp.int32),
        "source": draw_source(jax.random.fold_in(keys[13], 71), 0),
        "target": draw_target(jax.random.fold_in(keys[13], 71), 0),
        "wigner": draw_wigner(jax.random.fold_in(keys[13], 71), 0),
        "cotangent": noise(keys[6], (BATCHES, NODES, COEF, C), 1.0, 6.0, ((0, 32), (1, 16)), jnp.float32),
        "w_zero": noise(keys[7], (D0, D0), D0 ** -0.5, 0.1875, ((0, 16), (1, 32))),
        "w_one_real": noise(keys[8], (D1, D1), (2 * D1) ** -0.5, 0.15625, ((0, 16), (1, 32))),
        "w_one_imag": noise(keys[9], (D1, D1), (2 * D1) ** -0.5, 0.15625, ((0, 16), (1, 32))),
        "w_two_real": noise(keys[10], (D2, D2), (2 * D2) ** -0.5, 0.15625, ((0, 16), (1, 32))),
        "w_two_imag": noise(keys[11], (D2, D2), (2 * D2) ** -0.5, 0.15625, ((0, 16), (1, 32))),
        "attention": noise(keys[12], (C, HEADS), (C // 4) ** -0.5, 1.0),
    }


precise = lax.Precision.HIGHEST


def half_dot(left, right):
    return jnp.dot(left, right, preferred_element_type=jnp.float32)


def full_dot(left, right):
    return jnp.dot(left, right, precision=precise, preferred_element_type=jnp.float32)


def split_orders(field):
    bounds = [0, LMAX + 1, 2 * LMAX + 1, 3 * LMAX + 1, 4 * LMAX, 5 * LMAX - 1]
    rows = field.shape[0]
    return [field[:, bounds[i]:bounds[i + 1]].reshape(rows, -1) for i in range(5)]


def orders_forward(rotated, weights):
    w_zero, one_real, one_imag, two_real, two_imag = weights
    order_zero, one_plus, one_minus, two_plus, two_minus = split_orders(rotated)
    rows, channels = rotated.shape[0], rotated.shape[2]
    pieces = [half_dot(order_zero, w_zero),
              half_dot(one_plus, one_real) - half_dot(one_minus, one_imag),
              half_dot(one_minus, one_real) + half_dot(one_plus, one_imag),
              half_dot(two_plus, two_real) - half_dot(two_minus, two_imag),
              half_dot(two_minus, two_real) + half_dot(two_plus, two_imag)]
    return jnp.concatenate([p.reshape(rows, -1, channels) for p in pieces], axis=1)


def orders_backward(grad_conv, weights):
    w_zero, one_real, one_imag, two_real, two_imag = weights
    order_zero, one_plus, one_minus, two_plus, two_minus = split_orders(grad_conv)
    rows, channels = grad_conv.shape[0], grad_conv.shape[2]
    pieces = [half_dot(order_zero, w_zero.T),
              half_dot(one_plus, one_real.T) + half_dot(one_minus, one_imag.T),
              half_dot(one_minus, one_real.T) - half_dot(one_plus, one_imag.T),
              half_dot(two_plus, two_real.T) + half_dot(two_minus, two_imag.T),
              half_dot(two_minus, two_real.T) - half_dot(two_plus, two_imag.T)]
    return jnp.concatenate([p.reshape(rows, -1, channels) for p in pieces], axis=1)


def rotate(rotation, field):
    return jnp.einsum("kje,ejc->ekc", rotation, field, preferred_element_type=jnp.float32)


def rotate_back(rotation, field):
    return jnp.einsum("kje,ekc->ejc", rotation, field, preferred_element_type=jnp.float32)


def per_channel(values):
    rows = values.shape[0]
    return jnp.broadcast_to(values[:, :, None], (rows, HEADS, HEAD_DIM)).reshape(rows, C)


def reference(embeddings, atom_counts, edge_counts, source, target, wigner, cotangent, w_zero, w_one_real, w_one_imag, w_two_real, w_two_imag, attention):
    weights = (w_zero, w_one_real, w_one_imag, w_two_real, w_two_imag)

    def one_batch(batch_item):
        node_rows, atom_count, counts_here, source_ids, target_ids, rotation, grad_in = batch_item
        slot_ids = jnp.arange(EDGES, dtype=jnp.int32)
        in_use = ((slot_ids % EDGE_DEV) < counts_here[slot_ids // EDGE_DEV]).astype(jnp.float32)
        node_ids = jnp.arange(NODES, dtype=jnp.int32)
        target_hot = (target_ids[:, None] == node_ids[None, :]).astype(jnp.float32)
        incidence = ((source_ids[:, None] == node_ids[None, :]).astype(jnp.float32) + target_hot).astype(jnp.bfloat16)
        flattened = node_rows.reshape(NODES, COEF * C)
        paired = half_dot(incidence, flattened).astype(jnp.bfloat16).reshape(EDGES, COEF, C)
        rotated = rotate(rotation, paired).astype(jnp.bfloat16)
        convolved = orders_forward(rotated, weights)
        scalar = convolved[:, 0, :]
        gating = jax.nn.silu(scalar).astype(jnp.bfloat16)
        logits = half_dot(gating, attention)
        weight = in_use[:, None] * jnp.exp(logits)
        denominator = full_dot(target_hot.T, weight)
        normalized = weight / (full_dot(target_hot, denominator) + 1.0 - in_use[:, None])
        unrotated = rotate_back(rotation, convolved.astype(jnp.bfloat16))
        norm_wide = per_channel(normalized)
        message = unrotated * norm_wide[:, None, :]
        summed = full_dot(target_hot.T, message.reshape(EDGES, COEF * C))
        present = (node_ids < atom_count)[:, None]
        update = jnp.where(present, summed, 0.0).astype(jnp.bfloat16).reshape(NODES, COEF, C)
        grad_rows = jnp.where(present, grad_in.reshape(NODES, COEF * C), 0.0)
        grad_edge = full_dot(target_hot, grad_rows).reshape(EDGES, COEF, C)
        grad_unrot = (grad_edge * norm_wide[:, None, :]).astype(jnp.bfloat16)
        grad_norm = jnp.sum(grad_edge * unrotated, axis=1).reshape(EDGES, HEADS, HEAD_DIM).sum(axis=2)
        shared_sum = full_dot(target_hot.T, normalized * grad_norm)
        grad_logit = normalized * (grad_norm - full_dot(target_hot, shared_sum))
        grad_gating = full_dot(grad_logit, attention.astype(jnp.float32).T)
        grad_att = full_dot(gating.astype(jnp.float32).T, grad_logit)
        sigmoid_v = jax.nn.sigmoid(scalar)
        grad_scalar = grad_gating * sigmoid_v * (1.0 + scalar * (1.0 - sigmoid_v))
        grad_conv = rotate(rotation, grad_unrot).at[:, 0, :].add(grad_scalar).astype(jnp.bfloat16)
        grad_rotated = orders_backward(grad_conv, weights).astype(jnp.bfloat16)
        zero_in = split_orders(rotated)[0].reshape(N_GRAPH, EDGE_DEV, D0).astype(jnp.float32)
        zero_out = split_orders(grad_conv)[0].reshape(N_GRAPH, EDGE_DEV, D0).astype(jnp.float32)
        zero_blocks = jnp.einsum("gef,geh->gfh", zero_in, zero_out, precision=precise)
        zero_blocks = lax.optimization_barrier(zero_blocks.astype(jnp.bfloat16)).astype(jnp.float32)
        grad_zero = jnp.sum(zero_blocks, axis=0)
        grad_paired = rotate_back(rotation, grad_rotated).astype(jnp.bfloat16)
        block_incidence = incidence.reshape(N_GRAPH, EDGE_DEV, NODES).astype(jnp.float32)
        block_grads = grad_paired.reshape(N_GRAPH, EDGE_DEV, COEF * C).astype(jnp.float32)
        blocks = jnp.einsum("gen,gef->gnf", block_incidence, block_grads, precision=precise)
        blocks = lax.optimization_barrier(blocks.astype(jnp.bfloat16)).astype(jnp.float32)
        grad_here = jnp.sum(blocks, axis=0).astype(jnp.bfloat16).reshape(NODES, COEF, C)
        return update, grad_here, grad_zero, grad_att

    update, grad_nodes, grad_zero, grad_att = lax.map(one_batch, (embeddings, atom_counts, edge_counts, source, target, wigner, cotangent))
    return update, grad_nodes, jnp.sum(grad_zero, axis=0) / BATCHES, jnp.sum(grad_att, axis=0) / BATCHES
```

```python
import jax
import jax.numpy as jnp
from jax import lax
from jax.sharding import Mesh, PartitionSpec as P

LMAX = 6
LANES = 128
DP = ("xh", "z", "core")
COLUMN_GROUP = ("xh", "z")
GRAPH = ("y", "xl")
precise = lax.Precision.HIGHEST
f32 = jnp.float32
bf16 = jnp.bfloat16


def half_dot(left, right):
    return jnp.dot(left, right, preferred_element_type=f32)


def full_dot(left, right):
    return jnp.dot(left, right, precision=precise, preferred_element_type=f32)


def gather(block, axes):
    count = lax.axis_size(axes)
    copies = jnp.broadcast_to(block[None], (count,) + block.shape)
    return lax.all_to_all(copies, axes, split_axis=0, concat_axis=0, tiled=True)


def exchange(blocks, axes):
    return lax.all_to_all(blocks, axes, split_axis=0, concat_axis=0, tiled=True)


def split_orders(field):
    bounds = [0, LMAX + 1, 2 * LMAX + 1, 3 * LMAX + 1, 4 * LMAX, 5 * LMAX - 1]
    rows = field.shape[0]
    return [field[:, bounds[i] : bounds[i + 1]].reshape(rows, -1) for i in range(5)]


def orders_forward(rotated, weights):
    w_zero, one_real, one_imag, two_real, two_imag = weights
    order_zero, one_plus, one_minus, two_plus, two_minus = split_orders(rotated)
    rows, channels = (rotated.shape[0], rotated.shape[2])
    pieces = [
        half_dot(order_zero, w_zero),
        half_dot(one_plus, one_real) - half_dot(one_minus, one_imag),
        half_dot(one_minus, one_real) + half_dot(one_plus, one_imag),
        half_dot(two_plus, two_real) - half_dot(two_minus, two_imag),
        half_dot(two_minus, two_real) + half_dot(two_plus, two_imag),
    ]
    return jnp.concatenate([p.reshape(rows, -1, channels) for p in pieces], axis=1)


def orders_backward(grad_conv, weights):
    w_zero, one_real, one_imag, two_real, two_imag = weights
    order_zero, one_plus, one_minus, two_plus, two_minus = split_orders(grad_conv)
    rows, channels = (grad_conv.shape[0], grad_conv.shape[2])
    pieces = [
        half_dot(order_zero, w_zero.T),
        half_dot(one_plus, one_real.T) + half_dot(one_minus, one_imag.T),
        half_dot(one_minus, one_real.T) - half_dot(one_plus, one_imag.T),
        half_dot(two_plus, two_real.T) + half_dot(two_minus, two_imag.T),
        half_dot(two_minus, two_real.T) - half_dot(two_plus, two_imag.T),
    ]
    return jnp.concatenate([p.reshape(rows, -1, channels) for p in pieces], axis=1)


def rotate(rotation, field):
    return jnp.einsum("kje,ejc->ekc", rotation, field, preferred_element_type=f32)


def rotate_back(rotation, field):
    return jnp.einsum("kje,ekc->ejc", rotation, field, preferred_element_type=f32)


def per_channel(values, channels):
    rows, head_count = values.shape
    return jnp.broadcast_to(values[:, :, None], (rows, head_count, channels // head_count)).reshape(
        rows, channels
    )


def pad_to(block, rows, columns):
    return jnp.pad(block, ((0, rows - block.shape[0]), (0, columns - block.shape[1])))


def whole_lanes(count):
    return -(-count // LANES) * LANES


def column_tiles(block):
    rows, columns = block.shape
    tiles = block.reshape(rows, columns // LANES, LANES)
    return jnp.transpose(tiles, (1, 0, 2)).reshape(-1, LANES)


def gather_weights(shards):
    rows = [w.shape[0] for w in shards]
    columns = [w.shape[1] for w in shards]
    most = max(rows)
    packed = jnp.concatenate([pad_to(w, most, w.shape[1]) for w in shards], axis=1)
    packed = pad_to(packed, most, whole_lanes(packed.shape[1]))
    near = lax.all_gather(lax.all_gather(packed, "core"), "xl")
    blocks, at = [], 0
    for r, n in zip(rows, columns):
        piece = near[:, :, :r, at : at + n]
        blocks.append(jnp.transpose(piece, (0, 2, 1, 3)).reshape(2 * r, 2 * n))
        at += n
    first = lax.axis_index("core") == 0
    sets = ((0, 1), (2, 3, 4))
    lanes = whole_lanes(max(sum(2 * columns[i] for i in s) for s in sets))
    sent = [
        pad_to(
            jnp.concatenate([pad_to(blocks[i], 2 * most, 2 * columns[i]) for i in s], axis=1),
            2 * most,
            lanes,
        )
        for s in sets
    ]
    slabs = gather(jnp.where(first, sent[0], sent[1]), COLUMN_GROUP)
    whole = [2 * n * slabs.shape[0] for n in columns]
    tiled = []
    for s in sets:
        at, parts = 0, []
        for i in s:
            piece = slabs[:, : 2 * rows[i], at : at + 2 * columns[i]]
            at += 2 * columns[i]
            parts.append(
                column_tiles(jnp.transpose(piece, (1, 0, 2)).reshape(2 * rows[i], whole[i]))
            )
        tiled.append(jnp.concatenate(parts, axis=0))
    depth = max(t.shape[0] for t in tiled)
    tiled = [pad_to(t, depth, LANES) for t in tiled]
    half = lax.all_gather(jnp.where(first, tiled[0], tiled[1]), "y")
    both = lax.all_gather(half, "core")
    weights = []
    for half_index, s in enumerate(sets):
        at = 0
        for i in s:
            count = whole[i] // LANES
            part = both[half_index][:, at : at + count * 2 * rows[i]]
            at += count * 2 * rows[i]
            part = part.reshape(-1, count, 2 * rows[i], LANES)
            weights.append(jnp.transpose(part, (0, 2, 1, 3)).reshape(-1, whole[i]))
    return weights


def on_device(
    embeddings,
    atom_counts,
    edge_counts,
    source,
    target,
    wigner,
    cotangent,
    w_zero,
    w_one_real,
    w_one_imag,
    w_two_real,
    w_two_imag,
    attention,
):
    weights = gather_weights((w_zero, w_one_real, w_one_imag, w_two_real, w_two_imag))
    row_count = embeddings.shape[1]
    harmonics = embeddings.shape[2]
    channels = embeddings.shape[3]
    width = harmonics * channels
    edge_rows = source.shape[1]
    head_count = attention.shape[1]
    group = lax.axis_size(GRAPH)
    all_nodes = row_count * group
    source_ids = source[0]
    target_ids = target[0]
    rotation = wigner[0]
    in_use = (lax.iota(jnp.int32, edge_rows) < edge_counts[0, 0])[:, None]
    node_ids = lax.iota(jnp.int32, all_nodes)
    target_hot = (target_ids[:, None] == node_ids[None, :]).astype(f32)
    source_hot = (source_ids[:, None] == node_ids[None, :]).astype(f32)
    incidence = (source_hot + target_hot).astype(bf16)
    target_low = target_hot.astype(bf16)
    own_first = lax.axis_index(GRAPH) * row_count
    present = ((own_first + lax.iota(jnp.int32, row_count)) < atom_counts[0])[:, None]

    nodes = gather(embeddings[0].reshape(row_count, width), GRAPH).reshape(all_nodes, width)
    cot_rows = jnp.where(present, cotangent[0].reshape(row_count, width), 0.0).astype(bf16)
    cot_nodes = gather(cot_rows, GRAPH).reshape(all_nodes, width)

    paired = half_dot(incidence, nodes).astype(bf16).reshape(edge_rows, harmonics, channels)
    rotated = rotate(rotation, paired).astype(bf16)
    grad_edge = half_dot(target_low, cot_nodes).reshape(edge_rows, harmonics, channels)
    convolved = orders_forward(rotated, weights)
    scalar = convolved[:, 0, :]
    gating = jax.nn.silu(scalar).astype(bf16)
    logits = half_dot(gating, attention)
    weight = jnp.where(in_use, jnp.exp(logits), 0.0)
    unrotated = rotate_back(rotation, convolved.astype(bf16))
    grad_norm = (
        jnp.sum(grad_edge * unrotated, axis=1).reshape(edge_rows, head_count, -1).sum(axis=2)
    )
    own_sum = full_dot(target_hot.T, weight)
    at_edges = full_dot(target_hot, own_sum)
    own_norm = weight / jnp.where(at_edges > 0.0, at_edges, 1.0)
    own_shared = full_dot(target_hot.T, own_norm * grad_norm)
    stats = gather(jnp.concatenate([own_sum, own_shared], axis=1), GRAPH)
    sums = stats[:, :, :head_count]
    total = jnp.sum(sums, axis=0)
    shares = sums / jnp.where(total > 0.0, total, 1.0)[None]
    shared_sum = jnp.sum(shares * stats[:, :, head_count:], axis=0)
    own_share = own_sum / jnp.where(total > 0.0, total, 1.0)

    message = (unrotated * per_channel(own_norm, channels)[:, None, :]).reshape(edge_rows, width)
    message_sums = half_dot(target_low.T, message.astype(bf16)).astype(bf16)
    message_parts = exchange(message_sums.reshape(group, row_count, width), GRAPH)

    at_edges = full_dot(target_hot, jnp.concatenate([own_share, shared_sum], axis=1))
    normalized = own_norm * at_edges[:, :head_count]
    norm_wide = per_channel(normalized, channels)
    grad_unrot = (grad_edge * norm_wide[:, None, :]).astype(bf16)
    grad_logit = normalized * (grad_norm - at_edges[:, head_count:])
    grad_gating = full_dot(grad_logit, attention.astype(f32).T)
    grad_att = full_dot(gating.astype(f32).T, grad_logit)
    sigmoid_v = jax.nn.sigmoid(scalar)
    grad_scalar = grad_gating * sigmoid_v * (1.0 + scalar * (1.0 - sigmoid_v))
    grad_conv = rotate(rotation, grad_unrot).at[:, 0, :].add(grad_scalar).astype(bf16)

    columns = lax.axis_size(COLUMN_GROUP)
    depth = grad_conv.shape[2] * (LMAX + 1)
    share = depth // (2 * columns)
    core = lax.axis_index("core")
    zero_t = half_dot(split_orders(grad_conv)[0].T, split_orders(rotated)[0])
    zero_t = zero_t.reshape(columns, 2, share, depth)
    mine = jnp.where(core == 0, zero_t[:, 0], zero_t[:, 1])
    other = jnp.where(core == 0, zero_t[:, 1], zero_t[:, 0]).astype(bf16)
    mine = mine + lax.ppermute(other, "core", [(0, 1), (1, 0)]).astype(f32)
    grad_att = lax.psum(grad_att, "core")
    att_flat = grad_att.T.reshape(-1)
    terms, rest = [], att_flat
    for _ in range(3):
        low = lax.reduce_precision(rest, 8, 7)
        terms.append(low.astype(bf16))
        rest = rest - low
    extra = -(-3 * att_flat.shape[0] // depth)
    tail = jnp.pad(jnp.concatenate(terms), (0, extra * depth - 3 * att_flat.shape[0]))
    tail = jnp.broadcast_to(tail.reshape(1, extra, depth), (columns, extra, depth))
    zero_parts = exchange(jnp.concatenate([mine.astype(bf16), tail], axis=1), COLUMN_GROUP)
    zero_sum = jnp.sum(zero_parts.astype(f32), axis=0)
    att_flat = zero_sum[share:].reshape(-1)[: 3 * att_flat.shape[0]].reshape(3, -1).sum(axis=0)
    zero_send = jnp.transpose(zero_sum[:share].reshape(share, group, -1), (1, 0, 2))
    lanes = whole_lanes(zero_send.shape[2])
    zero_send = jnp.pad(zero_send, ((0, 0), (0, 0), (0, lanes - zero_send.shape[2])))
    att_rows = att_flat.size // LANES
    att_send = jnp.broadcast_to(att_flat.reshape(1, att_rows, LANES), (group, att_rows, LANES))
    att_send = jnp.pad(att_send, ((0, 0), (0, 0), (0, lanes - LANES)))

    grad_rotated = orders_backward(grad_conv, weights).astype(bf16)
    grad_paired = rotate_back(rotation, grad_rotated).astype(bf16).reshape(edge_rows, width)
    grad_blocks = half_dot(incidence.T, grad_paired).astype(bf16)
    grad_parts = exchange(grad_blocks.reshape(group, row_count, width), GRAPH)
    grad_nodes = jnp.sum(grad_parts.astype(f32), axis=0).astype(bf16)

    last = exchange(jnp.concatenate([zero_send, att_send], axis=1), GRAPH)
    last = jnp.sum(last, axis=0) * (1.0 / (2 * columns))
    grad_zero = last[:share, : depth // group].T
    grad_att = last[share:, :LANES].reshape(head_count, channels).T

    own_shares = lax.dynamic_slice_in_dim(shares, own_first, row_count, axis=1)
    wide = per_channel(own_shares.reshape(-1, head_count), channels)
    wide = wide.reshape(group, row_count, 1, channels)
    parts = message_parts.reshape(group, row_count, harmonics, channels).astype(f32)
    summed = jnp.sum(parts * wide, axis=0)
    update = jnp.where(present[:, :, None], summed, 0.0).astype(bf16)

    shape = (1, row_count, harmonics, channels)
    return (update.reshape(shape), grad_nodes.reshape(shape), grad_zero, grad_att)


def solution(mesh):
    columns, group = mesh.shape["dp"], mesh.shape["graph"]
    devices = mesh.devices.reshape(2, columns // 4, 2, group // 2, 2)
    fine = Mesh(devices, DP + GRAPH)
    in_specs = (
        P(DP, GRAPH, None, None),
        P(DP),
        P(DP, GRAPH),
        P(DP, GRAPH),
        P(DP, GRAPH),
        P(DP, None, None, GRAPH),
        P(DP, GRAPH, None, None),
        P(GRAPH, DP),
        P(GRAPH, DP),
        P(GRAPH, DP),
        P(GRAPH, DP),
        P(GRAPH, DP),
        P(),
    )
    out_specs = (P(DP, GRAPH, None, None), P(DP, GRAPH, None, None), P(GRAPH, DP), P())
    return jax.shard_map(
        on_device, mesh=fine, in_specs=in_specs, out_specs=out_specs, check_vma=False
    )
```

```python
import functools

import jax
import jax.numpy as jnp
from jax import lax
from jax.experimental import pallas as pl
from jax.experimental.pallas import tpu as pltpu
from jax.sharding import Mesh, PartitionSpec as P

LMAX = 6
LANES = 128
DP = ("xh", "z", "core")
COLUMN_GROUP = ("xh", "z")
GRAPH = ("y", "xl")
precise = lax.Precision.HIGHEST
f32 = jnp.float32
bf16 = jnp.bfloat16


def half_dot(left, right):
    return jnp.dot(left, right, preferred_element_type=f32)


def full_dot(left, right):
    return jnp.dot(left, right, precision=precise, preferred_element_type=f32)


def gather(block, axes):
    count = lax.axis_size(axes)
    copies = jnp.broadcast_to(block[None], (count,) + block.shape)
    return lax.all_to_all(copies, axes, split_axis=0, concat_axis=0, tiled=True)


def exchange(blocks, axes):
    return lax.all_to_all(blocks, axes, split_axis=0, concat_axis=0, tiled=True)


ROW_DEGREE = (
    list(range(LMAX + 1)) + list(range(1, LMAX + 1)) * 2 + list(range(2, LMAX + 1)) * 2
)
ROWS_OF = [[k for k, d in enumerate(ROW_DEGREE) if d == l] for l in range(LMAX + 1)]
COEFS_OF = [list(range(l * l, (l + 1) * (l + 1))) for l in range(LMAX + 1)]
REDUCED = len(ROW_DEGREE)
COEF = (LMAX + 1) ** 2
ZERO = (0, LMAX + 1)
ONE = (LMAX + 1, LMAX)
TWO = (3 * LMAX + 1, LMAX - 1)
CHUNK = 32
VMEM = pl.BlockSpec(memory_space=pltpu.VMEM)
ANY = pl.BlockSpec(memory_space=pl.ANY)
PARAMS = pltpu.CompilerParams(vmem_limit_bytes=48 * 1024 * 1024)


def nt_dot(left, right):
    return lax.dot_general(left, right, (((1,), (1,)), ((), ())), preferred_element_type=f32)


def nt_full(left, right):
    return lax.dot_general(
        left, right, (((1,), (1,)), ((), ())), precision=precise, preferred_element_type=f32
    )


def hot_rows(ids, count):
    rows = lax.broadcasted_iota(jnp.int32, (count, ids.shape[1]), 0)
    return (rows == ids).astype(f32)


def widen(values, channels):
    heads, edges = values.shape
    wide = jnp.broadcast_to(values[:, None, :], (heads, channels // heads, edges))
    return wide.reshape(channels, edges)


def chunks(channels, body):
    def step(i, carry):
        body(pl.ds(pl.multiple_of(i * CHUNK, CHUNK), CHUNK))
        return carry

    lax.fori_loop(0, channels // CHUNK, step, 0)


def copy_weights(first, mine, other, held, sems):
    def go(low, high):
        one = pltpu.make_async_copy(low, held.at[0], sems.at[0])
        two = pltpu.make_async_copy(high, held.at[1], sems.at[1])
        one.start()
        two.start()
        one.wait()
        two.wait()

    @pl.when(first == 0)
    def _():
        go(mine, other)

    @pl.when(first != 0)
    def _():
        go(other, mine)


def map_tiles(held, place, tiles):
    half, at, rows = place
    parts = []
    for t in tiles:
        part = held[half, :, at + t * rows : at + (t + 1) * rows, :]
        parts.append(part.reshape(-1, LANES))
    return parts[0] if len(parts) == 1 else jnp.concatenate(parts, axis=1)


def pairs(count):
    return [tuple(range(i, min(i + 2, count))) for i in range(0, count, 2)]


def rotate_kernel(ids, nodes, cots, wigner, z, grad_edge, paired, wide):
    count, edges = nodes.shape[0], wigner.shape[2]
    channels = LANES
    target = hot_rows(ids[1:2, :], count)
    both = (target + hot_rows(ids[0:1, :], count)).astype(bf16)
    target = target.astype(bf16)
    wide[...] = wigner[...].astype(f32)
    for j in range(COEF):
        at = slice(j * channels, (j + 1) * channels)
        paired[j] = half_dot(nodes[:, at].T, both).astype(bf16).astype(f32)
        grad_edge[j] = half_dot(cots[:, at].T, target).astype(bf16)
    for l in range(LMAX + 1):
        for k in ROWS_OF[l]:
            acc = None
            for j in COEFS_OF[l]:
                term = wide[k, j : j + 1, :] * paired[j]
                acc = term if acc is None else acc + term
            z[:, k * channels : (k + 1) * channels] = acc.T.astype(bf16)


def forward_kernel(
    places,
    first,
    ids,
    z,
    wigner,
    grad_edge,
    attention_t,
    mine,
    other,
    message,
    stats,
    scalar,
    per_edge,
    held,
    y,
    wide,
    norm,
    msg,
    heads_acc,
    sems,
):
    channels, edges = LANES, wigner.shape[2]
    heads = attention_t.shape[0]
    count = stats.shape[1]
    copy_weights(first[0, 0], mine, other, held, sems)
    wide[...] = wigner[...].astype(f32)
    base, rows = ZERO
    left = z[:, : rows * channels]
    for tiles in pairs(rows):
        out = half_dot(left, map_tiles(held, places[0], tiles))
        for i, t in enumerate(tiles):
            turned = out[:, i * channels : (i + 1) * channels].T
            if t == 0:
                scalar[...] = turned
            y[t] = turned.astype(bf16).astype(f32)
    for (base, rows), real, imag in ((ONE, places[1], places[2]), (TWO, places[3], places[4])):
        plus = z[:, base * channels : (base + rows) * channels]
        minus = z[:, (base + rows) * channels : (base + 2 * rows) * channels]
        left = jnp.concatenate([plus, minus], axis=0)
        crossed = jnp.concatenate([-minus, plus], axis=0)
        for tiles in pairs(rows):
            out = half_dot(left, map_tiles(held, real, tiles))
            out = out + half_dot(crossed, map_tiles(held, imag, tiles))
            for i, t in enumerate(tiles):
                at = slice(i * channels, (i + 1) * channels)
                y[base + t] = out[:edges, at].T.astype(bf16).astype(f32)
                y[base + rows + t] = out[edges:, at].T.astype(bf16).astype(f32)
    value = scalar[...]
    gating = (value / (1.0 + jnp.exp(-value))).astype(bf16)
    logits = half_dot(attention_t[...], gating)
    weight = jnp.where(ids[2:3, :] > 0, jnp.exp(logits), 0.0)
    target = hot_rows(ids[1:2, :], count)
    own_sum = nt_full(weight, target)
    at_edges = full_dot(own_sum, target)
    own_norm = weight / jnp.where(at_edges > 0.0, at_edges, 1.0)
    norm[...] = widen(own_norm, channels)

    def body(at):
        own = norm[at, :]
        total = jnp.zeros((CHUNK, edges), f32)
        for l in range(LMAX + 1):
            for j in COEFS_OF[l]:
                acc = None
                for k in ROWS_OF[l]:
                    term = wide[k, j : j + 1, :] * y[k, at, :]
                    acc = term if acc is None else acc + term
                total = total + acc * grad_edge[j, at, :].astype(f32)
                msg[j, at, :] = (acc * own).astype(bf16)
        heads_acc[at, :] = total

    chunks(channels, body)
    grad_norm = jnp.sum(heads_acc[...].reshape(heads, channels // heads, edges), axis=1)
    own_shared = nt_full(own_norm * grad_norm, target)
    stats[:heads, :] = own_sum
    stats[heads:, :] = own_shared
    per_edge[:heads, :] = own_norm
    per_edge[heads:, :] = grad_norm
    low = target.astype(bf16)
    for j in range(COEF):
        message[:, j * channels : (j + 1) * channels] = nt_dot(low, msg[j]).astype(bf16)


def backward_kernel(
    ids, stats, every, scalar, per_edge, wigner, grad_edge, attention, attention_t, z,
    grad_conv, zero, wide, norm, grad, turned,
):
    channels, edges = LANES, wigner.shape[2]
    heads = attention_t.shape[0]
    count = stats.shape[1]
    wide[...] = wigner[...].astype(f32)
    total = jnp.sum(every[:, :heads, :], axis=0)
    total = jnp.where(total > 0.0, total, 1.0)
    shared = jnp.sum(every[:, :heads, :] / total[None] * every[:, heads:, :], axis=0)
    own_share = stats[:heads, :] / total
    target = hot_rows(ids[1:2, :], count)
    normalized = per_edge[:heads, :] * full_dot(own_share, target)
    grad_logit = normalized * (per_edge[heads:, :] - full_dot(shared, target))
    value = scalar[...]
    sigmoid = 1.0 / (1.0 + jnp.exp(-value))
    gating = (value / (1.0 + jnp.exp(-value))).astype(bf16).astype(f32)
    att = nt_full(grad_logit, gating)
    grad_gating = full_dot(attention[...].astype(f32), grad_logit)
    grad_scalar = grad_gating * sigmoid * (1.0 + value * (1.0 - sigmoid))
    norm[...] = widen(normalized, channels)

    def body(at):
        own = norm[at, :]
        for l in range(LMAX + 1):
            fields = [
                (grad_edge[j, at, :].astype(f32) * own).astype(bf16).astype(f32)
                for j in COEFS_OF[l]
            ]
            for k in ROWS_OF[l]:
                acc = None
                for j, field in zip(COEFS_OF[l], fields):
                    term = wide[k, j : j + 1, :] * field
                    acc = term if acc is None else acc + term
                grad[k, at, :] = acc

    chunks(channels, body)
    grad[0] = grad[0] + grad_scalar
    grad_conv[...] = grad[...].astype(bf16)
    depth = (LMAX + 1) * channels
    parts, share = zero.shape[1], depth // (2 * zero.shape[1])
    order_zero = grad_conv[: LMAX + 1].reshape(depth, edges)
    turned[:depth, :] = half_dot(order_zero, z[:, :depth])
    turned[depth:, :] = jnp.zeros((turned.shape[0] - depth, depth), f32)
    padded = zero.shape[2]
    tail_row = lax.broadcasted_iota(jnp.int32, (padded, depth), 0)
    first = jnp.concatenate([att[h : h + 1, :] for h in range(LMAX + 1)], axis=1)
    rest = [att[h : h + 1, :] for h in range(LMAX + 1, heads)]
    rest = jnp.concatenate(rest + [jnp.zeros((1, depth - len(rest) * channels), f32)], axis=1)
    for core in range(2):
        for part in range(parts):
            at = (2 * part + core) * share
            block = turned[at : at + padded, :]
            block = jnp.where(tail_row == share, first, block)
            block = jnp.where(tail_row == share + 1, rest, block)
            zero[core, part] = block.astype(bf16)


def scatter_kernel(places, first, ids, grad_conv, wigner, mine, other, grads, held, wide, dz, gp, sems):
    channels, edges = LANES, wigner.shape[2]
    count = grads.shape[0]
    copy_weights(first[0, 0], mine, other, held, sems)
    wide[...] = wigner[...].astype(f32)
    base, rows = ZERO
    acc = None
    for tiles in pairs(rows):
        right = grad_conv[tiles[0] : tiles[-1] + 1].reshape(-1, edges)
        term = half_dot(map_tiles(held, places[0], tiles), right)
        acc = term if acc is None else acc + term
    dz[:rows] = acc.astype(bf16).astype(f32).reshape(rows, channels, edges)
    for (base, rows), real, imag in ((ONE, places[1], places[2]), (TWO, places[3], places[4])):
        acc = None
        for tiles in pairs(rows):
            lo, hi = base + tiles[0], base + tiles[-1] + 1
            plus = grad_conv[lo:hi].reshape(-1, edges)
            minus = grad_conv[lo + rows : hi + rows].reshape(-1, edges)
            term = half_dot(map_tiles(held, real, tiles), jnp.concatenate([plus, minus], axis=1))
            term = term + half_dot(
                map_tiles(held, imag, tiles), jnp.concatenate([minus, -plus], axis=1)
            )
            acc = term if acc is None else acc + term
        acc = acc.astype(bf16).astype(f32)
        dz[base : base + rows] = acc[:, :edges].reshape(rows, channels, edges)
        dz[base + rows : base + 2 * rows] = acc[:, edges:].reshape(rows, channels, edges)

    def body(at):
        for l in range(LMAX + 1):
            for j in COEFS_OF[l]:
                acc = None
                for k in ROWS_OF[l]:
                    term = wide[k, j : j + 1, :] * dz[k, at, :]
                    acc = term if acc is None else acc + term
                gp[j, at, :] = acc.astype(bf16)

    chunks(channels, body)
    both = (hot_rows(ids[1:2, :], count) + hot_rows(ids[0:1, :], count)).astype(bf16)
    for j in range(COEF):
        grads[:, j * channels : (j + 1) * channels] = nt_dot(both, gp[j]).astype(bf16)


def per_channel(values, channels):
    rows, head_count = values.shape
    return jnp.broadcast_to(values[:, :, None], (rows, head_count, channels // head_count)).reshape(
        rows, channels
    )


def pad_to(block, rows, columns):
    return jnp.pad(block, ((0, rows - block.shape[0]), (0, columns - block.shape[1])))


def whole_lanes(count):
    return -(-count // LANES) * LANES


def column_tiles(block):
    rows, columns = block.shape
    tiles = block.reshape(rows, columns // LANES, LANES)
    return jnp.transpose(tiles, (1, 0, 2)).reshape(-1, LANES)


def gather_weights(shards):
    rows = [w.shape[0] for w in shards]
    columns = [w.shape[1] for w in shards]
    most = max(rows)
    packed = jnp.concatenate([pad_to(w, most, w.shape[1]) for w in shards], axis=1)
    packed = pad_to(packed, most, whole_lanes(packed.shape[1]))
    near = lax.all_gather(lax.all_gather(packed, "core"), "xl")
    blocks, at = [], 0
    for r, n in zip(rows, columns):
        piece = near[:, :, :r, at : at + n]
        blocks.append(jnp.transpose(piece, (0, 2, 1, 3)).reshape(2 * r, 2 * n))
        at += n
    first = lax.axis_index("core") == 0
    sets = ((0, 1), (2, 3, 4))
    lanes = whole_lanes(max(sum(2 * columns[i] for i in s) for s in sets))
    sent = [
        pad_to(
            jnp.concatenate([pad_to(blocks[i], 2 * most, 2 * columns[i]) for i in s], axis=1),
            2 * most,
            lanes,
        )
        for s in sets
    ]
    slabs = gather(jnp.where(first, sent[0], sent[1]), COLUMN_GROUP)
    whole = [2 * n * slabs.shape[0] for n in columns]
    tiled = []
    for s in sets:
        at, parts = 0, []
        for i in s:
            piece = slabs[:, : 2 * rows[i], at : at + 2 * columns[i]]
            at += 2 * columns[i]
            parts.append(
                column_tiles(jnp.transpose(piece, (1, 0, 2)).reshape(2 * rows[i], whole[i]))
            )
        tiled.append(jnp.concatenate(parts, axis=0))
    depth = max(t.shape[0] for t in tiled)
    tiled = [pad_to(t, depth, LANES) for t in tiled]
    half = lax.all_gather(jnp.where(first, tiled[0], tiled[1]), "y")
    places = [None] * len(shards)
    for half_index, s in enumerate(sets):
        at = 0
        for i in s:
            places[i] = (half_index, at, 2 * rows[i])
            at += whole[i] // LANES * 2 * rows[i]
    return half, places, slabs


def on_device(
    embeddings,
    atom_counts,
    edge_counts,
    source,
    target,
    wigner,
    cotangent,
    w_zero,
    w_one_real,
    w_one_imag,
    w_two_real,
    w_two_imag,
    attention,
):
    half, places, slabs = gather_weights((w_zero, w_one_real, w_one_imag, w_two_real, w_two_imag))
    row_count = embeddings.shape[1]
    harmonics = embeddings.shape[2]
    channels = embeddings.shape[3]
    width = harmonics * channels
    edge_rows = source.shape[1]
    head_count = attention.shape[1]
    group = lax.axis_size(GRAPH)
    all_nodes = row_count * group
    rotation = wigner[0]
    in_use = (lax.iota(jnp.int32, edge_rows) < edge_counts[0, 0]).astype(jnp.int32)
    ids = jnp.stack([source[0], target[0], in_use] + [jnp.zeros_like(in_use)] * 5)
    attention_t = attention.T
    core = lax.axis_index("core")
    first = core.astype(jnp.int32).reshape(1, 1)
    own_first = lax.axis_index(GRAPH) * row_count
    present = ((own_first + lax.iota(jnp.int32, row_count)) < atom_counts[0])[:, None]
    cot_rows = jnp.where(present, cotangent[0].reshape(row_count, width), 0.0).astype(bf16)
    node_rows = embeddings[0].reshape(row_count, width)
    node_rows, cot_rows, slabs = lax.optimization_barrier((node_rows, cot_rows, slabs))
    nodes = gather(node_rows, GRAPH).reshape(all_nodes, width)
    cot_nodes = gather(cot_rows, GRAPH).reshape(all_nodes, width)

    smem = pl.BlockSpec(memory_space=pltpu.SMEM)
    field = (channels, edge_rows)
    wide = pltpu.VMEM(rotation.shape, f32)
    z, grad_edge = pl.pallas_call(
        rotate_kernel,
        out_shape=(
            jax.ShapeDtypeStruct((edge_rows, REDUCED * channels), bf16),
            jax.ShapeDtypeStruct((COEF,) + field, bf16),
        ),
        in_specs=[VMEM] * 4,
        out_specs=[VMEM] * 2,
        scratch_shapes=[pltpu.VMEM((COEF,) + field, f32), wide],
        compiler_params=PARAMS,
    )(ids, nodes, cot_nodes, rotation)
    half, z, grad_edge = lax.optimization_barrier((half, z, grad_edge))
    other = lax.ppermute(half, "core", [(0, 1), (1, 0)])
    held = pltpu.VMEM((2,) + half.shape, bf16)
    copies = pltpu.SemaphoreType.DMA((2,))

    message_sums, stats, scalar, per_edge = pl.pallas_call(
        functools.partial(forward_kernel, places),
        out_shape=(
            jax.ShapeDtypeStruct((all_nodes, width), bf16),
            jax.ShapeDtypeStruct((2 * head_count, all_nodes), f32),
            jax.ShapeDtypeStruct(field, f32),
            jax.ShapeDtypeStruct((2 * head_count, edge_rows), f32),
        ),
        in_specs=[smem] + [VMEM] * 5 + [ANY] * 2,
        out_specs=[VMEM] * 4,
        scratch_shapes=[
            held,
            pltpu.VMEM((REDUCED,) + field, f32),
            wide,
            pltpu.VMEM(field, f32),
            pltpu.VMEM((COEF,) + field, bf16),
            pltpu.VMEM(field, f32),
            copies,
        ],
        compiler_params=PARAMS,
    )(first, ids, z, rotation, grad_edge, attention_t, half, other)
    every = gather(stats, GRAPH)
    message_parts = exchange(message_sums.reshape(group, row_count, width), GRAPH)

    columns = lax.axis_size(COLUMN_GROUP)
    depth = channels * (LMAX + 1)
    share = depth // (2 * columns)
    padded = -(-(share + 2) // 16) * 16
    grad_conv, zero = pl.pallas_call(
        backward_kernel,
        out_shape=(
            jax.ShapeDtypeStruct((REDUCED,) + field, bf16),
            jax.ShapeDtypeStruct((2, columns, padded, depth), bf16),
        ),
        in_specs=[VMEM] * 10,
        out_specs=[VMEM] * 2,
        scratch_shapes=[
            wide,
            pltpu.VMEM(field, f32),
            pltpu.VMEM((REDUCED,) + field, f32),
            pltpu.VMEM((depth + padded, depth), f32),
        ],
        compiler_params=PARAMS,
    )(ids, stats, every, scalar, per_edge, rotation, grad_edge, attention, attention_t, z)

    mine = jnp.where(core == 0, zero[0], zero[1])
    theirs = jnp.where(core == 0, zero[1], zero[0])
    theirs = lax.ppermute(theirs, "core", [(0, 1), (1, 0)])
    mine = (mine.astype(f32) + theirs.astype(f32)).astype(bf16)
    zero_parts = exchange(mine, COLUMN_GROUP)
    zero_sum = jnp.sum(zero_parts.astype(f32), axis=0)
    att_flat = zero_sum[share : share + 2].reshape(-1)[: head_count * channels]
    zero_send = jnp.transpose(zero_sum[:share].reshape(share, group, -1), (1, 0, 2))
    lanes = whole_lanes(zero_send.shape[2])
    zero_send = jnp.pad(zero_send, ((0, 0), (0, 0), (0, lanes - zero_send.shape[2])))
    att_rows = att_flat.size // LANES
    att_send = jnp.broadcast_to(att_flat.reshape(1, att_rows, LANES), (group, att_rows, LANES))
    att_send = jnp.pad(att_send, ((0, 0), (0, 0), (0, lanes - LANES)))

    grad_blocks = pl.pallas_call(
        functools.partial(scatter_kernel, places),
        out_shape=jax.ShapeDtypeStruct((all_nodes, width), bf16),
        in_specs=[smem] + [VMEM] * 3 + [ANY] * 2,
        out_specs=VMEM,
        scratch_shapes=[
            held,
            wide,
            pltpu.VMEM((REDUCED,) + field, f32),
            pltpu.VMEM((COEF,) + field, bf16),
            copies,
        ],
        compiler_params=PARAMS,
    )(first, ids, grad_conv, rotation, half, other)
    grad_parts = exchange(grad_blocks.reshape(group, row_count, width), GRAPH)
    grad_nodes = jnp.sum(grad_parts.astype(f32), axis=0).astype(bf16)

    last = exchange(jnp.concatenate([zero_send, att_send], axis=1), GRAPH)
    last = jnp.sum(last, axis=0) * (1.0 / (2 * columns))
    grad_zero = last[:share, : depth // group].T
    grad_att = last[share:, :LANES].reshape(head_count, channels).T

    sums = lax.dynamic_slice_in_dim(every[:, :head_count], own_first, row_count, axis=2)
    sums = jnp.transpose(sums, (0, 2, 1))
    total = jnp.sum(sums, axis=0)
    own_shares = sums / jnp.where(total > 0.0, total, 1.0)[None]
    wide = per_channel(own_shares.reshape(-1, head_count), channels)
    wide = wide.reshape(group, row_count, 1, channels)
    parts = message_parts.reshape(group, row_count, harmonics, channels).astype(f32)
    summed = jnp.sum(parts * wide, axis=0)
    update = jnp.where(present[:, :, None], summed, 0.0).astype(bf16)

    shape = (1, row_count, harmonics, channels)
    return (update.reshape(shape), grad_nodes.reshape(shape), grad_zero, grad_att)


def solution(mesh):
    columns, group = mesh.shape["dp"], mesh.shape["graph"]
    devices = mesh.devices.reshape(2, columns // 4, 2, group // 2, 2)
    fine = Mesh(devices, DP + GRAPH)
    in_specs = (
        P(DP, GRAPH, None, None),
        P(DP),
        P(DP, GRAPH),
        P(DP, GRAPH),
        P(DP, GRAPH),
        P(DP, None, None, GRAPH),
        P(DP, GRAPH, None, None),
        P(GRAPH, DP),
        P(GRAPH, DP),
        P(GRAPH, DP),
        P(GRAPH, DP),
        P(GRAPH, DP),
        P(),
    )
    out_specs = (P(DP, GRAPH, None, None), P(DP, GRAPH, None, None), P(GRAPH, DP), P())
    return jax.shard_map(
        on_device, mesh=fine, in_specs=in_specs, out_specs=out_specs, check_vma=False
    )
```

```python
import functools

import jax
import jax.numpy as jnp
from jax import lax
from jax.experimental import pallas as pl
from jax.experimental.pallas import tpu as pltpu
from jax.sharding import Mesh, PartitionSpec as P

LMAX = 6
LANES = 128
DP = ("xh", "z", "core")
COLUMN_GROUP = ("xh", "z")
ROW_GROUP = ("xh", "y", "xl")
GRAPH = ("y", "xl")
precise = lax.Precision.HIGHEST
f32 = jnp.float32
bf16 = jnp.bfloat16


def half_dot(left, right):
    return jnp.dot(left, right, preferred_element_type=f32)


def full_dot(left, right):
    return jnp.dot(left, right, precision=precise, preferred_element_type=f32)


def gather(block, axes):
    count = lax.axis_size(axes)
    copies = jnp.broadcast_to(block[None], (count,) + block.shape)
    return lax.all_to_all(copies, axes, split_axis=0, concat_axis=0, tiled=True)


def exchange(blocks, axes):
    return lax.all_to_all(blocks, axes, split_axis=0, concat_axis=0, tiled=True)


ROW_DEGREE = (
    list(range(LMAX + 1)) + list(range(1, LMAX + 1)) * 2 + list(range(2, LMAX + 1)) * 2
)
ROWS_OF = [[k for k, d in enumerate(ROW_DEGREE) if d == l] for l in range(LMAX + 1)]
COEFS_OF = [list(range(l * l, (l + 1) * (l + 1))) for l in range(LMAX + 1)]
REDUCED = len(ROW_DEGREE)
COEF = (LMAX + 1) ** 2
ZERO = (0, LMAX + 1)
ONE = (LMAX + 1, LMAX)
TWO = (3 * LMAX + 1, LMAX - 1)
CHUNK = 32
VMEM = pl.BlockSpec(memory_space=pltpu.VMEM)
ANY = pl.BlockSpec(memory_space=pl.ANY)
PARAMS = pltpu.CompilerParams(vmem_limit_bytes=48 * 1024 * 1024)


def nt_dot(left, right):
    return lax.dot_general(left, right, (((1,), (1,)), ((), ())), preferred_element_type=f32)


def nt_full(left, right):
    return lax.dot_general(
        left, right, (((1,), (1,)), ((), ())), precision=precise, preferred_element_type=f32
    )


def hot_rows(ids, count):
    rows = lax.broadcasted_iota(jnp.int32, (count, ids.shape[1]), 0)
    return (rows == ids).astype(f32)


def widen(values, channels):
    heads, edges = values.shape
    wide = jnp.broadcast_to(values[:, None, :], (heads, channels // heads, edges))
    return wide.reshape(channels, edges)


def chunks(channels, body):
    def step(i, carry):
        body(pl.multiple_of(i * CHUNK, CHUNK))
        return carry

    lax.fori_loop(0, channels // CHUNK, step, 0)


def rows_at(k, start):
    return pl.ds(pl.multiple_of(k * LANES + start, CHUNK), CHUNK)


def copy_weights(first, mine, other, held, sems):
    def go(low, high):
        one = pltpu.make_async_copy(low, held.at[0], sems.at[0])
        two = pltpu.make_async_copy(high, held.at[1], sems.at[1])
        one.start()
        two.start()
        one.wait()
        two.wait()

    @pl.when(first == 0)
    def _():
        go(mine, other)

    @pl.when(first != 0)
    def _():
        go(other, mine)


def map_tiles(held, place, tiles):
    half, at, rows = place
    parts = []
    for t in tiles:
        part = held[half, :, at + t * rows : at + (t + 1) * rows, :]
        parts.append(part.reshape(-1, LANES))
    return parts[0] if len(parts) == 1 else jnp.concatenate(parts, axis=1)


def pairs(count):
    return [tuple(range(i, min(i + 2, count))) for i in range(0, count, 2)]


def spread(blocks, held, rows, base, out):
    zs = held.shape[1]
    size = rows // 2
    for z in range(zs):
        for xh in range(2):
            to = base + (xh * zs + z) * size
            at = (z * 2 + xh) * size
            out[to : to + size, :] = blocks[at : at + size, :]


def by_owner(target, turned, out, group):
    channels = turned.shape[1]
    own = target.shape[0] // group
    per = 16 // own
    for first in range(0, COEF, per):
        parts = []
        for j in range(first, first + per):
            if j < COEF:
                part = nt_dot(target, turned[j])
            else:
                part = jnp.zeros((target.shape[0], channels), f32)
            parts.append(part.reshape(group, 1, own, channels))
        block = jnp.concatenate(parts, axis=1).reshape(group, 16, channels)
        out[:, first * own : first * own + 16, :] = block.astype(bf16)


def rotate_kernel(ids, nodes, wigner, z, grad_edge, paired, wide):
    count, edges = nodes.shape[0], wigner.shape[2]
    channels = LANES
    target = hot_rows(ids[1:2, :], count)
    both = (target + hot_rows(ids[0:1, :], count)).astype(bf16)
    target = target.astype(bf16)
    wide[...] = wigner[...].astype(f32)
    for j in range(COEF):
        at = slice(j * channels, (j + 1) * channels)
        paired[j] = half_dot(nodes[:, at].T, both).astype(bf16).astype(f32)
        at = slice((COEF + j) * channels, (COEF + j + 1) * channels)
        grad_edge[j] = half_dot(nodes[:, at].T, target).astype(bf16)
    for l in range(LMAX + 1):
        for k in ROWS_OF[l]:
            acc = None
            for j in COEFS_OF[l]:
                term = wide[k, j : j + 1, :] * paired[j]
                acc = term if acc is None else acc + term
            z[k] = acc.astype(bf16)


def forward_kernel(
    places,
    group,
    first,
    ids,
    z,
    wigner,
    grad_edge,
    attention_t,
    mine,
    other,
    message,
    stats,
    scalar,
    per_edge,
    held,
    y,
    wide,
    norm,
    msg,
    heads_acc,
    sems,
):
    channels, edges = LANES, wigner.shape[2]
    heads = attention_t.shape[0]
    count = stats.shape[1] // 2
    copy_weights(first[0, 0], mine, other, held, sems)
    wide[...] = wigner[...].astype(f32)
    base, rows = ZERO
    acc = None
    for tiles in pairs(rows):
        right = z[tiles[0] : tiles[-1] + 1].reshape(-1, edges)
        term = half_dot(map_tiles(held, places[0], tiles), right)
        acc = term if acc is None else acc + term
    spread(acc, held, places[0][2], base, y)
    for (base, rows), real, imag in ((ONE, places[1], places[2]), (TWO, places[3], places[4])):
        acc = None
        for tiles in pairs(rows):
            lo, hi = base + tiles[0], base + tiles[-1] + 1
            plus = z[lo:hi].reshape(-1, edges)
            minus = z[lo + rows : hi + rows].reshape(-1, edges)
            term = half_dot(map_tiles(held, real, tiles), jnp.concatenate([plus, minus], axis=1))
            term = term + half_dot(
                map_tiles(held, imag, tiles), jnp.concatenate([-minus, plus], axis=1)
            )
            acc = term if acc is None else acc + term
        spread(acc[:, :edges], held, real[2], base * channels, y)
        spread(acc[:, edges:], held, real[2], (base + rows) * channels, y)
    value = y[:channels, :]
    scalar[...] = value
    y[...] = y[...].astype(bf16).astype(f32)
    gating = (value / (1.0 + jnp.exp(-value))).astype(bf16)
    logits = half_dot(attention_t[...], gating)
    weight = jnp.where(ids[2:3, :] > 0, jnp.exp(logits), 0.0)
    target = hot_rows(ids[1:2, :], count)
    own_sum = nt_full(weight, target)
    at_edges = full_dot(own_sum, target)
    own_norm = weight / jnp.where(at_edges > 0.0, at_edges, 1.0)
    norm[...] = widen(own_norm, channels)

    def body(start):
        at = pl.ds(start, CHUNK)
        own = norm[at, :]
        total = jnp.zeros((CHUNK, edges), f32)
        for l in range(LMAX + 1):
            for j in COEFS_OF[l]:
                acc = None
                for k in ROWS_OF[l]:
                    term = wide[k, j : j + 1, :] * y[rows_at(k, start), :]
                    acc = term if acc is None else acc + term
                total = total + acc * grad_edge[j, at, :].astype(f32)
                msg[j, at, :] = (acc * own).astype(bf16)
        heads_acc[at, :] = total

    chunks(channels, body)
    grad_norm = jnp.sum(heads_acc[...].reshape(heads, channels // heads, edges), axis=1)
    own_shared = nt_full(own_norm * grad_norm, target)
    both = jnp.concatenate([own_sum, own_shared], axis=1)
    stats[...] = both
    per_edge[:heads, :] = own_norm
    per_edge[heads:, :] = grad_norm
    by_owner(target.astype(bf16), msg, message, group)
    rest = both
    if 2 * count < channels:
        rest = jnp.concatenate([both, jnp.zeros((heads, channels - 2 * count), f32)], axis=1)
    terms = []
    for _ in range(3):
        low = rest.astype(bf16).astype(f32)
        terms.append(low)
        rest = rest - low
    tail = jnp.concatenate(terms + [jnp.zeros((heads, channels), f32)], axis=0).astype(bf16)
    for owner in range(group):
        message[owner, message.shape[1] - 4 * heads :, :] = tail


def backward_kernel(
    zs,
    first,
    ids,
    stats,
    received,
    scalar,
    per_edge,
    wigner,
    grad_edge,
    attention,
    attention_t,
    z,
    grad_rows,
    mine,
    theirs,
    every,
    wide,
    norm,
    grad,
    turned,
):
    channels, edges = LANES, wigner.shape[2]
    heads = attention_t.shape[0]
    count = stats.shape[1] // 2
    wide[...] = wigner[...].astype(f32)
    tail = received[:, received.shape[1] - 4 * heads :, :].astype(f32)
    decoded = tail[:, :heads] + tail[:, heads : 2 * heads] + tail[:, 2 * heads : 3 * heads]
    every[...] = decoded
    total = jnp.sum(decoded[:, :, :count], axis=0)
    total = jnp.where(total > 0.0, total, 1.0)
    shares = decoded[:, :, :count] / total[None]
    shared = jnp.sum(shares * decoded[:, :, count : 2 * count], axis=0)
    own_share = stats[:, :count] / total
    target = hot_rows(ids[1:2, :], count)
    normalized = per_edge[:heads, :] * full_dot(own_share, target)
    grad_logit = normalized * (per_edge[heads:, :] - full_dot(shared, target))
    value = scalar[...]
    sigmoid = 1.0 / (1.0 + jnp.exp(-value))
    gating = (value / (1.0 + jnp.exp(-value))).astype(bf16).astype(f32)
    att = nt_full(grad_logit, gating)
    grad_gating = full_dot(attention[...].astype(f32), grad_logit)
    grad_scalar = grad_gating * sigmoid * (1.0 + value * (1.0 - sigmoid))
    norm[...] = widen(normalized, channels)

    def body(start):
        at = pl.ds(start, CHUNK)
        own = norm[at, :]
        for l in range(LMAX + 1):
            fields = [
                (grad_edge[j, at, :].astype(f32) * own).astype(bf16).astype(f32)
                for j in COEFS_OF[l]
            ]
            for k in ROWS_OF[l]:
                acc = None
                for j, field in zip(COEFS_OF[l], fields):
                    term = wide[k, j : j + 1, :] * field
                    acc = term if acc is None else acc + term
                grad[rows_at(k, start), :] = acc

    chunks(channels, body)
    grad[:channels, :] = grad[:channels, :] + grad_scalar
    depth = (LMAX + 1) * channels
    parts, share = mine.shape[0], depth // (2 * mine.shape[0])
    turned[:depth, :] = nt_dot(grad[:depth, :].astype(bf16), z[: LMAX + 1].reshape(depth, edges))
    turned[depth:, :] = jnp.zeros((turned.shape[0] - depth, depth), f32)
    padded = mine.shape[1]
    tail_row = lax.broadcasted_iota(jnp.int32, (padded, depth), 0)
    one = jnp.concatenate([att[h : h + 1, :] for h in range(LMAX + 1)], axis=1)
    two = [att[h : h + 1, :] for h in range(LMAX + 1, heads)]
    two = jnp.concatenate(two + [jnp.zeros((1, depth - len(two) * channels), f32)], axis=1)

    def store(outs):
        for core in range(2):
            for part in range(parts):
                at = (2 * part + core) * share
                block = turned[at : at + padded, :]
                block = jnp.where(tail_row == share, one, block)
                block = jnp.where(tail_row == share + 1, two, block)
                outs[core][part] = block.astype(bf16)

    @pl.when(first[0, 0] == 0)
    def _():
        store((mine, theirs))

    @pl.when(first[0, 0] != 0)
    def _():
        store((theirs, mine))

    for base, rows in (ZERO, ONE, (ONE[0] + ONE[1], ONE[1]), TWO, (TWO[0] + TWO[1], TWO[1])):
        size = rows * channels // (2 * zs)
        blocks = []
        for zz in range(zs):
            for xh in range(2):
                at = base * channels + (xh * zs + zz) * size
                blocks.append(grad[at : at + size, :])
        ordered = jnp.concatenate(blocks, axis=0)
        for t in range(rows):
            at = slice(t * channels, (t + 1) * channels)
            to = (base + t) * channels
            grad_rows[:, to : to + channels] = ordered[at, :].T.astype(bf16)


def scatter_kernel(
    places, group, own, first, ids, grad_rows, wigner, mine, other, grads, held, wide, dz, gp, sems
):
    channels, edges = LANES, wigner.shape[2]
    count = own * group
    copy_weights(first[0, 0], mine, other, held, sems)
    wide[...] = wigner[...].astype(f32)
    base, rows = ZERO
    left = grad_rows[:, : rows * channels]
    for tiles in pairs(rows):
        out = half_dot(left, map_tiles(held, places[0], tiles)).astype(bf16).astype(f32)
        for i, t in enumerate(tiles):
            dz[t] = out[:, i * channels : (i + 1) * channels].T
    for (base, rows), real, imag in ((ONE, places[1], places[2]), (TWO, places[3], places[4])):
        plus = grad_rows[:, base * channels : (base + rows) * channels]
        minus = grad_rows[:, (base + rows) * channels : (base + 2 * rows) * channels]
        left = jnp.concatenate([plus, minus], axis=0)
        crossed = jnp.concatenate([minus, -plus], axis=0)
        for tiles in pairs(rows):
            out = half_dot(left, map_tiles(held, real, tiles))
            out = out + half_dot(crossed, map_tiles(held, imag, tiles))
            out = out.astype(bf16).astype(f32)
            for i, t in enumerate(tiles):
                at = slice(i * channels, (i + 1) * channels)
                dz[base + t] = out[:edges, at].T
                dz[base + rows + t] = out[edges:, at].T

    def body(start):
        at = pl.ds(start, CHUNK)
        for l in range(LMAX + 1):
            for j in COEFS_OF[l]:
                acc = None
                for k in ROWS_OF[l]:
                    term = wide[k, j : j + 1, :] * dz[k, at, :]
                    acc = term if acc is None else acc + term
                gp[j, at, :] = acc.astype(bf16)

    chunks(channels, body)
    both = (hot_rows(ids[1:2, :], count) + hot_rows(ids[0:1, :], count)).astype(bf16)
    by_owner(both, gp, grads, group)
    grads[:, node_rows(own) :, :] = jnp.zeros(
        (group, grads.shape[1] - node_rows(own), channels), bf16
    )


def node_rows(own):
    return -(-COEF * own // 16) * 16


def sum_kernel(parts, scale, nodes, tail, acc):
    group, own = parts.shape[0], nodes.shape[0]
    span = node_rows(own)
    total = jnp.zeros((span, LANES), f32)
    for g in range(group):
        part = parts[g, :span, :].astype(f32).reshape(span // 8, 8, LANES)
        total = total + (part * scale[g][None]).reshape(span, LANES)
    acc[...] = total
    for n in range(own):
        nodes[n] = acc[pl.ds(n, COEF, stride=own), :].astype(bf16)
    tail[...] = jnp.sum(parts[:, span:, :].astype(f32), axis=0)


def per_channel(values, channels):
    rows, head_count = values.shape
    return jnp.broadcast_to(values[:, :, None], (rows, head_count, channels // head_count)).reshape(
        rows, channels
    )


def pad_to(block, rows, columns):
    return jnp.pad(block, ((0, rows - block.shape[0]), (0, columns - block.shape[1])))


def whole_lanes(count):
    return -(-count // LANES) * LANES


def column_tiles(block):
    rows, columns = block.shape
    tiles = block.reshape(rows, columns // LANES, LANES)
    return jnp.transpose(tiles, (1, 0, 2)).reshape(-1, LANES)


def gather_weights(shards):
    rows = [w.shape[0] for w in shards]
    columns = [w.shape[1] for w in shards]
    most = max(columns)
    packed = jnp.concatenate([pad_to(w.T, most, w.shape[0]) for w in shards], axis=1)
    packed = pad_to(packed, most, whole_lanes(packed.shape[1]))
    near = lax.all_gather(packed, "core")
    blocks, at = [], 0
    for r, n in zip(rows, columns):
        blocks.append(near[:, :n, at : at + r].reshape(2 * n, r))
        at += r
    first = lax.axis_index("core") == 0
    sets = ((0, 1), (2, 3, 4))
    lanes = whole_lanes(max(sum(rows[i] for i in s) for s in sets))
    sent = [
        pad_to(
            jnp.concatenate([pad_to(blocks[i], 2 * most, rows[i]) for i in s], axis=1),
            2 * most,
            lanes,
        )
        for s in sets
    ]
    slabs = gather(jnp.where(first, sent[0], sent[1]), ROW_GROUP)
    pieces = slabs.reshape(2, -1, 2 * most, lanes)
    whole = [r * pieces.shape[1] for r in rows]
    tiled = []
    for s in sets:
        at, parts = 0, []
        for i in s:
            piece = pieces[:, :, : 2 * columns[i], at : at + rows[i]]
            at += rows[i]
            piece = jnp.transpose(piece, (0, 2, 1, 3)).reshape(4 * columns[i], whole[i])
            parts.append(column_tiles(piece))
        tiled.append(jnp.concatenate(parts, axis=0))
    depth = max(t.shape[0] for t in tiled)
    tiled = [pad_to(t, depth, LANES) for t in tiled]
    half = lax.all_gather(jnp.where(first, tiled[0], tiled[1]), "z")
    places = [None] * len(shards)
    for half_index, s in enumerate(sets):
        at = 0
        for i in s:
            places[i] = (half_index, at, 4 * columns[i])
            at += whole[i] // LANES * 4 * columns[i]
    return half, places, slabs


def on_device(
    embeddings,
    atom_counts,
    edge_counts,
    source,
    target,
    wigner,
    cotangent,
    w_zero,
    w_one_real,
    w_one_imag,
    w_two_real,
    w_two_imag,
    attention,
):
    half, places, slabs = gather_weights((w_zero, w_one_real, w_one_imag, w_two_real, w_two_imag))
    row_count = embeddings.shape[1]
    harmonics = embeddings.shape[2]
    channels = embeddings.shape[3]
    width = harmonics * channels
    edge_rows = source.shape[1]
    head_count = attention.shape[1]
    group = lax.axis_size(GRAPH)
    all_nodes = row_count * group
    rotation = wigner[0]
    in_use = (lax.iota(jnp.int32, edge_rows) < edge_counts[0, 0]).astype(jnp.int32)
    ids = jnp.stack([source[0], target[0], in_use] + [jnp.zeros_like(in_use)] * 5)
    attention_t = attention.T
    core = lax.axis_index("core")
    first = core.astype(jnp.int32).reshape(1, 1)
    own_first = lax.axis_index(GRAPH) * row_count
    present = ((own_first + lax.iota(jnp.int32, row_count)) < atom_counts[0])[:, None]
    cot_rows = jnp.where(present, cotangent[0].reshape(row_count, width), 0.0).astype(bf16)
    own_rows = jnp.concatenate([embeddings[0].reshape(row_count, width), cot_rows], axis=1)
    own_rows, slabs = lax.optimization_barrier((own_rows, slabs))
    nodes = gather(own_rows, GRAPH).reshape(all_nodes, 2 * width)

    smem = pl.BlockSpec(memory_space=pltpu.SMEM)
    field = (channels, edge_rows)
    wide = pltpu.VMEM(rotation.shape, f32)
    z, grad_edge = pl.pallas_call(
        rotate_kernel,
        out_shape=(
            jax.ShapeDtypeStruct((REDUCED,) + field, bf16),
            jax.ShapeDtypeStruct((COEF,) + field, bf16),
        ),
        in_specs=[VMEM] * 3,
        out_specs=[VMEM] * 2,
        scratch_shapes=[pltpu.VMEM((COEF,) + field, f32), wide],
        compiler_params=PARAMS,
    )(ids, nodes, rotation)
    half, z, grad_edge = lax.optimization_barrier((half, z, grad_edge))
    other = lax.ppermute(half, "core", [(0, 1), (1, 0)])
    held = pltpu.VMEM((2,) + half.shape, bf16)
    copies = pltpu.SemaphoreType.DMA((2,))

    span = node_rows(row_count)
    message_sums, stats, scalar, per_edge = pl.pallas_call(
        functools.partial(forward_kernel, places, group),
        out_shape=(
            jax.ShapeDtypeStruct((group, span + 4 * head_count, channels), bf16),
            jax.ShapeDtypeStruct((head_count, 2 * all_nodes), f32),
            jax.ShapeDtypeStruct(field, f32),
            jax.ShapeDtypeStruct((2 * head_count, edge_rows), f32),
        ),
        in_specs=[smem] + [VMEM] * 5 + [ANY] * 2,
        out_specs=[VMEM] * 4,
        scratch_shapes=[
            held,
            pltpu.VMEM((REDUCED * channels, edge_rows), f32),
            wide,
            pltpu.VMEM(field, f32),
            pltpu.VMEM((COEF,) + field, bf16),
            pltpu.VMEM(field, f32),
            copies,
        ],
        compiler_params=PARAMS,
    )(first, ids, z, rotation, grad_edge, attention_t, half, other)
    received = exchange(message_sums, GRAPH)

    columns = lax.axis_size(COLUMN_GROUP)
    depth = channels * (LMAX + 1)
    share = depth // (2 * columns)
    padded = -(-(share + 2) // 16) * 16
    partial = jax.ShapeDtypeStruct((columns, padded, depth), bf16)
    grad_rows, mine, theirs, every = pl.pallas_call(
        functools.partial(backward_kernel, half.shape[0]),
        out_shape=(
            jax.ShapeDtypeStruct((edge_rows, REDUCED * channels), bf16),
            partial,
            partial,
            jax.ShapeDtypeStruct((group, head_count, channels), f32),
        ),
        in_specs=[smem] + [VMEM] * 10,
        out_specs=[VMEM] * 4,
        scratch_shapes=[
            wide,
            pltpu.VMEM(field, f32),
            pltpu.VMEM((REDUCED * channels, edge_rows), f32),
            pltpu.VMEM((depth + padded, depth), f32),
        ],
        compiler_params=PARAMS,
    )(first, ids, stats, received, scalar, per_edge, rotation, grad_edge, attention, attention_t, z)

    theirs = lax.ppermute(theirs, "core", [(0, 1), (1, 0)])
    mine = (mine.astype(f32) + theirs.astype(f32)).astype(bf16)
    zero_parts = exchange(mine, COLUMN_GROUP)
    zero_sum = jnp.sum(zero_parts.astype(f32), axis=0)
    att_flat = zero_sum[share : share + 2].reshape(-1)[: head_count * channels]
    zero_send = jnp.transpose(zero_sum[:share].reshape(share, group, -1), (1, 0, 2))
    inner = zero_send.shape[2]
    lanes = whole_lanes(inner)
    zero_send = jnp.pad(zero_send, ((0, 0), (0, 0), (0, lanes - inner)))
    zero_send = zero_send.reshape(group, share * lanes // LANES, LANES)
    att_send = jnp.broadcast_to(
        att_flat.reshape(1, head_count, channels), (group, head_count, channels)
    )
    last_rows = jnp.concatenate([zero_send, att_send], axis=1).astype(bf16)
    rest = -last_rows.shape[1] % 16
    last_rows = jnp.pad(last_rows, ((0, 0), (0, rest), (0, 0)))

    grad_sums = pl.pallas_call(
        functools.partial(scatter_kernel, places, group, row_count),
        out_shape=jax.ShapeDtypeStruct((group, span + last_rows.shape[1], channels), bf16),
        in_specs=[smem] + [VMEM] * 3 + [ANY] * 2,
        out_specs=VMEM,
        scratch_shapes=[
            held,
            wide,
            pltpu.VMEM((REDUCED,) + field, f32),
            pltpu.VMEM((COEF,) + field, bf16),
            copies,
        ],
        compiler_params=PARAMS,
    )(first, ids, grad_rows, rotation, half, other)
    grad_sums = lax.dynamic_update_slice(grad_sums, last_rows, (0, span, 0))
    last = exchange(grad_sums, GRAPH)

    def sum_parts(parts, scale):
        return pl.pallas_call(
            sum_kernel,
            out_shape=(
                jax.ShapeDtypeStruct((row_count, harmonics, channels), bf16),
                jax.ShapeDtypeStruct((parts.shape[1] - span, channels), f32),
            ),
            in_specs=[VMEM] * 2,
            out_specs=[VMEM] * 2,
            scratch_shapes=[pltpu.VMEM((span, channels), f32)],
            compiler_params=PARAMS,
        )(parts, scale)

    sums = lax.dynamic_slice_in_dim(every, own_first, row_count, axis=2)
    sums = jnp.transpose(sums, (0, 2, 1))
    total = jnp.sum(sums, axis=0)
    own_shares = jnp.where(present, sums / jnp.where(total > 0.0, total, 1.0), 0.0)
    scale = per_channel(own_shares.reshape(-1, head_count), channels)
    scale = jnp.tile(scale.reshape(group, row_count, channels), (1, 8 // row_count, 1))
    update, _ = sum_parts(received, scale)
    grad_nodes, tail = sum_parts(last, jnp.ones_like(scale))
    tail = tail * (1.0 / (2 * columns))
    zero_rows = share * lanes // LANES
    grad_zero = tail[:zero_rows].reshape(share, lanes)[:, :inner].T
    grad_att = tail[zero_rows : zero_rows + head_count].T

    shape = (1, row_count, harmonics, channels)
    return (update.reshape(shape), grad_nodes.reshape(shape), grad_zero, grad_att)


def solution(mesh):
    columns, group = mesh.shape["dp"], mesh.shape["graph"]
    devices = mesh.devices.reshape(2, columns // 4, 2, group // 2, 2)
    fine = Mesh(devices, DP + GRAPH)
    in_specs = (
        P(DP, GRAPH, None, None),
        P(DP),
        P(DP, GRAPH),
        P(DP, GRAPH),
        P(DP, GRAPH),
        P(DP, None, None, GRAPH),
        P(DP, GRAPH, None, None),
        P(GRAPH, DP),
        P(GRAPH, DP),
        P(GRAPH, DP),
        P(GRAPH, DP),
        P(GRAPH, DP),
        P(),
    )
    out_specs = (P(DP, GRAPH, None, None), P(DP, GRAPH, None, None), P(GRAPH, DP), P())
    return jax.shard_map(
        on_device, mesh=fine, in_specs=in_specs, out_specs=out_specs, check_vma=False
    )
```

```python
import functools

import jax
import jax.numpy as jnp
from jax import lax
from jax.experimental import pallas as pl
from jax.experimental.pallas import tpu as pltpu
from jax.sharding import Mesh, PartitionSpec as P

LMAX = 6
LANES = 128
DP = ("xh", "z", "core")
COLUMN_GROUP = ("xh", "z")
ROW_GROUP = ("xh", "y", "xl")
GRAPH = ("y", "xl")
precise = lax.Precision.HIGHEST
f32 = jnp.float32
bf16 = jnp.bfloat16


def half_dot(left, right):
    return jnp.dot(left, right, preferred_element_type=f32)


def full_dot(left, right):
    return jnp.dot(left, right, precision=precise, preferred_element_type=f32)


def gather(block, axes):
    count = lax.axis_size(axes)
    copies = jnp.broadcast_to(block[None], (count,) + block.shape)
    return lax.all_to_all(copies, axes, split_axis=0, concat_axis=0, tiled=True)


def exchange(blocks, axes):
    return lax.all_to_all(blocks, axes, split_axis=0, concat_axis=0, tiled=True)


ROW_DEGREE = (
    list(range(LMAX + 1)) + list(range(1, LMAX + 1)) * 2 + list(range(2, LMAX + 1)) * 2
)
ROWS_OF = [[k for k, d in enumerate(ROW_DEGREE) if d == l] for l in range(LMAX + 1)]
COEFS_OF = [list(range(l * l, (l + 1) * (l + 1))) for l in range(LMAX + 1)]
REDUCED = len(ROW_DEGREE)
COEF = (LMAX + 1) ** 2
ZERO = (0, LMAX + 1)
ONE = (LMAX + 1, LMAX)
TWO = (3 * LMAX + 1, LMAX - 1)
CHUNK = 32
VMEM = pl.BlockSpec(memory_space=pltpu.VMEM)
ANY = pl.BlockSpec(memory_space=pl.ANY)
PARAMS = pltpu.CompilerParams(vmem_limit_bytes=48 * 1024 * 1024)


def nt_dot(left, right):
    return lax.dot_general(left, right, (((1,), (1,)), ((), ())), preferred_element_type=f32)


def nt_full(left, right):
    return lax.dot_general(
        left, right, (((1,), (1,)), ((), ())), precision=precise, preferred_element_type=f32
    )


def hot_rows(ids, count):
    rows = lax.broadcasted_iota(jnp.int32, (count, ids.shape[1]), 0)
    return (rows == ids).astype(f32)


def widen(values, channels):
    heads, edges = values.shape
    wide = jnp.broadcast_to(values[:, None, :], (heads, channels // heads, edges))
    return wide.reshape(channels, edges)


def chunks(channels, body):
    def step(i, carry):
        body(pl.multiple_of(i * CHUNK, CHUNK))
        return carry

    lax.fori_loop(0, channels // CHUNK, step, 0)


def rows_at(k, start):
    return pl.ds(pl.multiple_of(k * LANES + start, CHUNK), CHUNK)


def copy_weights(first, mine, other, held, sems):
    def go(low, high):
        one = pltpu.make_async_copy(low, held.at[0], sems.at[0])
        two = pltpu.make_async_copy(high, held.at[1], sems.at[1])
        one.start()
        two.start()
        one.wait()
        two.wait()

    @pl.when(first == 0)
    def _():
        go(mine, other)

    @pl.when(first != 0)
    def _():
        go(other, mine)


def map_tiles(held, place, tiles):
    half, at, rows = place
    parts = []
    for t in tiles:
        part = held[half, :, at + t * rows : at + (t + 1) * rows, :]
        parts.append(part.reshape(-1, LANES))
    return parts[0] if len(parts) == 1 else jnp.concatenate(parts, axis=1)


def pairs(count):
    return [tuple(range(i, min(i + 2, count))) for i in range(0, count, 2)]


def spread(blocks, held, rows, base, out):
    zs = held.shape[1]
    size = rows // 2
    for z in range(zs):
        for xh in range(2):
            to = base + (xh * zs + z) * size
            at = (z * 2 + xh) * size
            out[to : to + size, :] = blocks[at : at + size, :]


def by_owner(target, turned, out, group):
    channels = turned.shape[1]
    own = target.shape[0] // group
    per = 16 // own
    for first in range(0, COEF, per):
        parts = []
        for j in range(first, first + per):
            if j < COEF:
                part = nt_dot(target, turned[j])
            else:
                part = jnp.zeros((target.shape[0], channels), f32)
            parts.append(part.reshape(group, 1, own, channels))
        block = jnp.concatenate(parts, axis=1).reshape(group, 16, channels)
        out[:, first * own : first * own + 16, :] = block.astype(bf16)


def pack_kernel(places, *refs):
    shards, out, acc = refs[:-2], refs[-2], refs[-1]
    acc[...] = jnp.zeros_like(acc)
    for shard, at in zip(shards, places):
        rows, columns = shard.shape
        lane = lax.broadcasted_iota(jnp.int32, (rows, acc.shape[1]), 1)
        row = lax.broadcasted_iota(jnp.int32, (rows, acc.shape[1]), 0)
        place = (lane == row + at).astype(bf16)
        acc[:columns, :] += lax.dot_general(
            shard[...], place, (((0,), (0,)), ((), ())), preferred_element_type=f32
        )
    out[...] = acc[...].astype(bf16)


def share_kernel(stats, every, message, out):
    group = message.shape[0]
    count = stats.shape[1] // 2
    total = jnp.sum(every[:, :, :count], axis=0)
    share = stats[:, :count] / jnp.where(total > 0.0, total, 1.0)
    scale = widen(share, LANES).T.reshape(group, 1, count // group, LANES)
    per = 16 * group // count
    scale = jnp.broadcast_to(scale, (group, per, count // group, LANES)).reshape(group, 16, LANES)
    for at in range(0, message.shape[1], 16):
        part = message[:, at : at + 16, :].astype(f32) * scale
        out[:, at : at + 16, :] = part.astype(bf16)


def rotate_kernel(ids, nodes, wigner, z, grad_edge, paired, wide):
    count, edges = nodes.shape[0], wigner.shape[2]
    channels = LANES
    target = hot_rows(ids[1:2, :], count)
    both = (target + hot_rows(ids[0:1, :], count)).astype(bf16)
    target = target.astype(bf16)
    wide[...] = wigner[...].astype(f32)
    for j in range(COEF):
        at = slice(j * channels, (j + 1) * channels)
        paired[j] = half_dot(nodes[:, at].T, both).astype(bf16).astype(f32)
        at = slice((COEF + j) * channels, (COEF + j + 1) * channels)
        grad_edge[j] = half_dot(nodes[:, at].T, target).astype(bf16)
    for l in range(LMAX + 1):
        for k in ROWS_OF[l]:
            acc = None
            for j in COEFS_OF[l]:
                term = wide[k, j : j + 1, :] * paired[j]
                acc = term if acc is None else acc + term
            z[k] = acc.astype(bf16)


def forward_kernel(
    places,
    group,
    first,
    ids,
    z,
    wigner,
    grad_edge,
    attention_t,
    mine,
    other,
    message,
    stats,
    scalar,
    per_edge,
    held,
    y,
    wide,
    norm,
    msg,
    heads_acc,
    sems,
):
    channels, edges = LANES, wigner.shape[2]
    heads = attention_t.shape[0]
    count = stats.shape[1] // 2
    copy_weights(first[0, 0], mine, other, held, sems)
    wide[...] = wigner[...].astype(f32)
    base, rows = ZERO
    acc = None
    for tiles in pairs(rows):
        right = z[tiles[0] : tiles[-1] + 1].reshape(-1, edges)
        term = half_dot(map_tiles(held, places[0], tiles), right)
        acc = term if acc is None else acc + term
    spread(acc, held, places[0][2], base, y)
    for (base, rows), real, imag in ((ONE, places[1], places[2]), (TWO, places[3], places[4])):
        acc = None
        for tiles in pairs(rows):
            lo, hi = base + tiles[0], base + tiles[-1] + 1
            plus = z[lo:hi].reshape(-1, edges)
            minus = z[lo + rows : hi + rows].reshape(-1, edges)
            term = half_dot(map_tiles(held, real, tiles), jnp.concatenate([plus, minus], axis=1))
            term = term + half_dot(
                map_tiles(held, imag, tiles), jnp.concatenate([-minus, plus], axis=1)
            )
            acc = term if acc is None else acc + term
        spread(acc[:, :edges], held, real[2], base * channels, y)
        spread(acc[:, edges:], held, real[2], (base + rows) * channels, y)
    value = y[:channels, :]
    scalar[...] = value
    y[...] = y[...].astype(bf16).astype(f32)
    gating = (value / (1.0 + jnp.exp(-value))).astype(bf16)
    logits = half_dot(attention_t[...], gating)
    weight = jnp.where(ids[2:3, :] > 0, jnp.exp(logits), 0.0)
    target = hot_rows(ids[1:2, :], count)
    own_sum = nt_full(weight, target)
    at_edges = full_dot(own_sum, target)
    own_norm = weight / jnp.where(at_edges > 0.0, at_edges, 1.0)
    norm[...] = widen(own_norm, channels)

    def body(start):
        at = pl.ds(start, CHUNK)
        own = norm[at, :]
        total = jnp.zeros((CHUNK, edges), f32)
        for l in range(LMAX + 1):
            for j in COEFS_OF[l]:
                acc = None
                for k in ROWS_OF[l]:
                    term = wide[k, j : j + 1, :] * y[rows_at(k, start), :]
                    acc = term if acc is None else acc + term
                total = total + acc * grad_edge[j, at, :].astype(f32)
                msg[j, at, :] = (acc * own).astype(bf16)
        heads_acc[at, :] = total

    chunks(channels, body)
    grad_norm = jnp.sum(heads_acc[...].reshape(heads, channels // heads, edges), axis=1)
    own_shared = nt_full(own_norm * grad_norm, target)
    stats[...] = jnp.concatenate([own_sum, own_shared], axis=1)
    per_edge[:heads, :] = own_norm
    per_edge[heads:, :] = grad_norm
    by_owner(target.astype(bf16), msg, message, group)


def backward_kernel(
    first,
    ids,
    stats,
    every,
    scalar,
    per_edge,
    wigner,
    grad_edge,
    attention,
    attention_t,
    z,
    grad_conv,
    mine,
    theirs,
    wide,
    norm,
    grad,
    turned,
):
    channels, edges = LANES, wigner.shape[2]
    heads = attention_t.shape[0]
    count = stats.shape[1] // 2
    wide[...] = wigner[...].astype(f32)
    total = jnp.sum(every[:, :, :count], axis=0)
    total = jnp.where(total > 0.0, total, 1.0)
    shares = every[:, :, :count] / total[None]
    shared = jnp.sum(shares * every[:, :, count:], axis=0)
    own_share = stats[:, :count] / total
    target = hot_rows(ids[1:2, :], count)
    normalized = per_edge[:heads, :] * full_dot(own_share, target)
    grad_logit = normalized * (per_edge[heads:, :] - full_dot(shared, target))
    value = scalar[...]
    sigmoid = 1.0 / (1.0 + jnp.exp(-value))
    gating = (value / (1.0 + jnp.exp(-value))).astype(bf16).astype(f32)
    att = nt_full(grad_logit, gating)
    grad_gating = full_dot(attention[...].astype(f32), grad_logit)
    grad_scalar = grad_gating * sigmoid * (1.0 + value * (1.0 - sigmoid))
    norm[...] = widen(normalized, channels)

    def body(start):
        at = pl.ds(start, CHUNK)
        own = norm[at, :]
        for l in range(LMAX + 1):
            fields = [
                (grad_edge[j, at, :].astype(f32) * own).astype(bf16).astype(f32)
                for j in COEFS_OF[l]
            ]
            for k in ROWS_OF[l]:
                acc = None
                for j, field in zip(COEFS_OF[l], fields):
                    term = wide[k, j : j + 1, :] * field
                    acc = term if acc is None else acc + term
                grad[rows_at(k, start), :] = acc

    chunks(channels, body)
    grad[:channels, :] = grad[:channels, :] + grad_scalar
    depth = (LMAX + 1) * channels
    parts, share = mine.shape[0], depth // (2 * mine.shape[0])
    grad_conv[...] = grad[...].astype(bf16)
    turned[:depth, :] = nt_dot(grad_conv[:depth, :], z[: LMAX + 1].reshape(depth, edges))
    turned[depth:, :] = jnp.zeros((turned.shape[0] - depth, depth), f32)
    padded = mine.shape[1]
    tail_row = lax.broadcasted_iota(jnp.int32, (padded, depth), 0)
    one = jnp.concatenate([att[h : h + 1, :] for h in range(LMAX + 1)], axis=1)
    two = [att[h : h + 1, :] for h in range(LMAX + 1, heads)]
    two = jnp.concatenate(two + [jnp.zeros((1, depth - len(two) * channels), f32)], axis=1)

    def store(outs):
        for core in range(2):
            for part in range(parts):
                at = (2 * part + core) * share
                block = turned[at : at + padded, :]
                block = jnp.where(tail_row == share, one, block)
                block = jnp.where(tail_row == share + 1, two, block)
                outs[core][part] = block.astype(bf16)

    @pl.when(first[0, 0] == 0)
    def _():
        store((mine, theirs))

    @pl.when(first[0, 0] != 0)
    def _():
        store((theirs, mine))


def scatter_kernel(
    places,
    group,
    own,
    first,
    ids,
    grad_conv,
    wigner,
    mine,
    other,
    grads,
    held,
    wide,
    dz,
    gp,
    grad,
    grad_rows,
    sems,
):
    channels, edges = LANES, wigner.shape[2]
    count = own * group
    copy_weights(first[0, 0], mine, other, held, sems)
    wide[...] = wigner[...].astype(f32)
    grad[...] = grad_conv[...].astype(f32)
    zs = held.shape[1]
    for base, rows in (ZERO, ONE, (ONE[0] + ONE[1], ONE[1]), TWO, (TWO[0] + TWO[1], TWO[1])):
        size = rows * channels // (2 * zs)
        blocks = []
        for zz in range(zs):
            for xh in range(2):
                at = base * channels + (xh * zs + zz) * size
                blocks.append(grad[at : at + size, :])
        ordered = jnp.concatenate(blocks, axis=0)
        for t in range(rows):
            at = slice(t * channels, (t + 1) * channels)
            to = (base + t) * channels
            grad_rows[:, to : to + channels] = ordered[at, :].T.astype(bf16)
    base, rows = ZERO
    left = grad_rows[:, : rows * channels]
    for tiles in pairs(rows):
        out = half_dot(left, map_tiles(held, places[0], tiles)).astype(bf16).astype(f32)
        for i, t in enumerate(tiles):
            dz[t] = out[:, i * channels : (i + 1) * channels].T
    for (base, rows), real, imag in ((ONE, places[1], places[2]), (TWO, places[3], places[4])):
        plus = grad_rows[:, base * channels : (base + rows) * channels]
        minus = grad_rows[:, (base + rows) * channels : (base + 2 * rows) * channels]
        left = jnp.concatenate([plus, minus], axis=0)
        crossed = jnp.concatenate([minus, -plus], axis=0)
        for tiles in pairs(rows):
            out = half_dot(left, map_tiles(held, real, tiles))
            out = out + half_dot(crossed, map_tiles(held, imag, tiles))
            out = out.astype(bf16).astype(f32)
            for i, t in enumerate(tiles):
                at = slice(i * channels, (i + 1) * channels)
                dz[base + t] = out[:edges, at].T
                dz[base + rows + t] = out[edges:, at].T

    def body(start):
        at = pl.ds(start, CHUNK)
        for l in range(LMAX + 1):
            for j in COEFS_OF[l]:
                acc = None
                for k in ROWS_OF[l]:
                    term = wide[k, j : j + 1, :] * dz[k, at, :]
                    acc = term if acc is None else acc + term
                gp[j, at, :] = acc.astype(bf16)

    chunks(channels, body)
    both = (hot_rows(ids[1:2, :], count) + hot_rows(ids[0:1, :], count)).astype(bf16)
    by_owner(both, gp, grads, group)


def node_rows(own):
    return -(-COEF * own // 16) * 16


def sum_kernel(parts, nodes, total):
    group, own = parts.shape[0], nodes.shape[0]
    acc = parts[0].astype(f32)
    for g in range(1, group):
        acc = acc + parts[g].astype(f32)
    total[...] = acc
    for n in range(own):
        nodes[n] = total[pl.ds(n, COEF, stride=own), :].astype(bf16)


def pad_to(block, rows, columns):
    return jnp.pad(block, ((0, rows - block.shape[0]), (0, columns - block.shape[1])))


def whole_lanes(count):
    return -(-count // LANES) * LANES


def column_tiles(block):
    rows, columns = block.shape
    tiles = block.reshape(rows, columns // LANES, LANES)
    return jnp.transpose(tiles, (1, 0, 2)).reshape(-1, LANES)


def gather_weights(shards):
    rows = [w.shape[0] for w in shards]
    columns = [w.shape[1] for w in shards]
    most = -(-max(columns) // 16) * 16
    sets = ((0, 1), (2, 3, 4))
    lanes = whole_lanes(max(sum(rows[i] for i in s) for s in sets))
    starts = [0] * len(shards)
    for half_index, s in enumerate(sets):
        for n, i in enumerate(s):
            starts[i] = half_index * lanes + sum(rows[j] for j in s[:n])
    packed = pl.pallas_call(
        functools.partial(pack_kernel, starts),
        out_shape=jax.ShapeDtypeStruct((most, 2 * lanes), bf16),
        in_specs=[VMEM] * len(shards),
        out_specs=VMEM,
        scratch_shapes=[pltpu.VMEM((most, 2 * lanes), f32)],
        compiler_params=PARAMS,
    )(*shards)
    near = lax.all_gather(packed, "core")
    core = lax.axis_index("core")
    first = core == 0
    sent = lax.dynamic_slice_in_dim(near, core * lanes, lanes, axis=2)
    slabs = gather(sent.reshape(2 * most, lanes), ROW_GROUP)
    pieces = slabs.reshape(2, -1, 2, most, lanes)
    whole = [r * pieces.shape[1] for r in rows]
    tiled = []
    for s in sets:
        at, parts = 0, []
        for i in s:
            piece = pieces[:, :, :, : columns[i], at : at + rows[i]]
            at += rows[i]
            piece = jnp.transpose(piece, (0, 2, 3, 1, 4)).reshape(4 * columns[i], whole[i])
            parts.append(column_tiles(piece))
        tiled.append(jnp.concatenate(parts, axis=0))
    depth = max(t.shape[0] for t in tiled)
    tiled = [pad_to(t, depth, LANES) for t in tiled]
    half = lax.all_gather(jnp.where(first, tiled[0], tiled[1]), "z")
    places = [None] * len(shards)
    for half_index, s in enumerate(sets):
        at = 0
        for i in s:
            places[i] = (half_index, at, 4 * columns[i])
            at += whole[i] // LANES * 4 * columns[i]
    return half, places, slabs


def on_device(
    embeddings,
    atom_counts,
    edge_counts,
    source,
    target,
    wigner,
    cotangent,
    w_zero,
    w_one_real,
    w_one_imag,
    w_two_real,
    w_two_imag,
    attention,
):
    half, places, slabs = gather_weights((w_zero, w_one_real, w_one_imag, w_two_real, w_two_imag))
    row_count = embeddings.shape[1]
    harmonics = embeddings.shape[2]
    channels = embeddings.shape[3]
    width = harmonics * channels
    edge_rows = source.shape[1]
    head_count = attention.shape[1]
    group = lax.axis_size(GRAPH)
    all_nodes = row_count * group
    rotation = wigner[0]
    in_use = (lax.iota(jnp.int32, edge_rows) < edge_counts[0, 0]).astype(jnp.int32)
    ids = jnp.stack([source[0], target[0], in_use] + [jnp.zeros_like(in_use)] * 5)
    attention_t = attention.T
    core = lax.axis_index("core")
    first = core.astype(jnp.int32).reshape(1, 1)
    own_first = lax.axis_index(GRAPH) * row_count
    present = ((own_first + lax.iota(jnp.int32, row_count)) < atom_counts[0])[:, None]
    cot_rows = jnp.where(present, cotangent[0].reshape(row_count, width), 0.0).astype(bf16)
    own_rows = jnp.concatenate([embeddings[0].reshape(row_count, width), cot_rows], axis=1)
    own_rows, slabs = lax.optimization_barrier((own_rows, slabs))
    nodes = gather(own_rows, GRAPH).reshape(all_nodes, 2 * width)
    half, nodes = lax.optimization_barrier((half, nodes))
    other = lax.ppermute(half, "core", [(0, 1), (1, 0)])

    smem = pl.BlockSpec(memory_space=pltpu.SMEM)
    field = (channels, edge_rows)
    wide = pltpu.VMEM(rotation.shape, f32)
    z, grad_edge = pl.pallas_call(
        rotate_kernel,
        out_shape=(
            jax.ShapeDtypeStruct((REDUCED,) + field, bf16),
            jax.ShapeDtypeStruct((COEF,) + field, bf16),
        ),
        in_specs=[VMEM] * 3,
        out_specs=[VMEM] * 2,
        scratch_shapes=[pltpu.VMEM((COEF,) + field, f32), wide],
        compiler_params=PARAMS,
    )(ids, nodes, rotation)
    held = pltpu.VMEM((2,) + half.shape, bf16)
    copies = pltpu.SemaphoreType.DMA((2,))

    span = node_rows(row_count)
    message_sums, stats, scalar, per_edge = pl.pallas_call(
        functools.partial(forward_kernel, places, group),
        out_shape=(
            jax.ShapeDtypeStruct((group, span, channels), bf16),
            jax.ShapeDtypeStruct((head_count, 2 * all_nodes), f32),
            jax.ShapeDtypeStruct(field, f32),
            jax.ShapeDtypeStruct((2 * head_count, edge_rows), f32),
        ),
        in_specs=[smem] + [VMEM] * 5 + [ANY] * 2,
        out_specs=[VMEM] * 4,
        scratch_shapes=[
            held,
            pltpu.VMEM((REDUCED * channels, edge_rows), f32),
            wide,
            pltpu.VMEM(field, f32),
            pltpu.VMEM((COEF,) + field, bf16),
            pltpu.VMEM(field, f32),
            copies,
        ],
        compiler_params=PARAMS,
    )(first, ids, z, rotation, grad_edge, attention_t, half, other)
    every = gather(stats, GRAPH)
    shared_sums = pl.pallas_call(
        share_kernel,
        out_shape=jax.ShapeDtypeStruct(message_sums.shape, bf16),
        in_specs=[VMEM] * 3,
        out_specs=VMEM,
        compiler_params=PARAMS,
    )(stats, every, message_sums)
    every, shared_sums = lax.optimization_barrier((every, shared_sums))
    summed = lax.psum_scatter(shared_sums, GRAPH, scatter_dimension=0, tiled=True)

    columns = lax.axis_size(COLUMN_GROUP)
    depth = channels * (LMAX + 1)
    share = depth // (2 * columns)
    padded = -(-(share + 2) // 16) * 16
    partial = jax.ShapeDtypeStruct((columns, padded, depth), bf16)
    grad_conv, mine, theirs = pl.pallas_call(
        backward_kernel,
        out_shape=(
            jax.ShapeDtypeStruct((REDUCED * channels, edge_rows), bf16),
            partial,
            partial,
        ),
        in_specs=[smem] + [VMEM] * 10,
        out_specs=[VMEM] * 3,
        scratch_shapes=[
            wide,
            pltpu.VMEM(field, f32),
            pltpu.VMEM((REDUCED * channels, edge_rows), f32),
            pltpu.VMEM((depth + padded, depth), f32),
        ],
        compiler_params=PARAMS,
    )(first, ids, stats, every, scalar, per_edge, rotation, grad_edge, attention, attention_t, z)

    theirs = lax.ppermute(theirs, "core", [(0, 1), (1, 0)])
    mine = (mine.astype(f32) + theirs.astype(f32)).astype(bf16)
    zero_parts = exchange(mine, COLUMN_GROUP)
    zero_sum = jnp.sum(zero_parts.astype(f32), axis=0)
    att_flat = zero_sum[share : share + 2].reshape(-1)[: head_count * channels]
    zero_send = jnp.transpose(zero_sum[:share].reshape(share, group, -1), (1, 0, 2))
    inner = zero_send.shape[2]
    lanes = whole_lanes(inner)
    zero_send = jnp.pad(zero_send, ((0, 0), (0, 0), (0, lanes - inner)))
    zero_send = zero_send.reshape(group, share * lanes // LANES, LANES)
    att = att_flat.reshape(head_count, channels)
    spare = lanes - channels // 2
    beside = spare >= max(inner, channels // 2) and share >= 2 * head_count
    if beside:
        att = jnp.pad(att.reshape(2 * head_count, -1), ((0, share - 2 * head_count), (spare, 0)))
        last_rows = zero_send + att[None]
    else:
        att = jnp.broadcast_to(att[None], (group, head_count, channels))
        last_rows = jnp.concatenate([zero_send, att], axis=1)
    last_rows = last_rows.astype(bf16)

    used = harmonics * row_count
    zero_rows = share * lanes // LANES
    grad_sums = pl.pallas_call(
        functools.partial(scatter_kernel, places, group, row_count),
        out_shape=jax.ShapeDtypeStruct(
            (group, -(-(used + last_rows.shape[1]) // 16) * 16, channels), bf16
        ),
        in_specs=[smem] + [VMEM] * 3 + [ANY] * 2,
        out_specs=VMEM,
        scratch_shapes=[
            held,
            wide,
            pltpu.VMEM((REDUCED,) + field, f32),
            pltpu.VMEM((COEF,) + field, bf16),
            pltpu.VMEM((REDUCED * channels, edge_rows), f32),
            pltpu.VMEM((edge_rows, REDUCED * channels), bf16),
            copies,
        ],
        compiler_params=PARAMS,
    )(first, ids, grad_conv, rotation, half, other)
    grad_sums = lax.dynamic_update_slice(grad_sums, last_rows, (0, used, 0))
    last = exchange(grad_sums, GRAPH)

    grad_nodes, total = pl.pallas_call(
        sum_kernel,
        out_shape=(
            jax.ShapeDtypeStruct((row_count, harmonics, channels), bf16),
            jax.ShapeDtypeStruct(last.shape[1:], f32),
        ),
        in_specs=[VMEM],
        out_specs=[VMEM] * 2,
        compiler_params=PARAMS,
    )(last)
    tail = total[used : used + last_rows.shape[1]] * (1.0 / (2 * columns))
    grad_zero = tail[:zero_rows].reshape(share, lanes)[:, :inner].T
    if beside:
        grad_att = tail[: 2 * head_count, spare:].reshape(head_count, channels).T
    else:
        grad_att = tail[zero_rows:].T
    update = summed[0, :used].reshape(harmonics, row_count, channels)
    update = jnp.where(present[None], update, jnp.zeros_like(update))
    update = jnp.transpose(update, (1, 0, 2))

    shape = (1, row_count, harmonics, channels)
    return (update.reshape(shape), grad_nodes.reshape(shape), grad_zero, grad_att)


def solution(mesh):
    columns, group = mesh.shape["dp"], mesh.shape["graph"]
    devices = mesh.devices.reshape(2, columns // 4, 2, group // 2, 2)
    fine = Mesh(devices, DP + GRAPH)
    in_specs = (
        P(DP, GRAPH, None, None),
        P(DP),
        P(DP, GRAPH),
        P(DP, GRAPH),
        P(DP, GRAPH),
        P(DP, None, None, GRAPH),
        P(DP, GRAPH, None, None),
        P(GRAPH, DP),
        P(GRAPH, DP),
        P(GRAPH, DP),
        P(GRAPH, DP),
        P(GRAPH, DP),
        P(),
    )
    out_specs = (P(DP, GRAPH, None, None), P(DP, GRAPH, None, None), P(GRAPH, DP), P())
    return jax.shard_map(
        on_device, mesh=fine, in_specs=in_specs, out_specs=out_specs, check_vma=False
    )
```

```python
import functools

import jax
import jax.numpy as jnp
from jax import lax
from jax.experimental import pallas as pl
from jax.experimental.pallas import tpu as pltpu
from jax.sharding import Mesh, PartitionSpec as P

LMAX = 6
LANES = 128
DP = ("xh", "z", "core")
COLUMN_GROUP = ("xh", "z")
ROW_GROUP = ("xh", "y", "xl")
GRAPH = ("y", "xl")
precise = lax.Precision.HIGHEST
f32 = jnp.float32
bf16 = jnp.bfloat16


def half_dot(left, right):
    return jnp.dot(left, right, preferred_element_type=f32)


def full_dot(left, right):
    return jnp.dot(left, right, precision=precise, preferred_element_type=f32)


def gather(block, axes):
    count = lax.axis_size(axes)
    copies = jnp.broadcast_to(block[None], (count,) + block.shape)
    return lax.all_to_all(copies, axes, split_axis=0, concat_axis=0, tiled=True)


def exchange(blocks, axes):
    return lax.all_to_all(blocks, axes, split_axis=0, concat_axis=0, tiled=True)


ROW_DEGREE = (
    list(range(LMAX + 1)) + list(range(1, LMAX + 1)) * 2 + list(range(2, LMAX + 1)) * 2
)
ROWS_OF = [[k for k, d in enumerate(ROW_DEGREE) if d == l] for l in range(LMAX + 1)]
COEFS_OF = [list(range(l * l, (l + 1) * (l + 1))) for l in range(LMAX + 1)]
REDUCED = len(ROW_DEGREE)
COEF = (LMAX + 1) ** 2
ZERO = (0, LMAX + 1)
ONE = (LMAX + 1, LMAX)
TWO = (3 * LMAX + 1, LMAX - 1)
CHUNK = 32
VMEM = pl.BlockSpec(memory_space=pltpu.VMEM)
ANY = pl.BlockSpec(memory_space=pl.ANY)
PARAMS = pltpu.CompilerParams(vmem_limit_bytes=48 * 1024 * 1024)


def nt_dot(left, right):
    return lax.dot_general(left, right, (((1,), (1,)), ((), ())), preferred_element_type=f32)


def nt_full(left, right):
    return lax.dot_general(
        left, right, (((1,), (1,)), ((), ())), precision=precise, preferred_element_type=f32
    )


def hot_rows(ids, count):
    rows = lax.broadcasted_iota(jnp.int32, (count, ids.shape[1]), 0)
    return (rows == ids).astype(f32)


def widen(values, channels):
    heads, edges = values.shape
    wide = jnp.broadcast_to(values[:, None, :], (heads, channels // heads, edges))
    return wide.reshape(channels, edges)


def chunks(channels, body):
    def step(i, carry):
        body(pl.multiple_of(i * CHUNK, CHUNK))
        return carry

    lax.fori_loop(0, channels // CHUNK, step, 0)


def rows_at(k, start):
    return pl.ds(pl.multiple_of(k * LANES + start, CHUNK), CHUNK)


def start_weights(places, first, mine, other, held, sems):
    def go(halves):
        for i, (half, at, rows, tiles) in enumerate(places):
            span = pl.ds(at, tiles * rows)
            pltpu.make_async_copy(
                halves[half].at[:, span, :], held.at[half, :, span, :], sems.at[i]
            ).start()

    @pl.when(first == 0)
    def _():
        go((mine, other))

    @pl.when(first != 0)
    def _():
        go((other, mine))


def wait_weights(places, which, mine, held, sems):
    for i in which:
        half, at, rows, tiles = places[i]
        span = pl.ds(at, tiles * rows)
        pltpu.make_async_copy(mine.at[:, span, :], held.at[half, :, span, :], sems.at[i]).wait()


def map_tiles(held, place, tiles):
    half, at, rows, _ = place
    parts = []
    for t in tiles:
        part = held[half, :, at + t * rows : at + (t + 1) * rows, :]
        parts.append(part.reshape(-1, LANES))
    return parts[0] if len(parts) == 1 else jnp.concatenate(parts, axis=1)


def pairs(count):
    return [tuple(range(i, min(i + 2, count))) for i in range(0, count, 2)]


def spread(blocks, held, rows, base, out):
    zs = held.shape[1]
    size = rows // 2
    for z in range(zs):
        for xh in range(2):
            to = base + (xh * zs + z) * size
            at = (z * 2 + xh) * size
            out[to : to + size, :] = blocks[at : at + size, :]


def by_owner(target, turned, out, group, scale=None):
    channels = turned.shape[1]
    own = target.shape[0] // group
    per = 16 // own
    for first in range(0, COEF, per):
        parts = []
        for j in range(first, first + per):
            if j < COEF:
                part = nt_dot(target, turned[j])
                part = part if scale is None else part * scale
            else:
                part = jnp.zeros((target.shape[0], channels), f32)
            parts.append(part.reshape(group, 1, own, channels))
        block = jnp.concatenate(parts, axis=1).reshape(group, 16, channels)
        out[:, first * own : first * own + 16, :] = block.astype(bf16)


def pack_kernel(places, *refs):
    shards, out, acc = refs[:-2], refs[-2], refs[-1]
    acc[...] = jnp.zeros_like(acc)
    for shard, at in zip(shards, places):
        columns, rows = shard.shape
        lane = lax.broadcasted_iota(jnp.int32, (rows, acc.shape[1]), 1)
        row = lax.broadcasted_iota(jnp.int32, (rows, acc.shape[1]), 0)
        acc[:columns, :] += half_dot(shard[...], (lane == row + at).astype(bf16))
    out[...] = acc[...].astype(bf16)


def slab_kernel(sets, first, slabs, out):
    group, most, lanes = slabs.shape[0] // 2, slabs.shape[1] // 2, slabs.shape[2]
    blocks = [jnp.concatenate([slabs[g], slabs[group + g]], axis=0) for g in range(group)]

    def lay(which):
        to = 0
        for rows, columns, at in which:
            size = 4 * columns
            row = lax.broadcasted_iota(jnp.int32, (size, 4 * most), 0)
            lane = lax.broadcasted_iota(jnp.int32, (size, 4 * most), 1)
            kept = row // columns * most + row % columns
            chosen = (lane == kept).astype(bf16)
            source = lax.broadcasted_iota(jnp.int32, (lanes, LANES), 0)
            place = lax.broadcasted_iota(jnp.int32, (lanes, LANES), 1)
            for t in range(group * rows // LANES):
                acc = None
                for g in range(group):
                    if g * rows >= (t + 1) * LANES or (g + 1) * rows <= t * LANES:
                        continue
                    shift = g * rows - t * LANES - at
                    hit = (place == source + shift) & (source >= at) & (source < at + rows)
                    term = half_dot(blocks[g], hit.astype(bf16))
                    acc = term if acc is None else acc + term
                tile = half_dot(chosen, acc.astype(bf16))
                out[to : to + size, :] = tile.astype(bf16)
                to += size
        if to < out.shape[0]:
            out[to:, :] = jnp.zeros((out.shape[0] - to, LANES), bf16)

    @pl.when(first[0, 0] == 0)
    def _():
        lay(sets[0])

    @pl.when(first[0, 0] != 0)
    def _():
        lay(sets[1])


def message_kernel(ids, stats, every, msg, out):
    group = out.shape[0]
    count = stats.shape[1] // 2
    total = jnp.sum(every[:, :, :count], axis=0)
    share = stats[:, :count] / jnp.where(total > 0.0, total, 1.0)
    scale = widen(share, LANES).T
    by_owner(hot_rows(ids[1:2, :], count).astype(bf16), msg, out, group, scale)


def rotate_kernel(own, ids, nodes, wigner, z, grad_edge, paired, wide):
    group, edges = nodes.shape[0], wigner.shape[2]
    channels = LANES
    per = 16 // (2 * own)
    count = own * group
    target = hot_rows(ids[1:2, :], count)
    both = (target + hot_rows(ids[0:1, :], count)).astype(bf16)
    target = target.astype(bf16)
    wide[...] = wigner[...].astype(f32)
    for first in range(0, COEF, per):
        rows = nodes[:, first * 2 * own : first * 2 * own + 16, :].astype(f32)
        rows = rows.reshape(group, 2 * per, own, channels)
        for j in range(first, min(first + per, COEF)):
            at = 2 * (j - first)
            here = rows[:, at].reshape(count, channels).T.astype(bf16)
            paired[j] = half_dot(here, both).astype(bf16).astype(f32)
            here = rows[:, at + 1].reshape(count, channels).T.astype(bf16)
            grad_edge[j] = half_dot(here, target).astype(bf16)
    for l in range(LMAX + 1):
        for k in ROWS_OF[l]:
            acc = None
            for j in COEFS_OF[l]:
                term = wide[k, j : j + 1, :] * paired[j]
                acc = term if acc is None else acc + term
            z[k] = acc.astype(bf16)


def forward_kernel(
    places,
    group,
    first,
    ids,
    z,
    wigner,
    grad_edge,
    attention_t,
    mine,
    other,
    messages,
    stats,
    sent,
    scalar,
    per_edge,
    held,
    y,
    wide,
    norm,
    msg,
    heads_acc,
    sems,
    out_sem,
):
    channels, edges = LANES, wigner.shape[2]
    heads = attention_t.shape[0]
    count = stats.shape[1] // 2
    start_weights(places, first[0, 0], mine, other, held, sems)
    wide[...] = wigner[...].astype(f32)
    base, rows = ZERO
    acc = None
    wait_weights(places, (0,), mine, held, sems)
    for tiles in pairs(rows):
        right = z[tiles[0] : tiles[-1] + 1].reshape(-1, edges)
        term = half_dot(map_tiles(held, places[0], tiles), right)
        acc = term if acc is None else acc + term
    spread(acc, held, places[0][2], base, y)
    for (base, rows), real, imag in ((ONE, places[1], places[2]), (TWO, places[3], places[4])):
        wait_weights(places, (1, 2) if base == ONE[0] else (3, 4), mine, held, sems)
        acc = None
        for tiles in pairs(rows):
            lo, hi = base + tiles[0], base + tiles[-1] + 1
            plus = z[lo:hi].reshape(-1, edges)
            minus = z[lo + rows : hi + rows].reshape(-1, edges)
            term = half_dot(map_tiles(held, real, tiles), jnp.concatenate([plus, minus], axis=1))
            term = term + half_dot(
                map_tiles(held, imag, tiles), jnp.concatenate([-minus, plus], axis=1)
            )
            acc = term if acc is None else acc + term
        spread(acc[:, :edges], held, real[2], base * channels, y)
        spread(acc[:, edges:], held, real[2], (base + rows) * channels, y)
    value = y[:channels, :]
    scalar[...] = value
    y[...] = y[...].astype(bf16).astype(f32)
    gating = (value / (1.0 + jnp.exp(-value))).astype(bf16)
    logits = half_dot(attention_t[...], gating)
    weight = jnp.where(ids[2:3, :] > 0, jnp.exp(logits), 0.0)
    target = hot_rows(ids[1:2, :], count)
    own_sum = nt_full(weight, target)
    at_edges = full_dot(own_sum, target)
    own_norm = weight / jnp.where(at_edges > 0.0, at_edges, 1.0)
    norm[...] = widen(own_norm, channels)

    def body(start):
        at = pl.ds(start, CHUNK)
        own = norm[at, :]
        total = jnp.zeros((CHUNK, edges), f32)
        for l in range(LMAX + 1):
            for j in COEFS_OF[l]:
                acc = None
                for k in ROWS_OF[l]:
                    term = wide[k, j : j + 1, :] * y[rows_at(k, start), :]
                    acc = term if acc is None else acc + term
                total = total + acc * grad_edge[j, at, :].astype(f32)
                msg[j, at, :] = (acc * own).astype(bf16)
        heads_acc[at, :] = total

    chunks(channels, body)
    copy = pltpu.make_async_copy(msg, messages, out_sem.at[0])
    copy.start()
    grad_norm = jnp.sum(heads_acc[...].reshape(heads, channels // heads, edges), axis=1)
    own_shared = nt_full(own_norm * grad_norm, target)
    sums = jnp.concatenate([own_sum, own_shared], axis=1)
    stats[...] = sums
    for owner in range(group):
        sent[owner] = sums
    per_edge[:heads, :] = own_norm
    per_edge[heads:, :] = grad_norm
    copy.wait()


def backward_kernel(
    first,
    ids,
    stats,
    every,
    scalar,
    per_edge,
    wigner,
    grad_edge,
    attention,
    attention_t,
    z,
    grad_out,
    mine,
    theirs,
    wide,
    norm,
    grad,
    turned,
    grad_conv,
    out_sem,
):
    channels, edges = LANES, wigner.shape[2]
    heads = attention_t.shape[0]
    count = stats.shape[1] // 2
    wide[...] = wigner[...].astype(f32)
    total = jnp.sum(every[:, :, :count], axis=0)
    total = jnp.where(total > 0.0, total, 1.0)
    shares = every[:, :, :count] / total[None]
    shared = jnp.sum(shares * every[:, :, count:], axis=0)
    own_share = stats[:, :count] / total
    target = hot_rows(ids[1:2, :], count)
    normalized = per_edge[:heads, :] * full_dot(own_share, target)
    grad_logit = normalized * (per_edge[heads:, :] - full_dot(shared, target))
    value = scalar[...]
    sigmoid = 1.0 / (1.0 + jnp.exp(-value))
    gating = (value / (1.0 + jnp.exp(-value))).astype(bf16).astype(f32)
    att = nt_full(grad_logit, gating)
    grad_gating = full_dot(attention[...].astype(f32), grad_logit)
    grad_scalar = grad_gating * sigmoid * (1.0 + value * (1.0 - sigmoid))
    norm[...] = widen(normalized, channels)

    def body(start):
        at = pl.ds(start, CHUNK)
        own = norm[at, :]
        for l in range(LMAX + 1):
            fields = [
                (grad_edge[j, at, :].astype(f32) * own).astype(bf16).astype(f32)
                for j in COEFS_OF[l]
            ]
            for k in ROWS_OF[l]:
                acc = None
                for j, field in zip(COEFS_OF[l], fields):
                    term = wide[k, j : j + 1, :] * field
                    acc = term if acc is None else acc + term
                grad[rows_at(k, start), :] = acc

    chunks(channels, body)
    grad[:channels, :] = grad[:channels, :] + grad_scalar
    depth = (LMAX + 1) * channels
    parts, share = mine.shape[0], depth // (2 * mine.shape[0])
    grad_conv[...] = grad[...].astype(bf16)
    copy = pltpu.make_async_copy(grad_conv, grad_out, out_sem.at[0])
    copy.start()
    turned[:depth, :] = nt_dot(grad_conv[:depth, :], z[: LMAX + 1].reshape(depth, edges))
    turned[depth:, :] = jnp.zeros((turned.shape[0] - depth, depth), f32)
    padded = mine.shape[1]
    tail_row = lax.broadcasted_iota(jnp.int32, (padded, depth), 0)
    one = jnp.concatenate([att[h : h + 1, :] for h in range(LMAX + 1)], axis=1)
    two = [att[h : h + 1, :] for h in range(LMAX + 1, heads)]
    two = jnp.concatenate(two + [jnp.zeros((1, depth - len(two) * channels), f32)], axis=1)

    def store(outs):
        for core in range(2):
            for part in range(parts):
                at = (2 * part + core) * share
                block = turned[at : at + padded, :]
                block = jnp.where(tail_row == share, one, block)
                block = jnp.where(tail_row == share + 1, two, block)
                outs[core][part] = block.astype(bf16)

    @pl.when(first[0, 0] == 0)
    def _():
        store((mine, theirs))

    @pl.when(first[0, 0] != 0)
    def _():
        store((theirs, mine))

    copy.wait()


def scatter_kernel(
    places,
    group,
    own,
    first,
    ids,
    grad_conv,
    wigner,
    mine,
    other,
    grads,
    held,
    wide,
    dz,
    gp,
    grad,
    grad_rows,
    sems,
):
    channels, edges = LANES, wigner.shape[2]
    count = own * group
    start_weights(places, first[0, 0], mine, other, held, sems)
    wide[...] = wigner[...].astype(f32)
    grad[...] = grad_conv[...].astype(f32)
    zs = held.shape[1]
    for base, rows in (ZERO, ONE, (ONE[0] + ONE[1], ONE[1]), TWO, (TWO[0] + TWO[1], TWO[1])):
        size = rows * channels // (2 * zs)
        blocks = []
        for zz in range(zs):
            for xh in range(2):
                at = base * channels + (xh * zs + zz) * size
                blocks.append(grad[at : at + size, :])
        ordered = jnp.concatenate(blocks, axis=0)
        for t in range(rows):
            at = slice(t * channels, (t + 1) * channels)
            to = (base + t) * channels
            grad_rows[:, to : to + channels] = ordered[at, :].T.astype(bf16)
    base, rows = ZERO
    left = grad_rows[:, : rows * channels]
    wait_weights(places, (0,), mine, held, sems)
    for tiles in pairs(rows):
        out = half_dot(left, map_tiles(held, places[0], tiles)).astype(bf16).astype(f32)
        for i, t in enumerate(tiles):
            dz[t] = out[:, i * channels : (i + 1) * channels].T
    for (base, rows), real, imag in ((ONE, places[1], places[2]), (TWO, places[3], places[4])):
        wait_weights(places, (1, 2) if base == ONE[0] else (3, 4), mine, held, sems)
        plus = grad_rows[:, base * channels : (base + rows) * channels]
        minus = grad_rows[:, (base + rows) * channels : (base + 2 * rows) * channels]
        left = jnp.concatenate([plus, minus], axis=0)
        crossed = jnp.concatenate([minus, -plus], axis=0)
        for tiles in pairs(rows):
            out = half_dot(left, map_tiles(held, real, tiles))
            out = out + half_dot(crossed, map_tiles(held, imag, tiles))
            out = out.astype(bf16).astype(f32)
            for i, t in enumerate(tiles):
                at = slice(i * channels, (i + 1) * channels)
                dz[base + t] = out[:edges, at].T
                dz[base + rows + t] = out[edges:, at].T

    def body(start):
        at = pl.ds(start, CHUNK)
        for l in range(LMAX + 1):
            for j in COEFS_OF[l]:
                acc = None
                for k in ROWS_OF[l]:
                    term = wide[k, j : j + 1, :] * dz[k, at, :]
                    acc = term if acc is None else acc + term
                gp[j, at, :] = acc.astype(bf16)

    chunks(channels, body)
    both = (hot_rows(ids[1:2, :], count) + hot_rows(ids[0:1, :], count)).astype(bf16)
    by_owner(both, gp, grads, group)


def node_rows(own):
    return -(-COEF * own // 16) * 16


def sum_kernel(parts, nodes, tail, total):
    group = parts.shape[0]
    acc = parts[0].astype(f32)
    for g in range(1, group):
        acc = acc + parts[g].astype(f32)
    total[...] = acc
    used = nodes.shape[0] * nodes.shape[1]
    nodes[...] = acc[:used].astype(bf16).reshape(nodes.shape)
    tail[...] = total[used : used + tail.shape[0], :]


def pad_to(block, rows, columns):
    return jnp.pad(block, ((0, rows - block.shape[0]), (0, columns - block.shape[1])))


def whole_lanes(count):
    return -(-count // LANES) * LANES


def gather_weights(shards):
    rows = [w.shape[0] for w in shards]
    columns = [w.shape[1] for w in shards]
    most = -(-max(columns) // 16) * 16
    sets = ((0, 1), (2, 3, 4))
    lanes = whole_lanes(max(sum(rows[i] for i in s) for s in sets))
    starts = [0] * len(shards)
    for half_index, s in enumerate(sets):
        for n, i in enumerate(s):
            starts[i] = half_index * lanes + sum(rows[j] for j in s[:n])
    packed = pl.pallas_call(
        functools.partial(pack_kernel, starts),
        out_shape=jax.ShapeDtypeStruct((most, 2 * lanes), bf16),
        in_specs=[VMEM] * len(shards),
        out_specs=VMEM,
        scratch_shapes=[pltpu.VMEM((most, 2 * lanes), f32)],
        compiler_params=PARAMS,
    )(*[w.T for w in shards])
    core = lax.axis_index("core")
    near = lax.all_gather(packed, "core")
    sent = lax.dynamic_slice_in_dim(near, core * lanes, lanes, axis=2)
    slabs = gather(sent.reshape(2 * most, lanes), ROW_GROUP)
    group = slabs.shape[0] // 2
    places = [None] * len(shards)
    depth = 0
    for half_index, s in enumerate(sets):
        at = 0
        for i in s:
            tiles = group * rows[i] // LANES
            places[i] = (half_index, at, 4 * columns[i], tiles)
            at += tiles * 4 * columns[i]
        depth = max(depth, at)
    kinds = [[(rows[i], columns[i], starts[i] - n * lanes) for i in s] for n, s in enumerate(sets)]
    tiled = pl.pallas_call(
        functools.partial(slab_kernel, kinds),
        out_shape=jax.ShapeDtypeStruct((depth, LANES), bf16),
        in_specs=[pl.BlockSpec(memory_space=pltpu.SMEM), VMEM],
        out_specs=VMEM,
        compiler_params=PARAMS,
    )(core.astype(jnp.int32).reshape(1, 1), slabs)
    return lax.all_gather(tiled, "z"), places, tiled


def on_device(
    embeddings,
    atom_counts,
    edge_counts,
    source,
    target,
    wigner,
    cotangent,
    w_zero,
    w_one_real,
    w_one_imag,
    w_two_real,
    w_two_imag,
    attention,
):
    half, places, tiled = gather_weights((w_zero, w_one_real, w_one_imag, w_two_real, w_two_imag))
    row_count = embeddings.shape[1]
    harmonics = embeddings.shape[2]
    channels = embeddings.shape[3]
    width = harmonics * channels
    edge_rows = source.shape[1]
    head_count = attention.shape[1]
    group = lax.axis_size(GRAPH)
    all_nodes = row_count * group
    rotation = wigner[0]
    in_use = (lax.iota(jnp.int32, edge_rows) < edge_counts[0, 0]).astype(jnp.int32)
    ids = jnp.stack([source[0], target[0], in_use] + [jnp.zeros_like(in_use)] * 5)
    attention_t = attention.T
    core = lax.axis_index("core")
    first = core.astype(jnp.int32).reshape(1, 1)
    own_first = lax.axis_index(GRAPH) * row_count
    present = ((own_first + lax.iota(jnp.int32, row_count)) < atom_counts[0])[:, None]
    cot_rows = jnp.where(present[:, :, None], cotangent[0], 0.0).astype(bf16)
    own_rows = jnp.stack([embeddings[0], cot_rows])
    own_rows = jnp.transpose(own_rows, (2, 0, 1, 3)).reshape(-1, channels)
    own_rows = pad_to(own_rows, -(-own_rows.shape[0] // 16) * 16, channels)
    own_rows, tiled = lax.optimization_barrier((own_rows, tiled))
    nodes = gather(own_rows, GRAPH)
    half, nodes = lax.optimization_barrier((half, nodes))
    other = lax.ppermute(half, "core", [(0, 1), (1, 0)])

    smem = pl.BlockSpec(memory_space=pltpu.SMEM)
    field = (channels, edge_rows)
    wide = pltpu.VMEM(rotation.shape, f32)
    z, grad_edge = pl.pallas_call(
        functools.partial(rotate_kernel, row_count),
        out_shape=(
            jax.ShapeDtypeStruct((REDUCED,) + field, bf16),
            jax.ShapeDtypeStruct((COEF,) + field, bf16),
        ),
        in_specs=[VMEM] * 3,
        out_specs=[VMEM] * 2,
        scratch_shapes=[pltpu.VMEM((COEF,) + field, f32), wide],
        compiler_params=PARAMS,
    )(ids, nodes, rotation)
    held = pltpu.VMEM((2,) + half.shape, bf16)
    copies = pltpu.SemaphoreType.DMA((len(places),))
    out_copy = pltpu.SemaphoreType.DMA((1,))

    span = node_rows(row_count)
    sums = (head_count, 2 * all_nodes)
    messages, stats, sent, scalar, per_edge = pl.pallas_call(
        functools.partial(forward_kernel, places, group),
        out_shape=(
            jax.ShapeDtypeStruct((COEF,) + field, bf16),
            jax.ShapeDtypeStruct(sums, f32),
            jax.ShapeDtypeStruct((group,) + sums, f32),
            jax.ShapeDtypeStruct(field, f32),
            jax.ShapeDtypeStruct((2 * head_count, edge_rows), f32),
        ),
        in_specs=[smem] + [VMEM] * 5 + [ANY] * 2,
        out_specs=[ANY] + [VMEM] * 4,
        scratch_shapes=[
            held,
            pltpu.VMEM((REDUCED * channels, edge_rows), f32),
            wide,
            pltpu.VMEM(field, f32),
            pltpu.VMEM((COEF,) + field, bf16),
            pltpu.VMEM(field, f32),
            copies,
            out_copy,
        ],
        compiler_params=PARAMS,
    )(first, ids, z, rotation, grad_edge, attention_t, half, other)
    every = exchange(sent, GRAPH)

    columns = lax.axis_size(COLUMN_GROUP)
    depth = channels * (LMAX + 1)
    share = depth // (2 * columns)
    padded = -(-(share + 2) // 16) * 16
    partial = jax.ShapeDtypeStruct((columns, padded, depth), bf16)
    grad_conv, mine, theirs = pl.pallas_call(
        backward_kernel,
        out_shape=(
            jax.ShapeDtypeStruct((REDUCED * channels, edge_rows), bf16),
            partial,
            partial,
        ),
        in_specs=[smem] + [VMEM] * 10,
        out_specs=[ANY] + [VMEM] * 2,
        scratch_shapes=[
            wide,
            pltpu.VMEM(field, f32),
            pltpu.VMEM((REDUCED * channels, edge_rows), f32),
            pltpu.VMEM((depth + padded, depth), f32),
            pltpu.VMEM((REDUCED * channels, edge_rows), bf16),
            out_copy,
        ],
        compiler_params=PARAMS,
    )(first, ids, stats, every, scalar, per_edge, rotation, grad_edge, attention, attention_t, z)

    theirs = lax.ppermute(theirs, "core", [(0, 1), (1, 0)])
    mine = (mine.astype(f32) + theirs.astype(f32)).astype(bf16)
    mine, messages = lax.optimization_barrier((mine, messages))
    zero_parts = exchange(mine, COLUMN_GROUP)
    message_sums = pl.pallas_call(
        message_kernel,
        out_shape=jax.ShapeDtypeStruct((group, span, channels), bf16),
        in_specs=[VMEM] * 4,
        out_specs=VMEM,
        compiler_params=PARAMS,
    )(ids, stats, every, messages)
    message_sums = message_sums.reshape(group // 2, 2 * span, channels)
    near_sums = lax.psum_scatter(message_sums, "y", scatter_dimension=0, tiled=True)
    near_sums = near_sums.reshape(2, span, channels)
    side = lax.axis_index("xl")
    kept = lax.dynamic_index_in_dim(near_sums, side, keepdims=False)
    passed = lax.dynamic_index_in_dim(near_sums, 1 - side, keepdims=False)
    passed = lax.ppermute(passed, "xl", [(0, 1), (1, 0)])
    summed = kept.astype(f32) + passed.astype(f32)
    zero_sum = jnp.sum(zero_parts.astype(f32), axis=0)
    att_flat = zero_sum[share : share + 2].reshape(-1)[: head_count * channels]
    zero_send = jnp.transpose(zero_sum[:share].reshape(share, group, -1), (1, 0, 2))
    inner = zero_send.shape[2]
    lanes = whole_lanes(inner)
    zero_send = jnp.pad(zero_send, ((0, 0), (0, 0), (0, lanes - inner)))
    zero_send = zero_send.reshape(group, share * lanes // LANES, LANES)
    att = att_flat.reshape(head_count, channels)
    used = harmonics * row_count
    spare = lanes - channels // 2
    beside = spare >= max(inner, channels // 2) and share >= 2 * head_count
    if beside:
        att = jnp.concatenate([att[:, :spare], att[:, spare:]], axis=0)
        att = jnp.pad(att, ((0, share - 2 * head_count), (spare, 0)))
        last_rows = zero_send + att[None]
    else:
        att = jnp.broadcast_to(att[None], (group, head_count, channels))
        last_rows = jnp.concatenate([zero_send, att], axis=1)
    last_rows = last_rows.astype(bf16)

    zero_rows = share * lanes // LANES
    grad_sums = pl.pallas_call(
        functools.partial(scatter_kernel, places, group, row_count),
        out_shape=jax.ShapeDtypeStruct(
            (group, -(-(used + last_rows.shape[1]) // 16) * 16, channels), bf16
        ),
        in_specs=[smem] + [VMEM] * 3 + [ANY] * 2,
        out_specs=VMEM,
        scratch_shapes=[
            held,
            wide,
            pltpu.VMEM((REDUCED,) + field, f32),
            pltpu.VMEM((COEF,) + field, bf16),
            pltpu.VMEM((REDUCED * channels, edge_rows), f32),
            pltpu.VMEM((edge_rows, REDUCED * channels), bf16),
            copies,
        ],
        compiler_params=PARAMS,
    )(first, ids, grad_conv, rotation, half, other)
    grad_sums = lax.dynamic_update_slice(grad_sums, last_rows, (0, used, 0))
    last = exchange(grad_sums, GRAPH)

    grad_nodes, tail = pl.pallas_call(
        sum_kernel,
        out_shape=(
            jax.ShapeDtypeStruct((harmonics, row_count, channels), bf16),
            jax.ShapeDtypeStruct(last_rows.shape[1:], f32),
        ),
        in_specs=[VMEM],
        out_specs=[VMEM] * 2,
        scratch_shapes=[pltpu.VMEM(last.shape[1:], f32)],
        compiler_params=PARAMS,
    )(last)
    tail = tail * (1.0 / (2 * columns))
    grad_zero = tail[:zero_rows].reshape(share, lanes)[:, :inner].T
    if beside:
        grad_att = jnp.concatenate(
            [tail[:head_count, spare:], tail[head_count : 2 * head_count, spare:]], axis=1
        ).T
    else:
        grad_att = tail[zero_rows:].T
    update = summed[:used].reshape(harmonics, row_count, channels)
    update = jnp.transpose(jnp.where(present[None], update, 0.0).astype(bf16), (1, 0, 2))
    grad_nodes = jnp.transpose(grad_nodes, (1, 0, 2))

    shape = (1, row_count, harmonics, channels)
    return (update.reshape(shape), grad_nodes.reshape(shape), grad_zero, grad_att)


def solution(mesh):
    columns, group = mesh.shape["dp"], mesh.shape["graph"]
    devices = mesh.devices.reshape(2, columns // 4, 2, group // 2, 2)
    fine = Mesh(devices, DP + GRAPH)
    in_specs = (
        P(DP, GRAPH, None, None),
        P(DP),
        P(DP, GRAPH),
        P(DP, GRAPH),
        P(DP, GRAPH),
        P(DP, None, None, GRAPH),
        P(DP, GRAPH, None, None),
        P(GRAPH, DP),
        P(GRAPH, DP),
        P(GRAPH, DP),
        P(GRAPH, DP),
        P(GRAPH, DP),
        P(),
    )
    out_specs = (P(DP, GRAPH, None, None), P(DP, GRAPH, None, None), P(GRAPH, DP), P())
    return jax.shard_map(
        on_device, mesh=fine, in_specs=in_specs, out_specs=out_specs, check_vma=False
    )
```

```python
import functools

import jax
import jax.numpy as jnp
from jax import lax
from jax.experimental import pallas as pl
from jax.experimental.pallas import tpu as pltpu
from jax.sharding import Mesh, PartitionSpec as P

LMAX = 6
LANES = 128
DP = ("xh", "z", "core")
COLUMN_GROUP = ("xh", "z")
ROW_GROUP = ("xh", "y", "xl")
GRAPH = ("y", "xl")
precise = lax.Precision.HIGHEST
f32 = jnp.float32
bf16 = jnp.bfloat16


def half_dot(left, right):
    return jnp.dot(left, right, preferred_element_type=f32)


def full_dot(left, right):
    return jnp.dot(left, right, precision=precise, preferred_element_type=f32)


def gather(block, axes):
    count = lax.axis_size(axes)
    copies = jnp.broadcast_to(block[None], (count,) + block.shape)
    return lax.all_to_all(copies, axes, split_axis=0, concat_axis=0, tiled=True)


def exchange(blocks, axes):
    return lax.all_to_all(blocks, axes, split_axis=0, concat_axis=0, tiled=True)


ROW_DEGREE = (
    list(range(LMAX + 1)) + list(range(1, LMAX + 1)) * 2 + list(range(2, LMAX + 1)) * 2
)
ROWS_OF = [[k for k, d in enumerate(ROW_DEGREE) if d == l] for l in range(LMAX + 1)]
COEFS_OF = [list(range(l * l, (l + 1) * (l + 1))) for l in range(LMAX + 1)]
REDUCED = len(ROW_DEGREE)
COEF = (LMAX + 1) ** 2
ZERO = (0, LMAX + 1)
ONE = (LMAX + 1, LMAX)
TWO = (3 * LMAX + 1, LMAX - 1)
CHUNK = 32
VMEM = pl.BlockSpec(memory_space=pltpu.VMEM)
HBM = pl.BlockSpec(memory_space=pltpu.HBM)
PARAMS = pltpu.CompilerParams(vmem_limit_bytes=28 * 1024 * 1024)


def nt_dot(left, right):
    return lax.dot_general(left, right, (((1,), (1,)), ((), ())), preferred_element_type=f32)


def nt_full(left, right):
    return lax.dot_general(
        left, right, (((1,), (1,)), ((), ())), precision=precise, preferred_element_type=f32
    )


def hot_rows(ids, count):
    rows = lax.broadcasted_iota(jnp.int32, (count, ids.shape[1]), 0)
    return (rows == ids).astype(f32)


def widen(values, channels):
    heads, edges = values.shape
    wide = jnp.broadcast_to(values[:, None, :], (heads, channels // heads, edges))
    return wide.reshape(channels, edges)


def chunks(channels, body):
    def step(i, carry):
        body(pl.multiple_of(i * CHUNK, CHUNK))
        return carry

    lax.fori_loop(0, channels // CHUNK, step, 0)


def rows_at(k, start):
    return pl.ds(pl.multiple_of(k * LANES + start, CHUNK), CHUNK)


def start_weights(places, first, mine, other, held, sems):
    def go(halves):
        for i, (half, at, rows, tiles) in enumerate(places):
            span = pl.ds(at, tiles * rows)
            pltpu.make_async_copy(
                halves[half].at[:, span, :], held.at[half, :, span, :], sems.at[i]
            ).start()

    @pl.when(first == 0)
    def _():
        go((mine, other))

    @pl.when(first != 0)
    def _():
        go((other, mine))


def wait_weights(places, which, mine, held, sems):
    for i in which:
        half, at, rows, tiles = places[i]
        span = pl.ds(at, tiles * rows)
        pltpu.make_async_copy(mine.at[:, span, :], held.at[half, :, span, :], sems.at[i]).wait()


def map_tiles(held, place, tiles):
    half, at, rows, _ = place
    parts = []
    for t in tiles:
        part = held[half, :, at + t * rows : at + (t + 1) * rows, :]
        parts.append(part.reshape(-1, LANES))
    return parts[0] if len(parts) == 1 else jnp.concatenate(parts, axis=1)


def pairs(count):
    return [tuple(range(i, min(i + 2, count))) for i in range(0, count, 2)]


def spread(blocks, held, rows, base, out):
    zs = held.shape[1]
    size = rows // 2
    for z in range(zs):
        for xh in range(2):
            to = base + (xh * zs + z) * size
            at = (z * 2 + xh) * size
            out[to : to + size, :] = blocks[at : at + size, :]


def by_owner(target, turned, out, group, scale=None):
    channels = turned.shape[1]
    own = target.shape[0] // group
    per = 16 // own
    for first in range(0, COEF, per):
        parts = []
        for j in range(first, first + per):
            if j < COEF:
                part = nt_dot(target, turned[j])
                part = part if scale is None else part * scale
            else:
                part = jnp.zeros((target.shape[0], channels), f32)
            parts.append(part.reshape(group, 1, own, channels))
        block = jnp.concatenate(parts, axis=1).reshape(group, 16, channels)
        out[:, first * own : first * own + 16, :] = block.astype(bf16)


def pack_kernel(places, *refs):
    count = len(places)
    shards, out = refs[:count], refs[count]
    held, acc, sems = refs[count + 1 : -2], refs[-2], refs[-1]
    copies = [pltpu.make_async_copy(shards[i], held[i], sems.at[i]) for i in range(count)]
    for copy in copies:
        copy.start()
    acc[...] = jnp.zeros_like(acc)
    for copy, shard, at in zip(copies, held, places):
        columns, rows = shard.shape
        lane = lax.broadcasted_iota(jnp.int32, (rows, acc.shape[1]), 1)
        row = lax.broadcasted_iota(jnp.int32, (rows, acc.shape[1]), 0)
        place = (lane == row + at).astype(bf16)
        copy.wait()
        acc[:columns, :] += half_dot(shard[...], place)
    out[...] = acc[...].astype(bf16)


def slab_kernel(sets, first, slabs, out):
    group, most, lanes = slabs.shape[0] // 2, slabs.shape[1] // 2, slabs.shape[2]
    blocks = [jnp.concatenate([slabs[g], slabs[group + g]], axis=0) for g in range(group)]

    def lay(which):
        to = 0
        for rows, columns, at in which:
            size = 4 * columns
            row = lax.broadcasted_iota(jnp.int32, (size, 4 * most), 0)
            lane = lax.broadcasted_iota(jnp.int32, (size, 4 * most), 1)
            kept = row // columns * most + row % columns
            chosen = (lane == kept).astype(bf16)
            source = lax.broadcasted_iota(jnp.int32, (lanes, LANES), 0)
            place = lax.broadcasted_iota(jnp.int32, (lanes, LANES), 1)
            for t in range(group * rows // LANES):
                acc = None
                for g in range(group):
                    if g * rows >= (t + 1) * LANES or (g + 1) * rows <= t * LANES:
                        continue
                    shift = g * rows - t * LANES - at
                    hit = (place == source + shift) & (source >= at) & (source < at + rows)
                    term = half_dot(blocks[g], hit.astype(bf16))
                    acc = term if acc is None else acc + term
                tile = half_dot(chosen, acc.astype(bf16))
                out[to : to + size, :] = tile.astype(bf16)
                to += size
        if to < out.shape[0]:
            out[to:, :] = jnp.zeros((out.shape[0] - to, LANES), bf16)

    @pl.when(first[0, 0] == 0)
    def _():
        lay(sets[0])

    @pl.when(first[0, 0] != 0)
    def _():
        lay(sets[1])


def message_kernel(ids, stats, every, msg, out):
    group = out.shape[0]
    count = stats.shape[1] // 2
    total = jnp.sum(every[:, :, :count], axis=0)
    share = stats[:, :count] / jnp.where(total > 0.0, total, 1.0)
    scale = widen(share, LANES).T
    by_owner(hot_rows(ids[1:2, :], count).astype(bf16), msg, out, group, scale)


def rotate_kernel(own, ids, nodes, wigner, z, edge_out, paired, wide, grad_edge, out_sem):
    group, edges = nodes.shape[0], wigner.shape[2]
    channels = LANES
    per = 16 // (2 * own)
    count = own * group
    target = hot_rows(ids[1:2, :], count)
    both = (target + hot_rows(ids[0:1, :], count)).astype(bf16)
    target = target.astype(bf16)
    wide[...] = wigner[...].astype(f32)
    for first in range(0, COEF, per):
        rows = nodes[:, first * 2 * own : first * 2 * own + 16, :].astype(f32)
        rows = rows.reshape(group, 2 * per, own, channels)
        for j in range(first, min(first + per, COEF)):
            at = 2 * (j - first)
            here = rows[:, at].reshape(count, channels).T.astype(bf16)
            paired[j] = half_dot(here, both).astype(bf16).astype(f32)
            here = rows[:, at + 1].reshape(count, channels).T.astype(bf16)
            grad_edge[j] = half_dot(here, target).astype(bf16)
    copy = pltpu.make_async_copy(grad_edge, edge_out, out_sem.at[0])
    copy.start()
    for l in range(LMAX + 1):
        for k in ROWS_OF[l]:
            acc = None
            for j in COEFS_OF[l]:
                term = wide[j, k : k + 1, :] * paired[j]
                acc = term if acc is None else acc + term
            z[k] = acc.astype(bf16)
    copy.wait()


def forward_kernel(
    places,
    group,
    first,
    ids,
    z,
    wigner,
    edge_in,
    attention_t,
    mine,
    other,
    messages,
    stats,
    sent,
    scalar,
    per_edge,
    held,
    y,
    wide,
    norm,
    msg,
    heads_acc,
    grad_edge,
    sems,
    out_sem,
):
    channels, edges = LANES, wigner.shape[2]
    heads = attention_t.shape[0]
    count = stats.shape[1] // 2
    start_weights(places, first[0, 0], mine, other, held, sems)
    edge_copy = pltpu.make_async_copy(edge_in, grad_edge, out_sem.at[1])
    edge_copy.start()
    wide[...] = wigner[...].astype(f32)
    base, rows = ZERO
    acc = None
    wait_weights(places, (0,), mine, held, sems)
    for tiles in pairs(rows):
        right = z[tiles[0] : tiles[-1] + 1].reshape(-1, edges)
        term = half_dot(map_tiles(held, places[0], tiles), right)
        acc = term if acc is None else acc + term
    spread(acc, held, places[0][2], base, y)
    for (base, rows), real, imag in ((ONE, places[1], places[2]), (TWO, places[3], places[4])):
        wait_weights(places, (1, 2) if base == ONE[0] else (3, 4), mine, held, sems)
        acc = None
        for tiles in pairs(rows):
            lo, hi = base + tiles[0], base + tiles[-1] + 1
            plus = z[lo:hi].reshape(-1, edges)
            minus = z[lo + rows : hi + rows].reshape(-1, edges)
            term = half_dot(map_tiles(held, real, tiles), jnp.concatenate([plus, minus], axis=1))
            term = term + half_dot(
                map_tiles(held, imag, tiles), jnp.concatenate([-minus, plus], axis=1)
            )
            acc = term if acc is None else acc + term
        spread(acc[:, :edges], held, real[2], base * channels, y)
        spread(acc[:, edges:], held, real[2], (base + rows) * channels, y)
    value = y[:channels, :]
    scalar[...] = value
    y[...] = y[...].astype(bf16).astype(f32)
    gating = (value / (1.0 + jnp.exp(-value))).astype(bf16)
    logits = half_dot(attention_t[...], gating)
    weight = jnp.where(ids[2:3, :] > 0, jnp.exp(logits), 0.0)
    target = hot_rows(ids[1:2, :], count)
    own_sum = nt_full(weight, target)
    at_edges = full_dot(own_sum, target)
    own_norm = weight / jnp.where(at_edges > 0.0, at_edges, 1.0)
    norm[...] = widen(own_norm, channels)

    def body(start):
        at = pl.ds(start, CHUNK)
        own = norm[at, :]
        total = jnp.zeros((CHUNK, edges), f32)
        for l in range(LMAX + 1):
            for j in COEFS_OF[l]:
                acc = None
                for k in ROWS_OF[l]:
                    term = wide[j, k : k + 1, :] * y[rows_at(k, start), :]
                    acc = term if acc is None else acc + term
                total = total + acc * grad_edge[j, at, :].astype(f32)
                msg[j, at, :] = (acc * own).astype(bf16)
        heads_acc[at, :] = total

    edge_copy.wait()
    chunks(channels, body)
    copy = pltpu.make_async_copy(msg, messages, out_sem.at[0])
    copy.start()
    grad_norm = jnp.sum(heads_acc[...].reshape(heads, channels // heads, edges), axis=1)
    own_shared = nt_full(own_norm * grad_norm, target)
    sums = jnp.concatenate([own_sum, own_shared], axis=1)
    stats[...] = sums
    for owner in range(group):
        sent[owner] = sums
    per_edge[:heads, :] = own_norm
    per_edge[heads:, :] = grad_norm
    copy.wait()


def backward_kernel(
    first,
    ids,
    stats,
    every,
    scalar,
    per_edge,
    wigner,
    edge_in,
    attention,
    attention_t,
    z,
    grad_out,
    mine,
    theirs,
    wide,
    norm,
    grad,
    turned,
    grad_conv,
    grad_edge,
    out_sem,
):
    channels, edges = LANES, wigner.shape[2]
    heads = attention_t.shape[0]
    count = stats.shape[1] // 2
    edge_copy = pltpu.make_async_copy(edge_in, grad_edge, out_sem.at[1])
    edge_copy.start()
    wide[...] = wigner[...].astype(f32)
    total = jnp.sum(every[:, :, :count], axis=0)
    total = jnp.where(total > 0.0, total, 1.0)
    shares = every[:, :, :count] / total[None]
    shared = jnp.sum(shares * every[:, :, count:], axis=0)
    own_share = stats[:, :count] / total
    target = hot_rows(ids[1:2, :], count)
    normalized = per_edge[:heads, :] * full_dot(own_share, target)
    grad_logit = normalized * (per_edge[heads:, :] - full_dot(shared, target))
    value = scalar[...]
    sigmoid = 1.0 / (1.0 + jnp.exp(-value))
    gating = (value / (1.0 + jnp.exp(-value))).astype(bf16).astype(f32)
    att = nt_full(grad_logit, gating)
    grad_gating = full_dot(attention[...].astype(f32), grad_logit)
    grad_scalar = grad_gating * sigmoid * (1.0 + value * (1.0 - sigmoid))
    norm[...] = widen(normalized, channels)

    def body(start):
        at = pl.ds(start, CHUNK)
        own = norm[at, :]
        for l in range(LMAX + 1):
            fields = [
                (grad_edge[j, at, :].astype(f32) * own).astype(bf16).astype(f32)
                for j in COEFS_OF[l]
            ]
            for k in ROWS_OF[l]:
                acc = None
                for j, field in zip(COEFS_OF[l], fields):
                    term = wide[j, k : k + 1, :] * field
                    acc = term if acc is None else acc + term
                grad[rows_at(k, start), :] = acc

    edge_copy.wait()
    chunks(channels, body)
    grad[:channels, :] = grad[:channels, :] + grad_scalar
    depth = (LMAX + 1) * channels
    parts, share = mine.shape[0], depth // (2 * mine.shape[0])
    grad_conv[...] = grad[...].astype(bf16)
    copy = pltpu.make_async_copy(grad_conv, grad_out, out_sem.at[0])
    copy.start()
    turned[:depth, :] = nt_dot(grad_conv[:depth, :], z[: LMAX + 1].reshape(depth, edges))
    turned[depth:, :] = jnp.zeros((turned.shape[0] - depth, depth), f32)
    padded = mine.shape[1]
    tail_row = lax.broadcasted_iota(jnp.int32, (padded, depth), 0)
    one = jnp.concatenate([att[h : h + 1, :] for h in range(LMAX + 1)], axis=1)
    two = [att[h : h + 1, :] for h in range(LMAX + 1, heads)]
    two = jnp.concatenate(two + [jnp.zeros((1, depth - len(two) * channels), f32)], axis=1)

    def store(outs):
        for core in range(2):
            for part in range(parts):
                at = (2 * part + core) * share
                block = turned[at : at + padded, :]
                block = jnp.where(tail_row == share, one, block)
                block = jnp.where(tail_row == share + 1, two, block)
                outs[core][part] = block.astype(bf16)

    @pl.when(first[0, 0] == 0)
    def _():
        store((mine, theirs))

    @pl.when(first[0, 0] != 0)
    def _():
        store((theirs, mine))

    copy.wait()


def scatter_kernel(
    places,
    group,
    own,
    first,
    ids,
    grad_conv,
    wigner,
    mine,
    other,
    grads_out,
    held,
    wide,
    dz,
    gp,
    grad,
    grad_rows,
    grads,
    sems,
    out_sem,
):
    channels, edges = LANES, wigner.shape[2]
    count = own * group
    start_weights(places, first[0, 0], mine, other, held, sems)
    wide[...] = wigner[...].astype(f32)
    grad[...] = grad_conv[...].astype(f32)
    zs = held.shape[1]
    for base, rows in (ZERO, ONE, (ONE[0] + ONE[1], ONE[1]), TWO, (TWO[0] + TWO[1], TWO[1])):
        size = rows * channels // (2 * zs)
        blocks = []
        for zz in range(zs):
            for xh in range(2):
                at = base * channels + (xh * zs + zz) * size
                blocks.append(grad[at : at + size, :])
        ordered = jnp.concatenate(blocks, axis=0)
        for t in range(rows):
            at = slice(t * channels, (t + 1) * channels)
            to = (base + t) * channels
            grad_rows[:, to : to + channels] = ordered[at, :].T.astype(bf16)
    base, rows = ZERO
    left = grad_rows[:, : rows * channels]
    wait_weights(places, (0,), mine, held, sems)
    for tiles in pairs(rows):
        out = half_dot(left, map_tiles(held, places[0], tiles)).astype(bf16).astype(f32)
        for i, t in enumerate(tiles):
            dz[t] = out[:, i * channels : (i + 1) * channels].T
    for (base, rows), real, imag in ((ONE, places[1], places[2]), (TWO, places[3], places[4])):
        wait_weights(places, (1, 2) if base == ONE[0] else (3, 4), mine, held, sems)
        plus = grad_rows[:, base * channels : (base + rows) * channels]
        minus = grad_rows[:, (base + rows) * channels : (base + 2 * rows) * channels]
        left = jnp.concatenate([plus, minus], axis=0)
        crossed = jnp.concatenate([minus, -plus], axis=0)
        for tiles in pairs(rows):
            out = half_dot(left, map_tiles(held, real, tiles))
            out = out + half_dot(crossed, map_tiles(held, imag, tiles))
            out = out.astype(bf16).astype(f32)
            for i, t in enumerate(tiles):
                at = slice(i * channels, (i + 1) * channels)
                dz[base + t] = out[:edges, at].T
                dz[base + rows + t] = out[edges:, at].T

    def body(start):
        at = pl.ds(start, CHUNK)
        for l in range(LMAX + 1):
            for j in COEFS_OF[l]:
                acc = None
                for k in ROWS_OF[l]:
                    term = wide[j, k : k + 1, :] * dz[k, at, :]
                    acc = term if acc is None else acc + term
                gp[j, at, :] = acc.astype(bf16)

    chunks(channels, body)
    both = (hot_rows(ids[1:2, :], count) + hot_rows(ids[0:1, :], count)).astype(bf16)
    by_owner(both, gp, grads, group)
    whole = pl.ds(0, grads.shape[1])
    copy = pltpu.make_async_copy(grads, grads_out.at[:, whole, :], out_sem.at[0])
    copy.start()
    copy.wait()


def node_rows(own):
    return -(-COEF * own // 16) * 16


def one_hot(rows, columns, shift, low, high):
    row = lax.broadcasted_iota(jnp.int32, (rows, columns), 0)
    column = lax.broadcasted_iota(jnp.int32, (rows, columns), 1)
    return ((column == row + shift) & (row >= low) & (row < high)).astype(bf16)


def tail_kernel(used, share, heads, parts, grads_in, grads, total, att, window, sems):
    count, depth = parts.shape[0], parts.shape[2]
    group, rows = window.shape[0], window.shape[1]
    inner, skip = depth // group, used % 16
    base = used - skip
    old = pltpu.make_async_copy(
        grads_in.at[:, pl.ds(base, 16), :], window.at[:, pl.ds(0, 16), :], sems.at[0]
    )
    old.start()
    acc = parts[0].astype(f32)
    for p in range(1, count):
        acc = acc + parts[p].astype(f32)
    total[...] = acc
    for h in range(heads):
        row, at = share + h // (depth // LANES), h % (depth // LANES) * LANES
        att[h : h + 1, :] = total[row : row + 1, at : at + LANES]
    low = att[...].astype(bf16)
    half = LANES // 2
    left = half_dot(low, one_hot(LANES, LANES, half, 0, half)).astype(bf16)
    right = half_dot(low, one_hot(LANES, LANES, 0, half, LANES)).astype(bf16)
    row = lax.broadcasted_iota(jnp.int32, (rows, heads), 0)
    head = lax.broadcasted_iota(jnp.int32, (rows, heads), 1)
    tail = half_dot((row == head + skip).astype(bf16), left)
    tail = tail + half_dot((row == head + skip + heads).astype(bf16), right)
    moved = half_dot(one_hot(rows, total.shape[0], -skip, skip, skip + share), acc.astype(bf16))
    moved = moved.astype(bf16)
    kept = lax.broadcasted_iota(jnp.int32, (rows, LANES), 0) < skip
    old.wait()
    for g in range(group):
        first = g * inner // LANES * LANES
        last = -(-(g + 1) * inner // LANES) * LANES
        shift = g * inner - first
        place = one_hot(last - first, LANES, -shift, shift, shift + inner)
        piece = half_dot(moved[:, first:last], place) + tail
        before = window[g, :16, :].astype(f32)
        if rows > 16:
            before = jnp.concatenate([before, jnp.zeros((rows - 16, LANES), f32)], axis=0)
        window[g] = jnp.where(kept, before, piece).astype(bf16)
    new = pltpu.make_async_copy(window, grads.at[:, pl.ds(base, rows), :], sems.at[1])
    new.start()
    new.wait()


def last_kernel(scale, parts, nodes, zero, att, total):
    acc = parts[0].astype(f32)
    for g in range(1, parts.shape[0]):
        acc = acc + parts[g].astype(f32)
    total[...] = acc
    used = nodes.shape[0] * nodes.shape[1]
    heads, half = att.shape[0], LANES // 2
    nodes[...] = acc[:used].astype(bf16).reshape(nodes.shape)
    zero[...] = total[used : used + zero.shape[0], :][:, : zero.shape[1]] * scale
    left = full_dot(
        total[used : used + heads, :], one_hot(LANES, LANES, -half, half, LANES).astype(f32)
    )
    lane = lax.broadcasted_iota(jnp.int32, (heads, LANES), 1)
    right = jnp.where(lane >= half, total[used + heads : used + 2 * heads, :], 0.0)
    att[...] = (left + right) * scale


def sum_kernel(parts, nodes, tail, total):
    acc = parts[0].astype(f32)
    for g in range(1, parts.shape[0]):
        acc = acc + parts[g].astype(f32)
    total[...] = acc
    used = nodes.shape[0] * nodes.shape[1]
    nodes[...] = acc[:used].astype(bf16).reshape(nodes.shape)
    tail[...] = total[used : used + tail.shape[0], :]


def pad_to(block, rows, columns):
    return jnp.pad(block, ((0, rows - block.shape[0]), (0, columns - block.shape[1])))


def whole_lanes(count):
    return -(-count // LANES) * LANES


def gather_weights(shards):
    rows = [w.shape[0] for w in shards]
    columns = [w.shape[1] for w in shards]
    most = -(-max(columns) // 16) * 16
    sets = ((0, 1), (2, 3, 4))
    lanes = whole_lanes(max(sum(rows[i] for i in s) for s in sets))
    starts = [0] * len(shards)
    for half_index, s in enumerate(sets):
        for n, i in enumerate(s):
            starts[i] = half_index * lanes + sum(rows[j] for j in s[:n])
    packed = pl.pallas_call(
        functools.partial(pack_kernel, starts),
        out_shape=jax.ShapeDtypeStruct((most, 2 * lanes), bf16),
        in_specs=[HBM] * len(shards),
        out_specs=VMEM,
        scratch_shapes=[pltpu.VMEM(w.shape[::-1], bf16) for w in shards]
        + [pltpu.VMEM((most, 2 * lanes), f32), pltpu.SemaphoreType.DMA((len(shards),))],
        compiler_params=PARAMS,
    )(*[w.T for w in shards])
    core = lax.axis_index("core")
    near = lax.all_gather(packed, "core")
    sent = lax.dynamic_slice_in_dim(near, core * lanes, lanes, axis=2)
    slabs = gather(sent.reshape(2 * most, lanes), ROW_GROUP)
    group = slabs.shape[0] // 2
    places = [None] * len(shards)
    depth = 0
    for half_index, s in enumerate(sets):
        at = 0
        for i in s:
            tiles = group * rows[i] // LANES
            places[i] = (half_index, at, 4 * columns[i], tiles)
            at += tiles * 4 * columns[i]
        depth = max(depth, at)
    kinds = [[(rows[i], columns[i], starts[i] - n * lanes) for i in s] for n, s in enumerate(sets)]
    tiled = pl.pallas_call(
        functools.partial(slab_kernel, kinds),
        out_shape=jax.ShapeDtypeStruct((depth, LANES), bf16),
        in_specs=[pl.BlockSpec(memory_space=pltpu.SMEM), VMEM],
        out_specs=VMEM,
        compiler_params=PARAMS,
    )(core.astype(jnp.int32).reshape(1, 1), slabs)
    return lax.all_gather(tiled, "z"), places, tiled


def on_device(
    embeddings,
    atom_counts,
    edge_counts,
    source,
    target,
    wigner,
    cotangent,
    w_zero,
    w_one_real,
    w_one_imag,
    w_two_real,
    w_two_imag,
    attention,
):
    half, places, tiled = gather_weights((w_zero, w_one_real, w_one_imag, w_two_real, w_two_imag))
    row_count = embeddings.shape[1]
    harmonics = embeddings.shape[2]
    channels = embeddings.shape[3]
    width = harmonics * channels
    edge_rows = source.shape[1]
    head_count = attention.shape[1]
    group = lax.axis_size(GRAPH)
    all_nodes = row_count * group
    rotation = jnp.transpose(wigner[0], (1, 0, 2))
    in_use = (lax.iota(jnp.int32, edge_rows) < edge_counts[0, 0]).astype(jnp.int32)
    ids = jnp.stack([source[0], target[0], in_use] + [jnp.zeros_like(in_use)] * 5)
    attention_t = attention.T
    core = lax.axis_index("core")
    first = core.astype(jnp.int32).reshape(1, 1)
    own_first = lax.axis_index(GRAPH) * row_count
    present = ((own_first + lax.iota(jnp.int32, row_count)) < atom_counts[0])[:, None]
    cot_rows = jnp.where(present[:, :, None], cotangent[0], 0.0).astype(bf16)
    own_rows = jnp.stack([embeddings[0], cot_rows])
    own_rows = jnp.transpose(own_rows, (2, 0, 1, 3)).reshape(-1, channels)
    own_rows = pad_to(own_rows, -(-own_rows.shape[0] // 16) * 16, channels)
    own_rows, tiled = lax.optimization_barrier((own_rows, tiled))
    nodes = gather(own_rows, GRAPH)
    half, nodes = lax.optimization_barrier((half, nodes))
    other = lax.ppermute(half, "core", [(0, 1), (1, 0)])

    smem = pl.BlockSpec(memory_space=pltpu.SMEM)
    field = (channels, edge_rows)
    wide = pltpu.VMEM(rotation.shape, f32)
    out_copy = pltpu.SemaphoreType.DMA((1,))
    two_copies = pltpu.SemaphoreType.DMA((2,))
    edge_field = pltpu.VMEM((COEF,) + field, bf16)
    z, grad_edge = pl.pallas_call(
        functools.partial(rotate_kernel, row_count),
        out_shape=(
            jax.ShapeDtypeStruct((REDUCED,) + field, bf16),
            jax.ShapeDtypeStruct((COEF,) + field, bf16),
        ),
        in_specs=[VMEM] * 3,
        out_specs=[VMEM, HBM],
        scratch_shapes=[
            pltpu.VMEM((COEF,) + field, f32),
            wide,
            pltpu.VMEM((COEF,) + field, bf16),
            out_copy,
        ],
        compiler_params=PARAMS,
    )(ids, nodes, rotation)
    held = pltpu.VMEM((2,) + half.shape, bf16)
    copies = pltpu.SemaphoreType.DMA((len(places),))

    span = node_rows(row_count)
    sums = (head_count, 2 * all_nodes)
    messages, stats, sent, scalar, per_edge = pl.pallas_call(
        functools.partial(forward_kernel, places, group),
        out_shape=(
            jax.ShapeDtypeStruct((COEF,) + field, bf16),
            jax.ShapeDtypeStruct(sums, f32),
            jax.ShapeDtypeStruct((group,) + sums, f32),
            jax.ShapeDtypeStruct(field, f32),
            jax.ShapeDtypeStruct((2 * head_count, edge_rows), f32),
        ),
        in_specs=[smem] + [VMEM] * 3 + [HBM, VMEM] + [HBM] * 2,
        out_specs=[HBM] + [VMEM] * 4,
        scratch_shapes=[
            held,
            pltpu.VMEM((REDUCED * channels, edge_rows), f32),
            wide,
            pltpu.VMEM(field, f32),
            pltpu.VMEM((COEF,) + field, bf16),
            pltpu.VMEM(field, f32),
            edge_field,
            copies,
            two_copies,
        ],
        compiler_params=PARAMS,
    )(first, ids, z, rotation, grad_edge, attention_t, half, other)
    every = exchange(sent, GRAPH)

    columns = lax.axis_size(COLUMN_GROUP)
    depth = channels * (LMAX + 1)
    share = depth // (2 * columns)
    padded = -(-(share + 2) // 16) * 16
    partial = jax.ShapeDtypeStruct((columns, padded, depth), bf16)
    grad_conv, mine, theirs = pl.pallas_call(
        backward_kernel,
        out_shape=(
            jax.ShapeDtypeStruct((REDUCED * channels, edge_rows), bf16),
            partial,
            partial,
        ),
        in_specs=[smem] + [VMEM] * 6 + [HBM] + [VMEM] * 3,
        out_specs=[HBM] + [VMEM] * 2,
        scratch_shapes=[
            wide,
            pltpu.VMEM(field, f32),
            pltpu.VMEM((REDUCED * channels, edge_rows), f32),
            pltpu.VMEM((depth + padded, depth), f32),
            pltpu.VMEM((REDUCED * channels, edge_rows), bf16),
            edge_field,
            two_copies,
        ],
        compiler_params=PARAMS,
    )(first, ids, stats, every, scalar, per_edge, rotation, grad_edge, attention, attention_t, z)

    theirs = lax.ppermute(theirs, "core", [(0, 1), (1, 0)])
    mine = (mine.astype(f32) + theirs.astype(f32)).astype(bf16)
    mine, messages = lax.optimization_barrier((mine, messages))
    zero_parts = exchange(mine, COLUMN_GROUP)
    message_sums = pl.pallas_call(
        message_kernel,
        out_shape=jax.ShapeDtypeStruct((group, span, channels), bf16),
        in_specs=[VMEM] * 4,
        out_specs=VMEM,
        compiler_params=PARAMS,
    )(ids, stats, every, messages)
    message_sums, grad_conv = lax.optimization_barrier((message_sums, grad_conv))
    message_sums = message_sums.reshape(group // 2, 2 * span, channels)
    near_sums = lax.psum_scatter(message_sums, "y", scatter_dimension=0, tiled=True)
    near_sums = near_sums.reshape(2, span, channels)
    side = lax.axis_index("xl")
    kept = lax.dynamic_index_in_dim(near_sums, side, keepdims=False)
    passed = lax.dynamic_index_in_dim(near_sums, 1 - side, keepdims=False)
    passed = lax.ppermute(passed, "xl", [(0, 1), (1, 0)])
    summed = kept.astype(f32) + passed.astype(f32)
    used = harmonics * row_count
    inner = depth // group
    lanes = whole_lanes(inner)
    beside = lanes - inner >= channels // 2 and lanes == channels and share >= 2 * head_count
    tail_rows = share if beside else share * lanes // LANES + head_count
    grad_sums = pl.pallas_call(
        functools.partial(scatter_kernel, places, group, row_count),
        out_shape=jax.ShapeDtypeStruct(
            (group, -(-(used + tail_rows) // 16) * 16, channels), bf16
        ),
        in_specs=[smem] + [VMEM] * 3 + [HBM] * 2,
        out_specs=HBM,
        scratch_shapes=[
            held,
            wide,
            pltpu.VMEM((REDUCED,) + field, f32),
            pltpu.VMEM((COEF,) + field, bf16),
            pltpu.VMEM((REDUCED * channels, edge_rows), f32),
            pltpu.VMEM((edge_rows, REDUCED * channels), bf16),
            pltpu.VMEM((group, span, channels), bf16),
            copies,
            out_copy,
        ],
        compiler_params=PARAMS,
    )(first, ids, grad_conv, rotation, half, other)
    nodes_shape = jax.ShapeDtypeStruct((harmonics, row_count, channels), bf16)
    batch_scale = 1.0 / (2 * columns)
    if beside:
        window = -(-(used % 16 + share) // 16) * 16
        grad_sums = pl.pallas_call(
            functools.partial(tail_kernel, used, share, head_count),
            out_shape=jax.ShapeDtypeStruct(grad_sums.shape, bf16),
            in_specs=[VMEM, HBM],
            out_specs=HBM,
            input_output_aliases={1: 0},
            scratch_shapes=[
                pltpu.VMEM((padded, depth), f32),
                pltpu.VMEM((head_count, channels), f32),
                pltpu.VMEM((group, window, channels), bf16),
                two_copies,
            ],
            compiler_params=PARAMS,
        )(zero_parts, grad_sums)
        last = exchange(grad_sums, GRAPH)
        grad_nodes, grad_zero, grad_att = pl.pallas_call(
            functools.partial(last_kernel, batch_scale),
            out_shape=(
                nodes_shape,
                jax.ShapeDtypeStruct((share, inner), f32),
                jax.ShapeDtypeStruct((head_count, channels), f32),
            ),
            in_specs=[VMEM],
            out_specs=[VMEM] * 3,
            scratch_shapes=[pltpu.VMEM(last.shape[1:], f32)],
            compiler_params=PARAMS,
        )(last)
        grad_zero, grad_att = grad_zero.T, grad_att.T
    else:
        zero_sum = jnp.sum(zero_parts.astype(f32), axis=0)
        att = zero_sum[share : share + 2].reshape(-1)[: head_count * channels]
        zero_send = jnp.transpose(zero_sum[:share].reshape(share, group, inner), (1, 0, 2))
        zero_send = jnp.pad(zero_send, ((0, 0), (0, 0), (0, lanes - inner)))
        zero_send = zero_send.reshape(group, share * lanes // LANES, LANES)
        att = jnp.broadcast_to(
            att.reshape(1, head_count, channels), (group, head_count, channels)
        )
        last_rows = jnp.concatenate([zero_send, att], axis=1).astype(bf16)
        grad_sums = lax.dynamic_update_slice(grad_sums, last_rows, (0, used, 0))
        last = exchange(grad_sums, GRAPH)
        grad_nodes, tail = pl.pallas_call(
            sum_kernel,
            out_shape=(nodes_shape, jax.ShapeDtypeStruct((tail_rows, channels), f32)),
            in_specs=[VMEM],
            out_specs=[VMEM] * 2,
            scratch_shapes=[pltpu.VMEM(last.shape[1:], f32)],
            compiler_params=PARAMS,
        )(last)
        tail = tail * batch_scale
        zero_rows = share * lanes // LANES
        grad_zero = tail[:zero_rows].reshape(share, lanes)[:, :inner].T
        grad_att = tail[zero_rows:].T
    update = summed[:used].reshape(harmonics, row_count, channels)
    update = jnp.transpose(jnp.where(present[None], update, 0.0).astype(bf16), (1, 0, 2))
    grad_nodes = jnp.transpose(grad_nodes, (1, 0, 2))

    shape = (1, row_count, harmonics, channels)
    return (update.reshape(shape), grad_nodes.reshape(shape), grad_zero, grad_att)


def solution(mesh):
    columns, group = mesh.shape["dp"], mesh.shape["graph"]
    devices = mesh.devices.reshape(2, columns // 4, 2, group // 2, 2)
    fine = Mesh(devices, DP + GRAPH)
    in_specs = (
        P(DP, GRAPH, None, None),
        P(DP),
        P(DP, GRAPH),
        P(DP, GRAPH),
        P(DP, GRAPH),
        P(DP, None, None, GRAPH),
        P(DP, GRAPH, None, None),
        P(GRAPH, DP),
        P(GRAPH, DP),
        P(GRAPH, DP),
        P(GRAPH, DP),
        P(GRAPH, DP),
        P(),
    )
    out_specs = (P(DP, GRAPH, None, None), P(DP, GRAPH, None, None), P(GRAPH, DP), P())
    return jax.shard_map(
        on_device, mesh=fine, in_specs=in_specs, out_specs=out_specs, check_vma=False
    )
```

```python
import functools

import jax
import jax.numpy as jnp
from jax import lax
from jax.experimental import pallas as pl
from jax.experimental.pallas import tpu as pltpu
from jax.sharding import Mesh, PartitionSpec as P

LMAX = 6
LANES = 128
DP = ("xh", "z", "core")
COLUMN_GROUP = ("xh", "z")
ROW_GROUP = ("xh", "y", "xl")
GRAPH = ("y", "xl")
precise = lax.Precision.HIGHEST
f32 = jnp.float32
bf16 = jnp.bfloat16


def half_dot(left, right):
    return jnp.dot(left, right, preferred_element_type=f32)


def full_dot(left, right):
    return jnp.dot(left, right, precision=precise, preferred_element_type=f32)


def gather(block, axes):
    count = lax.axis_size(axes)
    copies = jnp.broadcast_to(block[None], (count,) + block.shape)
    return lax.all_to_all(copies, axes, split_axis=0, concat_axis=0, tiled=True)


def exchange(blocks, axes):
    return lax.all_to_all(blocks, axes, split_axis=0, concat_axis=0, tiled=True)


ROW_DEGREE = (
    list(range(LMAX + 1)) + list(range(1, LMAX + 1)) * 2 + list(range(2, LMAX + 1)) * 2
)
ROWS_OF = [[k for k, d in enumerate(ROW_DEGREE) if d == l] for l in range(LMAX + 1)]
COEFS_OF = [list(range(l * l, (l + 1) * (l + 1))) for l in range(LMAX + 1)]
REDUCED = len(ROW_DEGREE)
COEF = (LMAX + 1) ** 2
ZERO = (0, LMAX + 1)
ONE = (LMAX + 1, LMAX)
TWO = (3 * LMAX + 1, LMAX - 1)
CHUNK = 32
VMEM = pl.BlockSpec(memory_space=pltpu.VMEM)
HBM = pl.BlockSpec(memory_space=pltpu.HBM)
SMALL = pltpu.CompilerParams(vmem_limit_bytes=28 * 1024 * 1024)
LARGE = pltpu.CompilerParams(vmem_limit_bytes=48 * 1024 * 1024)
WHOLE = pltpu.CompilerParams(vmem_limit_bytes=60 * 1024 * 1024)
EDGE_PART = (0, COEF)
MESSAGE_PART = (COEF, COEF)
CONV_PART = (2 * COEF, REDUCED)
ZERO_PART = (2 * COEF + REDUCED, LMAX + 1)
SPILL = 1200


def nt_dot(left, right):
    return lax.dot_general(left, right, (((1,), (1,)), ((), ())), preferred_element_type=f32)


def nt_full(left, right):
    return lax.dot_general(
        left, right, (((1,), (1,)), ((), ())), precision=precise, preferred_element_type=f32
    )


def hot_rows(ids, count):
    rows = lax.broadcasted_iota(jnp.int32, (count, ids.shape[1]), 0)
    return (rows == ids).astype(f32)


def widen(values, channels):
    heads, edges = values.shape
    wide = jnp.broadcast_to(values[:, None, :], (heads, channels // heads, edges))
    return wide.reshape(channels, edges)


def part_of(spill, part):
    return spill.at[pl.ds(part[0], part[1])]


def chunks(channels, body):
    def step(i, carry):
        body(pl.multiple_of(i * CHUNK, CHUNK))
        return carry

    lax.fori_loop(0, channels // CHUNK, step, 0)


def rows_at(k, start):
    return pl.ds(pl.multiple_of(k * LANES + start, CHUNK), CHUNK)


def start_weights(places, first, mine, other, held, sems):
    def go(halves):
        for i, (half, at, rows, tiles) in enumerate(places):
            span = pl.ds(at, tiles * rows)
            pltpu.make_async_copy(
                halves[half].at[:, span, :], held.at[half, :, span, :], sems.at[i]
            ).start()

    @pl.when(first == 0)
    def _():
        go((mine, other))

    @pl.when(first != 0)
    def _():
        go((other, mine))


def wait_weights(places, which, mine, held, sems):
    for i in which:
        half, at, rows, tiles = places[i]
        span = pl.ds(at, tiles * rows)
        pltpu.make_async_copy(mine.at[:, span, :], held.at[half, :, span, :], sems.at[i]).wait()


def map_tiles(held, place, tiles):
    half, at, rows, _ = place
    parts = []
    for t in tiles:
        part = held[half, :, at + t * rows : at + (t + 1) * rows, :]
        parts.append(part.reshape(-1, LANES))
    return parts[0] if len(parts) == 1 else jnp.concatenate(parts, axis=1)


def pairs(count):
    return [tuple(range(i, min(i + 2, count))) for i in range(0, count, 2)]


def spread(blocks, held, rows, base, out):
    zs = held.shape[1]
    size = rows // 2
    for z in range(zs):
        for xh in range(2):
            to = base + (xh * zs + z) * size
            at = (z * 2 + xh) * size
            out[to : to + size, :] = blocks[at : at + size, :]


def by_owner(target, turned, out, group, scale=None):
    channels = turned.shape[1]
    own = target.shape[0] // group
    per = 16 // own
    for first in range(0, COEF, per):
        parts = []
        for j in range(first, first + per):
            if j < COEF:
                part = nt_dot(target, turned[j])
                part = part if scale is None else part * scale
            else:
                part = jnp.zeros((target.shape[0], channels), f32)
            parts.append(part.reshape(group, 1, own, channels))
        block = jnp.concatenate(parts, axis=1).reshape(group, 16, channels)
        out[:, first * own : first * own + 16, :] = block.astype(bf16)


def pack_kernel(places, *refs):
    count = len(places)
    shards, out = refs[:count], refs[count]
    held, acc, sems = refs[count + 1 : -2], refs[-2], refs[-1]
    copies = [pltpu.make_async_copy(shards[i], held[i], sems.at[i]) for i in range(count)]
    for copy in copies:
        copy.start()
    acc[...] = jnp.zeros_like(acc)
    for copy, shard, at in zip(copies, held, places):
        columns, rows = shard.shape
        lane = lax.broadcasted_iota(jnp.int32, (rows, acc.shape[1]), 1)
        row = lax.broadcasted_iota(jnp.int32, (rows, acc.shape[1]), 0)
        place = (lane == row + at).astype(bf16)
        copy.wait()
        acc[:columns, :] += half_dot(shard[...], place)
    out[...] = acc[...].astype(bf16)


def slab_kernel(sets, first, slabs, out):
    group, most, lanes = slabs.shape[0] // 2, slabs.shape[1] // 2, slabs.shape[2]
    blocks = [jnp.concatenate([slabs[g], slabs[group + g]], axis=0) for g in range(group)]

    def lay(which):
        to = 0
        for rows, columns, at in which:
            size = 4 * columns
            row = lax.broadcasted_iota(jnp.int32, (size, 4 * most), 0)
            lane = lax.broadcasted_iota(jnp.int32, (size, 4 * most), 1)
            kept = row // columns * most + row % columns
            chosen = (lane == kept).astype(bf16)
            source = lax.broadcasted_iota(jnp.int32, (lanes, LANES), 0)
            place = lax.broadcasted_iota(jnp.int32, (lanes, LANES), 1)
            for t in range(group * rows // LANES):
                acc = None
                for g in range(group):
                    if g * rows >= (t + 1) * LANES or (g + 1) * rows <= t * LANES:
                        continue
                    shift = g * rows - t * LANES - at
                    hit = (place == source + shift) & (source >= at) & (source < at + rows)
                    term = half_dot(blocks[g], hit.astype(bf16))
                    acc = term if acc is None else acc + term
                tile = half_dot(chosen, acc.astype(bf16))
                out[to : to + size, :] = tile.astype(bf16)
                to += size
        if to < out.shape[0]:
            out[to:, :] = jnp.zeros((out.shape[0] - to, LANES), bf16)

    @pl.when(first[0, 0] == 0)
    def _():
        lay(sets[0])

    @pl.when(first[0, 0] != 0)
    def _():
        lay(sets[1])


def message_kernel(ids, stats, every, spill, out, msg, sem):
    copy = pltpu.make_async_copy(part_of(spill, MESSAGE_PART), msg, sem.at[0])
    copy.start()
    group = out.shape[0]
    count = stats.shape[1] // 2
    total = jnp.sum(every[:, :, :count], axis=0)
    share = stats[:, :count] / jnp.where(total > 0.0, total, 1.0)
    scale = widen(share, LANES).T
    copy.wait()
    by_owner(hot_rows(ids[1:2, :], count).astype(bf16), msg, out, group, scale)


def rotate_kernel(own, ids, nodes, wigner, z, spill, paired, wide, grad_edge, out_sem):
    group, edges = nodes.shape[0], wigner.shape[2]
    channels = LANES
    per = 16 // (2 * own)
    count = own * group
    target = hot_rows(ids[1:2, :], count)
    both = (target + hot_rows(ids[0:1, :], count)).astype(bf16)
    target = target.astype(bf16)
    wide[...] = wigner[...].astype(f32)
    for first in range(0, COEF, per):
        rows = nodes[:, first * 2 * own : first * 2 * own + 16, :].astype(f32)
        rows = rows.reshape(group, 2 * per, own, channels)
        for j in range(first, min(first + per, COEF)):
            at = 2 * (j - first)
            here = rows[:, at].reshape(count, channels).T.astype(bf16)
            paired[j] = half_dot(here, both).astype(bf16).astype(f32)
            here = rows[:, at + 1].reshape(count, channels).T.astype(bf16)
            grad_edge[j] = half_dot(here, target).astype(bf16)
    copy = pltpu.make_async_copy(grad_edge, part_of(spill, EDGE_PART), out_sem.at[0])
    copy.start()
    for l in range(LMAX + 1):
        for k in ROWS_OF[l]:
            acc = None
            for j in COEFS_OF[l]:
                term = wide[j, k : k + 1, :] * paired[j]
                acc = term if acc is None else acc + term
            z[k] = acc.astype(bf16)
    zero_copy = pltpu.make_async_copy(
        z.at[pl.ds(0, LMAX + 1)], part_of(spill, ZERO_PART), out_sem.at[1]
    )
    zero_copy.start()
    copy.wait()
    zero_copy.wait()


def forward_kernel(
    places,
    group,
    first,
    ids,
    z,
    wigner,
    spill_in,
    attention_t,
    mine,
    other,
    spill,
    stats,
    sent,
    scalar,
    per_edge,
    held,
    y,
    wide,
    norm,
    msg,
    heads_acc,
    grad_edge,
    sems,
    out_sem,
):
    channels, edges = LANES, wigner.shape[2]
    heads = attention_t.shape[0]
    count = stats.shape[1] // 2
    start_weights(places, first[0, 0], mine, other, held, sems)
    edge_copy = pltpu.make_async_copy(part_of(spill_in, EDGE_PART), grad_edge, out_sem.at[1])
    edge_copy.start()
    wide[...] = wigner[...].astype(f32)
    base, rows = ZERO
    acc = None
    wait_weights(places, (0,), mine, held, sems)
    for tiles in pairs(rows):
        right = z[tiles[0] : tiles[-1] + 1].reshape(-1, edges)
        term = half_dot(map_tiles(held, places[0], tiles), right)
        acc = term if acc is None else acc + term
    spread(acc, held, places[0][2], base, y)
    for (base, rows), real, imag in ((ONE, places[1], places[2]), (TWO, places[3], places[4])):
        wait_weights(places, (1, 2) if base == ONE[0] else (3, 4), mine, held, sems)
        acc = None
        for tiles in pairs(rows):
            lo, hi = base + tiles[0], base + tiles[-1] + 1
            plus = z[lo:hi].reshape(-1, edges)
            minus = z[lo + rows : hi + rows].reshape(-1, edges)
            term = half_dot(map_tiles(held, real, tiles), jnp.concatenate([plus, minus], axis=1))
            term = term + half_dot(
                map_tiles(held, imag, tiles), jnp.concatenate([-minus, plus], axis=1)
            )
            acc = term if acc is None else acc + term
        spread(acc[:, :edges], held, real[2], base * channels, y)
        spread(acc[:, edges:], held, real[2], (base + rows) * channels, y)
    value = y[:channels, :]
    scalar[...] = value
    y[...] = y[...].astype(bf16).astype(f32)
    gating = (value / (1.0 + jnp.exp(-value))).astype(bf16)
    logits = half_dot(attention_t[...], gating)
    weight = jnp.where(ids[2:3, :] > 0, jnp.exp(logits), 0.0)
    target = hot_rows(ids[1:2, :], count)
    own_sum = nt_full(weight, target)
    at_edges = full_dot(own_sum, target)
    own_norm = weight / jnp.where(at_edges > 0.0, at_edges, 1.0)
    norm[...] = widen(own_norm, channels)

    def body(start):
        at = pl.ds(start, CHUNK)
        own = norm[at, :]
        total = jnp.zeros((CHUNK, edges), f32)
        for l in range(LMAX + 1):
            for j in COEFS_OF[l]:
                acc = None
                for k in ROWS_OF[l]:
                    term = wide[j, k : k + 1, :] * y[rows_at(k, start), :]
                    acc = term if acc is None else acc + term
                total = total + acc * grad_edge[j, at, :].astype(f32)
                msg[j, at, :] = (acc * own).astype(bf16)
        heads_acc[at, :] = total

    edge_copy.wait()
    chunks(channels, body)
    copy = pltpu.make_async_copy(msg, part_of(spill, MESSAGE_PART), out_sem.at[0])
    copy.start()
    grad_norm = jnp.sum(heads_acc[...].reshape(heads, channels // heads, edges), axis=1)
    own_shared = nt_full(own_norm * grad_norm, target)
    sums = jnp.concatenate([own_sum, own_shared], axis=1)
    stats[...] = sums
    for owner in range(group):
        sent[owner] = sums
    per_edge[:heads, :] = own_norm
    per_edge[heads:, :] = grad_norm
    copy.wait()


def backward_kernel(
    first,
    ids,
    stats,
    every,
    scalar,
    per_edge,
    wigner,
    spill_in,
    attention,
    attention_t,
    spill,
    mine,
    theirs,
    wide,
    norm,
    grad,
    turned,
    grad_conv,
    grad_edge,
    z,
    out_sem,
):
    channels, edges = LANES, wigner.shape[2]
    heads = attention_t.shape[0]
    count = stats.shape[1] // 2
    edge_copy = pltpu.make_async_copy(part_of(spill_in, EDGE_PART), grad_edge, out_sem.at[1])
    edge_copy.start()
    zero_copy = pltpu.make_async_copy(part_of(spill_in, ZERO_PART), z, out_sem.at[2])
    zero_copy.start()
    wide[...] = wigner[...].astype(f32)
    total = jnp.sum(every[:, :, :count], axis=0)
    total = jnp.where(total > 0.0, total, 1.0)
    shares = every[:, :, :count] / total[None]
    shared = jnp.sum(shares * every[:, :, count:], axis=0)
    own_share = stats[:, :count] / total
    target = hot_rows(ids[1:2, :], count)
    normalized = per_edge[:heads, :] * full_dot(own_share, target)
    grad_logit = normalized * (per_edge[heads:, :] - full_dot(shared, target))
    value = scalar[...]
    sigmoid = 1.0 / (1.0 + jnp.exp(-value))
    gating = (value / (1.0 + jnp.exp(-value))).astype(bf16).astype(f32)
    att = nt_full(grad_logit, gating)
    grad_gating = full_dot(attention[...].astype(f32), grad_logit)
    grad_scalar = grad_gating * sigmoid * (1.0 + value * (1.0 - sigmoid))
    norm[...] = widen(normalized, channels)

    def body(start):
        at = pl.ds(start, CHUNK)
        own = norm[at, :]
        for l in range(LMAX + 1):
            fields = [
                (grad_edge[j, at, :].astype(f32) * own).astype(bf16).astype(f32)
                for j in COEFS_OF[l]
            ]
            for k in ROWS_OF[l]:
                acc = None
                for j, field in zip(COEFS_OF[l], fields):
                    term = wide[j, k : k + 1, :] * field
                    acc = term if acc is None else acc + term
                grad[rows_at(k, start), :] = acc

    edge_copy.wait()
    chunks(channels, body)
    grad[:channels, :] = grad[:channels, :] + grad_scalar
    depth = (LMAX + 1) * channels
    parts, share = mine.shape[0], depth // (2 * mine.shape[0])
    grad_conv[...] = grad[...].astype(bf16).reshape(grad_conv.shape)
    copy = pltpu.make_async_copy(grad_conv, part_of(spill, CONV_PART), out_sem.at[0])
    copy.start()
    zero_copy.wait()
    turned[:depth, :] = nt_dot(
        grad_conv[: LMAX + 1].reshape(depth, edges), z[...].reshape(depth, edges)
    )
    turned[depth:, :] = jnp.zeros((turned.shape[0] - depth, depth), f32)
    padded = mine.shape[1]
    tail_row = lax.broadcasted_iota(jnp.int32, (padded, depth), 0)
    one = jnp.concatenate([att[h : h + 1, :] for h in range(LMAX + 1)], axis=1)
    two = [att[h : h + 1, :] for h in range(LMAX + 1, heads)]
    two = jnp.concatenate(two + [jnp.zeros((1, depth - len(two) * channels), f32)], axis=1)

    def store(outs):
        for core in range(2):
            for part in range(parts):
                at = (2 * part + core) * share
                block = turned[at : at + padded, :]
                block = jnp.where(tail_row == share, one, block)
                block = jnp.where(tail_row == share + 1, two, block)
                outs[core][part] = block.astype(bf16)

    @pl.when(first[0, 0] == 0)
    def _():
        store((mine, theirs))

    @pl.when(first[0, 0] != 0)
    def _():
        store((theirs, mine))

    copy.wait()


def scatter_kernel(
    places,
    group,
    own,
    first,
    ids,
    spill,
    wigner,
    mine,
    other,
    grads_out,
    held,
    wide,
    dz,
    gp,
    grad,
    grad_rows,
    grads,
    grad_conv,
    sems,
    out_sem,
):
    channels, edges = LANES, wigner.shape[2]
    count = own * group
    conv_copy = pltpu.make_async_copy(part_of(spill, CONV_PART), grad_conv, out_sem.at[1])
    conv_copy.start()
    start_weights(places, first[0, 0], mine, other, held, sems)
    wide[...] = wigner[...].astype(f32)
    conv_copy.wait()
    grad[...] = grad_conv[...].astype(f32).reshape(grad.shape)
    zs = held.shape[1]
    for base, rows in (ZERO, ONE, (ONE[0] + ONE[1], ONE[1]), TWO, (TWO[0] + TWO[1], TWO[1])):
        size = rows * channels // (2 * zs)
        blocks = []
        for zz in range(zs):
            for xh in range(2):
                at = base * channels + (xh * zs + zz) * size
                blocks.append(grad[at : at + size, :])
        ordered = jnp.concatenate(blocks, axis=0)
        for t in range(rows):
            at = slice(t * channels, (t + 1) * channels)
            to = (base + t) * channels
            grad_rows[:, to : to + channels] = ordered[at, :].T.astype(bf16)
    base, rows = ZERO
    left = grad_rows[:, : rows * channels]
    wait_weights(places, (0,), mine, held, sems)
    for tiles in pairs(rows):
        out = half_dot(left, map_tiles(held, places[0], tiles)).astype(bf16).astype(f32)
        for i, t in enumerate(tiles):
            dz[t] = out[:, i * channels : (i + 1) * channels].T
    for (base, rows), real, imag in ((ONE, places[1], places[2]), (TWO, places[3], places[4])):
        wait_weights(places, (1, 2) if base == ONE[0] else (3, 4), mine, held, sems)
        plus = grad_rows[:, base * channels : (base + rows) * channels]
        minus = grad_rows[:, (base + rows) * channels : (base + 2 * rows) * channels]
        left = jnp.concatenate([plus, minus], axis=0)
        crossed = jnp.concatenate([minus, -plus], axis=0)
        for tiles in pairs(rows):
            out = half_dot(left, map_tiles(held, real, tiles))
            out = out + half_dot(crossed, map_tiles(held, imag, tiles))
            out = out.astype(bf16).astype(f32)
            for i, t in enumerate(tiles):
                at = slice(i * channels, (i + 1) * channels)
                dz[base + t] = out[:edges, at].T
                dz[base + rows + t] = out[edges:, at].T

    def body(start):
        at = pl.ds(start, CHUNK)
        for l in range(LMAX + 1):
            for j in COEFS_OF[l]:
                acc = None
                for k in ROWS_OF[l]:
                    term = wide[j, k : k + 1, :] * dz[k, at, :]
                    acc = term if acc is None else acc + term
                gp[j, at, :] = acc.astype(bf16)

    chunks(channels, body)
    both = (hot_rows(ids[1:2, :], count) + hot_rows(ids[0:1, :], count)).astype(bf16)
    by_owner(both, gp, grads, group)
    whole = pl.ds(0, grads.shape[1])
    copy = pltpu.make_async_copy(grads, grads_out.at[:, whole, :], out_sem.at[0])
    copy.start()
    copy.wait()


def node_rows(own):
    return -(-COEF * own // 16) * 16


def one_hot(rows, columns, shift, low, high):
    row = lax.broadcasted_iota(jnp.int32, (rows, columns), 0)
    column = lax.broadcasted_iota(jnp.int32, (rows, columns), 1)
    return ((column == row + shift) & (row >= low) & (row < high)).astype(bf16)


def tail_kernel(used, share, heads, parts, grads_in, grads, total, att, window, sems):
    count, depth = parts.shape[0], parts.shape[2]
    group, rows = window.shape[0], window.shape[1]
    inner, skip = depth // group, used % 16
    base = used - skip
    old = pltpu.make_async_copy(
        grads_in.at[:, pl.ds(base, 16), :], window.at[:, pl.ds(0, 16), :], sems.at[0]
    )
    old.start()
    acc = parts[0].astype(f32)
    for p in range(1, count):
        acc = acc + parts[p].astype(f32)
    total[...] = acc
    for h in range(heads):
        row, at = share + h // (depth // LANES), h % (depth // LANES) * LANES
        att[h : h + 1, :] = total[row : row + 1, at : at + LANES]
    low = att[...].astype(bf16)
    half = LANES // 2
    left = half_dot(low, one_hot(LANES, LANES, half, 0, half)).astype(bf16)
    right = half_dot(low, one_hot(LANES, LANES, 0, half, LANES)).astype(bf16)
    row = lax.broadcasted_iota(jnp.int32, (rows, heads), 0)
    head = lax.broadcasted_iota(jnp.int32, (rows, heads), 1)
    tail = half_dot((row == head + skip).astype(bf16), left)
    tail = tail + half_dot((row == head + skip + heads).astype(bf16), right)
    moved = half_dot(one_hot(rows, total.shape[0], -skip, skip, skip + share), acc.astype(bf16))
    moved = moved.astype(bf16)
    kept = lax.broadcasted_iota(jnp.int32, (rows, LANES), 0) < skip
    old.wait()
    for g in range(group):
        first = g * inner // LANES * LANES
        last = -(-(g + 1) * inner // LANES) * LANES
        shift = g * inner - first
        place = one_hot(last - first, LANES, -shift, shift, shift + inner)
        piece = half_dot(moved[:, first:last], place) + tail
        before = window[g, :16, :].astype(f32)
        if rows > 16:
            before = jnp.concatenate([before, jnp.zeros((rows - 16, LANES), f32)], axis=0)
        window[g] = jnp.where(kept, before, piece).astype(bf16)
    new = pltpu.make_async_copy(window, grads.at[:, pl.ds(base, rows), :], sems.at[1])
    new.start()
    new.wait()


def last_kernel(scale, parts, nodes, zero, att, total):
    acc = parts[0].astype(f32)
    for g in range(1, parts.shape[0]):
        acc = acc + parts[g].astype(f32)
    total[...] = acc
    used = nodes.shape[0] * nodes.shape[1]
    heads, half = att.shape[0], LANES // 2
    nodes[...] = acc[:used].astype(bf16).reshape(nodes.shape)
    zero[...] = total[used : used + zero.shape[0], :][:, : zero.shape[1]] * scale
    left = full_dot(
        total[used : used + heads, :], one_hot(LANES, LANES, -half, half, LANES).astype(f32)
    )
    lane = lax.broadcasted_iota(jnp.int32, (heads, LANES), 1)
    right = jnp.where(lane >= half, total[used + heads : used + 2 * heads, :], 0.0)
    att[...] = (left + right) * scale


def sum_kernel(parts, nodes, tail, total):
    acc = parts[0].astype(f32)
    for g in range(1, parts.shape[0]):
        acc = acc + parts[g].astype(f32)
    total[...] = acc
    used = nodes.shape[0] * nodes.shape[1]
    nodes[...] = acc[:used].astype(bf16).reshape(nodes.shape)
    tail[...] = total[used : used + tail.shape[0], :]


def pad_to(block, rows, columns):
    return jnp.pad(block, ((0, rows - block.shape[0]), (0, columns - block.shape[1])))


def whole_lanes(count):
    return -(-count // LANES) * LANES


def gather_weights(shards):
    rows = [w.shape[0] for w in shards]
    columns = [w.shape[1] for w in shards]
    most = -(-max(columns) // 16) * 16
    sets = ((0, 1), (2, 3, 4))
    lanes = whole_lanes(max(sum(rows[i] for i in s) for s in sets))
    starts = [0] * len(shards)
    for half_index, s in enumerate(sets):
        for n, i in enumerate(s):
            starts[i] = half_index * lanes + sum(rows[j] for j in s[:n])
    packed = pl.pallas_call(
        functools.partial(pack_kernel, starts),
        out_shape=jax.ShapeDtypeStruct((most, 2 * lanes), bf16),
        in_specs=[HBM] * len(shards),
        out_specs=VMEM,
        scratch_shapes=[pltpu.VMEM(w.shape[::-1], bf16) for w in shards]
        + [pltpu.VMEM((most, 2 * lanes), f32), pltpu.SemaphoreType.DMA((len(shards),))],
        compiler_params=WHOLE,
    )(*[w.T for w in shards])
    core = lax.axis_index("core")
    near = lax.all_gather(packed, "core")
    sent = lax.dynamic_slice_in_dim(near, core * lanes, lanes, axis=2)
    slabs = gather(sent.reshape(2 * most, lanes), ROW_GROUP)
    group = slabs.shape[0] // 2
    places = [None] * len(shards)
    depth = 0
    for half_index, s in enumerate(sets):
        at = 0
        for i in s:
            tiles = group * rows[i] // LANES
            places[i] = (half_index, at, 4 * columns[i], tiles)
            at += tiles * 4 * columns[i]
        depth = max(depth, at)
    kinds = [[(rows[i], columns[i], starts[i] - n * lanes) for i in s] for n, s in enumerate(sets)]
    tiled = pl.pallas_call(
        functools.partial(slab_kernel, kinds),
        out_shape=jax.ShapeDtypeStruct((depth, LANES), bf16),
        in_specs=[pl.BlockSpec(memory_space=pltpu.SMEM), VMEM],
        out_specs=VMEM,
        compiler_params=SMALL,
    )(core.astype(jnp.int32).reshape(1, 1), slabs)
    return lax.all_gather(tiled, "z"), places, tiled


def on_device(
    embeddings,
    atom_counts,
    edge_counts,
    source,
    target,
    wigner,
    cotangent,
    w_zero,
    w_one_real,
    w_one_imag,
    w_two_real,
    w_two_imag,
    attention,
):
    half, places, tiled = gather_weights((w_zero, w_one_real, w_one_imag, w_two_real, w_two_imag))
    row_count = embeddings.shape[1]
    harmonics = embeddings.shape[2]
    channels = embeddings.shape[3]
    width = harmonics * channels
    edge_rows = source.shape[1]
    head_count = attention.shape[1]
    group = lax.axis_size(GRAPH)
    all_nodes = row_count * group
    rotation = jnp.transpose(wigner[0], (1, 0, 2))
    in_use = (lax.iota(jnp.int32, edge_rows) < edge_counts[0, 0]).astype(jnp.int32)
    ids = jnp.stack([source[0], target[0], in_use] + [jnp.zeros_like(in_use)] * 5)
    attention_t = attention.T
    core = lax.axis_index("core")
    first = core.astype(jnp.int32).reshape(1, 1)
    own_first = lax.axis_index(GRAPH) * row_count
    present = ((own_first + lax.iota(jnp.int32, row_count)) < atom_counts[0])[:, None]
    cot_rows = jnp.where(present[:, :, None], cotangent[0], 0.0).astype(bf16)
    own_rows = jnp.stack([embeddings[0], cot_rows])
    own_rows = jnp.transpose(own_rows, (2, 0, 1, 3)).reshape(-1, channels)
    own_rows = pad_to(own_rows, -(-own_rows.shape[0] // 16) * 16, channels)
    own_rows, tiled = lax.optimization_barrier((own_rows, tiled))
    nodes = gather(own_rows, GRAPH)
    half, nodes = lax.optimization_barrier((half, nodes))
    other = lax.ppermute(half, "core", [(0, 1), (1, 0)])

    smem = pl.BlockSpec(memory_space=pltpu.SMEM)
    field = (channels, edge_rows)
    wide = pltpu.VMEM(rotation.shape, f32)
    spill_shape = jax.ShapeDtypeStruct((SPILL,) + field, bf16)
    out_copy = pltpu.SemaphoreType.DMA((1,))
    two_copies = pltpu.SemaphoreType.DMA((2,))
    edge_field = pltpu.VMEM((COEF,) + field, bf16)
    z, spill = pl.pallas_call(
        functools.partial(rotate_kernel, row_count),
        out_shape=(
            jax.ShapeDtypeStruct((REDUCED,) + field, bf16),
            spill_shape,
        ),
        in_specs=[VMEM] * 3,
        out_specs=[VMEM, HBM],
        scratch_shapes=[
            pltpu.VMEM((COEF,) + field, f32),
            wide,
            edge_field,
            two_copies,
        ],
        compiler_params=LARGE,
    )(ids, nodes, rotation)
    held = pltpu.VMEM((2,) + half.shape, bf16)
    copies = pltpu.SemaphoreType.DMA((len(places),))

    span = node_rows(row_count)
    sums = (head_count, 2 * all_nodes)
    spill, stats, sent, scalar, per_edge = pl.pallas_call(
        functools.partial(forward_kernel, places, group),
        out_shape=(
            spill_shape,
            jax.ShapeDtypeStruct(sums, f32),
            jax.ShapeDtypeStruct((group,) + sums, f32),
            jax.ShapeDtypeStruct(field, f32),
            jax.ShapeDtypeStruct((2 * head_count, edge_rows), f32),
        ),
        in_specs=[smem] + [VMEM] * 3 + [HBM, VMEM] + [HBM] * 2,
        out_specs=[HBM] + [VMEM] * 4,
        scratch_shapes=[
            held,
            pltpu.VMEM((REDUCED * channels, edge_rows), f32),
            wide,
            pltpu.VMEM(field, f32),
            pltpu.VMEM((COEF,) + field, bf16),
            pltpu.VMEM(field, f32),
            edge_field,
            copies,
            two_copies,
        ],
        input_output_aliases={4: 0},
        compiler_params=LARGE,
    )(first, ids, z, rotation, spill, attention_t, half, other)
    every = exchange(sent, GRAPH)

    columns = lax.axis_size(COLUMN_GROUP)
    depth = channels * (LMAX + 1)
    share = depth // (2 * columns)
    padded = -(-(share + 2) // 16) * 16
    partial = jax.ShapeDtypeStruct((columns, padded, depth), bf16)
    spill, mine, theirs = pl.pallas_call(
        backward_kernel,
        out_shape=(
            spill_shape,
            partial,
            partial,
        ),
        in_specs=[smem] + [VMEM] * 6 + [HBM] + [VMEM] * 2,
        out_specs=[HBM] + [VMEM] * 2,
        scratch_shapes=[
            wide,
            pltpu.VMEM(field, f32),
            pltpu.VMEM((REDUCED * channels, edge_rows), f32),
            pltpu.VMEM((depth + padded, depth), f32),
            pltpu.VMEM((REDUCED,) + field, bf16),
            edge_field,
            pltpu.VMEM((LMAX + 1,) + field, bf16),
            pltpu.SemaphoreType.DMA((3,)),
        ],
        input_output_aliases={7: 0},
        compiler_params=LARGE,
    )(first, ids, stats, every, scalar, per_edge, rotation, spill, attention, attention_t)

    theirs = lax.ppermute(theirs, "core", [(0, 1), (1, 0)])
    mine = (mine.astype(f32) + theirs.astype(f32)).astype(bf16)
    mine, spill = lax.optimization_barrier((mine, spill))
    zero_parts = exchange(mine, COLUMN_GROUP)
    message_sums = pl.pallas_call(
        message_kernel,
        out_shape=jax.ShapeDtypeStruct((group, span, channels), bf16),
        in_specs=[VMEM] * 3 + [HBM],
        out_specs=VMEM,
        scratch_shapes=[edge_field, out_copy],
        compiler_params=LARGE,
    )(ids, stats, every, spill)
    message_sums, spill = lax.optimization_barrier((message_sums, spill))
    message_sums = message_sums.reshape(group // 2, 2 * span, channels)
    near_sums = lax.psum_scatter(message_sums, "y", scatter_dimension=0, tiled=True)
    near_sums = near_sums.reshape(2, span, channels)
    side = lax.axis_index("xl")
    kept = lax.dynamic_index_in_dim(near_sums, side, keepdims=False)
    passed = lax.dynamic_index_in_dim(near_sums, 1 - side, keepdims=False)
    passed = lax.ppermute(passed, "xl", [(0, 1), (1, 0)])
    summed = kept.astype(f32) + passed.astype(f32)
    used = harmonics * row_count
    inner = depth // group
    lanes = whole_lanes(inner)
    beside = lanes - inner >= channels // 2 and lanes == channels and share >= 2 * head_count
    tail_rows = share if beside else share * lanes // LANES + head_count
    grad_sums = pl.pallas_call(
        functools.partial(scatter_kernel, places, group, row_count),
        out_shape=jax.ShapeDtypeStruct(
            (group, -(-(used + tail_rows) // 16) * 16, channels), bf16
        ),
        in_specs=[smem, VMEM, HBM, VMEM] + [HBM] * 2,
        out_specs=HBM,
        scratch_shapes=[
            held,
            wide,
            pltpu.VMEM((REDUCED,) + field, f32),
            pltpu.VMEM((COEF,) + field, bf16),
            pltpu.VMEM((REDUCED * channels, edge_rows), f32),
            pltpu.VMEM((edge_rows, REDUCED * channels), bf16),
            pltpu.VMEM((group, span, channels), bf16),
            pltpu.VMEM((REDUCED,) + field, bf16),
            copies,
            two_copies,
        ],
        compiler_params=LARGE,
    )(first, ids, spill, rotation, half, other)
    nodes_shape = jax.ShapeDtypeStruct((harmonics, row_count, channels), bf16)
    batch_scale = 1.0 / (2 * columns)
    if beside:
        window = -(-(used % 16 + share) // 16) * 16
        grad_sums = pl.pallas_call(
            functools.partial(tail_kernel, used, share, head_count),
            out_shape=jax.ShapeDtypeStruct(grad_sums.shape, bf16),
            in_specs=[VMEM, HBM],
            out_specs=HBM,
            input_output_aliases={1: 0},
            scratch_shapes=[
                pltpu.VMEM((padded, depth), f32),
                pltpu.VMEM((head_count, channels), f32),
                pltpu.VMEM((group, window, channels), bf16),
                two_copies,
            ],
            compiler_params=SMALL,
        )(zero_parts, grad_sums)
        last = exchange(grad_sums, GRAPH)
        grad_nodes, grad_zero, grad_att = pl.pallas_call(
            functools.partial(last_kernel, batch_scale),
            out_shape=(
                nodes_shape,
                jax.ShapeDtypeStruct((share, inner), f32),
                jax.ShapeDtypeStruct((head_count, channels), f32),
            ),
            in_specs=[VMEM],
            out_specs=[VMEM] * 3,
            scratch_shapes=[pltpu.VMEM(last.shape[1:], f32)],
            compiler_params=SMALL,
        )(last)
        grad_zero, grad_att = grad_zero.T, grad_att.T
    else:
        zero_sum = jnp.sum(zero_parts.astype(f32), axis=0)
        att = zero_sum[share : share + 2].reshape(-1)[: head_count * channels]
        zero_send = jnp.transpose(zero_sum[:share].reshape(share, group, inner), (1, 0, 2))
        zero_send = jnp.pad(zero_send, ((0, 0), (0, 0), (0, lanes - inner)))
        zero_send = zero_send.reshape(group, share * lanes // LANES, LANES)
        att = jnp.broadcast_to(
            att.reshape(1, head_count, channels), (group, head_count, channels)
        )
        last_rows = jnp.concatenate([zero_send, att], axis=1).astype(bf16)
        grad_sums = lax.dynamic_update_slice(grad_sums, last_rows, (0, used, 0))
        last = exchange(grad_sums, GRAPH)
        grad_nodes, tail = pl.pallas_call(
            sum_kernel,
            out_shape=(nodes_shape, jax.ShapeDtypeStruct((tail_rows, channels), f32)),
            in_specs=[VMEM],
            out_specs=[VMEM] * 2,
            scratch_shapes=[pltpu.VMEM(last.shape[1:], f32)],
            compiler_params=SMALL,
        )(last)
        tail = tail * batch_scale
        zero_rows = share * lanes // LANES
        grad_zero = tail[:zero_rows].reshape(share, lanes)[:, :inner].T
        grad_att = tail[zero_rows:].T
    update = summed[:used].reshape(harmonics, row_count, channels)
    update = jnp.transpose(jnp.where(present[None], update, 0.0).astype(bf16), (1, 0, 2))
    grad_nodes = jnp.transpose(grad_nodes, (1, 0, 2))

    shape = (1, row_count, harmonics, channels)
    return (update.reshape(shape), grad_nodes.reshape(shape), grad_zero, grad_att)


def solution(mesh):
    columns, group = mesh.shape["dp"], mesh.shape["graph"]
    devices = mesh.devices.reshape(2, columns // 4, 2, group // 2, 2)
    fine = Mesh(devices, DP + GRAPH)
    in_specs = (
        P(DP, GRAPH, None, None),
        P(DP),
        P(DP, GRAPH),
        P(DP, GRAPH),
        P(DP, GRAPH),
        P(DP, None, None, GRAPH),
        P(DP, GRAPH, None, None),
        P(GRAPH, DP),
        P(GRAPH, DP),
        P(GRAPH, DP),
        P(GRAPH, DP),
        P(GRAPH, DP),
        P(),
    )
    out_specs = (P(DP, GRAPH, None, None), P(DP, GRAPH, None, None), P(GRAPH, DP), P())
    return jax.shard_map(
        on_device, mesh=fine, in_specs=in_specs, out_specs=out_specs, check_vma=False
    )
```

```python
import functools

import jax
import jax.numpy as jnp
from jax import lax
from jax.experimental import pallas as pl
from jax.experimental.pallas import tpu as pltpu
from jax.sharding import Mesh, PartitionSpec as P

LMAX = 6
LANES = 128
DP = ("xh", "z", "core")
COLUMN_GROUP = ("xh", "z")
ROW_GROUP = ("xh", "y", "xl")
GRAPH = ("y", "xl")
precise = lax.Precision.HIGHEST
f32 = jnp.float32
bf16 = jnp.bfloat16


def half_dot(left, right):
    return jnp.dot(left, right, preferred_element_type=f32)


def full_dot(left, right):
    return jnp.dot(left, right, precision=precise, preferred_element_type=f32)


def gather(block, axes):
    count = lax.axis_size(axes)
    copies = jnp.broadcast_to(block[None], (count,) + block.shape)
    return lax.all_to_all(copies, axes, split_axis=0, concat_axis=0, tiled=True)


def exchange(blocks, axes):
    return lax.all_to_all(blocks, axes, split_axis=0, concat_axis=0, tiled=True)


ROW_DEGREE = (
    list(range(LMAX + 1)) + list(range(1, LMAX + 1)) * 2 + list(range(2, LMAX + 1)) * 2
)
ROWS_OF = [[k for k, d in enumerate(ROW_DEGREE) if d == l] for l in range(LMAX + 1)]
COEFS_OF = [list(range(l * l, (l + 1) * (l + 1))) for l in range(LMAX + 1)]
REDUCED = len(ROW_DEGREE)
COEF = (LMAX + 1) ** 2
ZERO = (0, LMAX + 1)
ONE = (LMAX + 1, LMAX)
TWO = (3 * LMAX + 1, LMAX - 1)
CHUNK = 32
VMEM = pl.BlockSpec(memory_space=pltpu.VMEM)
HBM = pl.BlockSpec(memory_space=pltpu.HBM)
SMALL = pltpu.CompilerParams(vmem_limit_bytes=28 * 1024 * 1024)
LARGE = pltpu.CompilerParams(vmem_limit_bytes=48 * 1024 * 1024)
WHOLE = pltpu.CompilerParams(vmem_limit_bytes=60 * 1024 * 1024)
EDGE_PART = (0, COEF)
MESSAGE_PART = (COEF, COEF)
CONV_PART = (2 * COEF, REDUCED)
ZERO_PART = (2 * COEF + REDUCED, LMAX + 1)
SUM_START = 2 * COEF + REDUCED + LMAX + 1
SPILL = 1200


def nt_dot(left, right):
    return lax.dot_general(left, right, (((1,), (1,)), ((), ())), preferred_element_type=f32)


def nt_full(left, right):
    return lax.dot_general(
        left, right, (((1,), (1,)), ((), ())), precision=precise, preferred_element_type=f32
    )


def hot_rows(ids, count):
    rows = lax.broadcasted_iota(jnp.int32, (count, ids.shape[1]), 0)
    return (rows == ids).astype(f32)


def widen(values, channels):
    heads, edges = values.shape
    wide = jnp.broadcast_to(values[:, None, :], (heads, channels // heads, edges))
    return wide.reshape(channels, edges)


def part_of(spill, part):
    return spill.at[pl.ds(part[0], part[1])]


def chunks(channels, body):
    def step(i, carry):
        body(pl.multiple_of(i * CHUNK, CHUNK))
        return carry

    lax.fori_loop(0, channels // CHUNK, step, 0)


def rows_at(k, start):
    return pl.ds(pl.multiple_of(k * LANES + start, CHUNK), CHUNK)


def start_weights(places, first, mine, other, held, sems):
    def go(halves):
        for i, (half, at, rows, tiles) in enumerate(places):
            span = pl.ds(at, tiles * rows)
            pltpu.make_async_copy(
                halves[half].at[:, span, :], held.at[half, :, span, :], sems.at[i]
            ).start()

    @pl.when(first == 0)
    def _():
        go((mine, other))

    @pl.when(first != 0)
    def _():
        go((other, mine))


def wait_weights(places, which, mine, held, sems):
    for i in which:
        half, at, rows, tiles = places[i]
        span = pl.ds(at, tiles * rows)
        pltpu.make_async_copy(mine.at[:, span, :], held.at[half, :, span, :], sems.at[i]).wait()


def map_tiles(held, place, tiles):
    half, at, rows, _ = place
    parts = []
    for t in tiles:
        part = held[half, :, at + t * rows : at + (t + 1) * rows, :]
        parts.append(part.reshape(-1, LANES))
    return parts[0] if len(parts) == 1 else jnp.concatenate(parts, axis=1)


def pairs(count):
    return [tuple(range(i, min(i + 2, count))) for i in range(0, count, 2)]


def spread(blocks, held, rows, base, out):
    zs = held.shape[1]
    size = rows // 2
    for z in range(zs):
        for xh in range(2):
            to = base + (xh * zs + z) * size
            at = (z * 2 + xh) * size
            out[to : to + size, :] = blocks[at : at + size, :]


def by_owner(target, turned, out, group, scale=None, split=False):
    channels = turned.shape[1]
    own = target.shape[0] // group
    per = 16 // own
    for first in range(0, COEF, per):
        parts = []
        for j in range(first, first + per):
            if j < COEF:
                part = nt_dot(target, turned[j])
                part = part if scale is None else part * scale
            else:
                part = jnp.zeros((target.shape[0], channels), f32)
            parts.append(part.reshape(group, 1, own, channels))
        block = jnp.concatenate(parts, axis=1).reshape(group, 16, channels)
        at = first * own
        if split:
            half, at = at // LANES * group, at % LANES
            out[half : half + group, at : at + 16, :] = block.astype(bf16)
        else:
            out[:, at : at + 16, :] = block.astype(bf16)


def pack_kernel(places, *refs):
    count = len(places)
    shards, out = refs[:count], refs[count]
    held, acc, sems = refs[count + 1 : -2], refs[-2], refs[-1]
    copies = [pltpu.make_async_copy(shards[i], held[i], sems.at[i]) for i in range(count)]
    for copy in copies:
        copy.start()
    acc[...] = jnp.zeros_like(acc)
    for copy, shard, at in zip(copies, held, places):
        columns, rows = shard.shape
        lane = lax.broadcasted_iota(jnp.int32, (rows, acc.shape[1]), 1)
        row = lax.broadcasted_iota(jnp.int32, (rows, acc.shape[1]), 0)
        place = (lane == row + at).astype(bf16)
        copy.wait()
        acc[:columns, :] += half_dot(shard[...], place)
    out[...] = acc[...].astype(bf16)


def slab_kernel(sets, first, slabs, out):
    group, most, lanes = slabs.shape[0] // 2, slabs.shape[1] // 2, slabs.shape[2]
    blocks = [jnp.concatenate([slabs[g], slabs[group + g]], axis=0) for g in range(group)]

    def rolled(which):
        wide = [block.astype(f32) for block in blocks]
        lane = lax.broadcasted_iota(jnp.int32, wide[0].shape, 1)
        to = 0
        for rows, columns, at in which:
            size = 4 * columns
            row = lax.broadcasted_iota(jnp.int32, (size, 4 * most), 0)
            column = lax.broadcasted_iota(jnp.int32, (size, 4 * most), 1)
            chosen = (column == row // columns * most + row % columns).astype(bf16)
            tiles = [None] * (group * rows // LANES)
            for g in range(group):
                t, off = divmod(g * rows, LANES)
                shift = (off - at) % LANES
                moved = pltpu.roll(wide[g], shift, 1) if shift else wide[g]
                tiles[t] = moved if tiles[t] is None else jnp.where(lane >= off, moved, tiles[t])
                if off + rows > LANES:
                    tiles[t + 1] = moved
            for t in range(0, len(tiles), 2):
                pair = jnp.concatenate([tile.astype(bf16) for tile in tiles[t : t + 2]], axis=1)
                pair = half_dot(chosen, pair).astype(bf16)
                for i in range(len(tiles[t : t + 2])):
                    out[to : to + size, :] = pair[:, i * LANES : (i + 1) * LANES]
                    to += size
        if to < out.shape[0]:
            out[to:, :] = jnp.zeros((out.shape[0] - to, LANES), bf16)

    def lay(which):
        if lanes == LANES:
            return rolled(which)
        to = 0
        for rows, columns, at in which:
            size = 4 * columns
            row = lax.broadcasted_iota(jnp.int32, (size, 4 * most), 0)
            lane = lax.broadcasted_iota(jnp.int32, (size, 4 * most), 1)
            kept = row // columns * most + row % columns
            chosen = (lane == kept).astype(bf16)
            source = lax.broadcasted_iota(jnp.int32, (lanes, LANES), 0)
            place = lax.broadcasted_iota(jnp.int32, (lanes, LANES), 1)
            for t in range(group * rows // LANES):
                acc = None
                for g in range(group):
                    if g * rows >= (t + 1) * LANES or (g + 1) * rows <= t * LANES:
                        continue
                    shift = g * rows - t * LANES - at
                    hit = (place == source + shift) & (source >= at) & (source < at + rows)
                    term = half_dot(blocks[g], hit.astype(bf16))
                    acc = term if acc is None else acc + term
                tile = half_dot(chosen, acc.astype(bf16))
                out[to : to + size, :] = tile.astype(bf16)
                to += size
        if to < out.shape[0]:
            out[to:, :] = jnp.zeros((out.shape[0] - to, LANES), bf16)

    @pl.when(first[0, 0] == 0)
    def _():
        lay(sets[0])

    @pl.when(first[0, 0] != 0)
    def _():
        lay(sets[1])


def message_kernel(ids, stats, every, spill, out, msg, sem):
    copy = pltpu.make_async_copy(part_of(spill, MESSAGE_PART), msg, sem.at[0])
    copy.start()
    group = out.shape[0]
    count = stats.shape[1] // 2
    total = jnp.sum(every[:, :, :count], axis=0)
    share = stats[:, :count] / jnp.where(total > 0.0, total, 1.0)
    scale = widen(share, LANES).T
    copy.wait()
    by_owner(hot_rows(ids[1:2, :], count).astype(bf16), msg, out, group, scale)


def rotate_kernel(own, ids, nodes, wigner, z, spill, paired, wide, grad_edge, out_sem):
    group, edges = nodes.shape[0], wigner.shape[2]
    channels = LANES
    per = 16 // (2 * own)
    count = own * group
    target = hot_rows(ids[1:2, :], count)
    both = (target + hot_rows(ids[0:1, :], count)).astype(bf16)
    target = target.astype(bf16)
    wide[...] = wigner[...].astype(f32)
    for first in range(0, COEF, per):
        rows = nodes[:, first * 2 * own : first * 2 * own + 16, :].astype(f32)
        rows = rows.reshape(group, 2 * per, own, channels)
        for j in range(first, min(first + per, COEF)):
            at = 2 * (j - first)
            here = rows[:, at].reshape(count, channels).T.astype(bf16)
            paired[j] = half_dot(here, both).astype(bf16).astype(f32)
            here = rows[:, at + 1].reshape(count, channels).T.astype(bf16)
            grad_edge[j] = half_dot(here, target).astype(bf16)
    copy = pltpu.make_async_copy(grad_edge, part_of(spill, EDGE_PART), out_sem.at[0])
    copy.start()
    for l in range(LMAX + 1):
        for k in ROWS_OF[l]:
            acc = None
            for j in COEFS_OF[l]:
                term = wide[j, k : k + 1, :] * paired[j]
                acc = term if acc is None else acc + term
            z[k] = acc.astype(bf16)
    zero_copy = pltpu.make_async_copy(
        z.at[pl.ds(0, LMAX + 1)], part_of(spill, ZERO_PART), out_sem.at[1]
    )
    zero_copy.start()
    copy.wait()
    zero_copy.wait()


def forward_kernel(
    places,
    group,
    first,
    ids,
    z,
    wigner,
    spill_in,
    attention_t,
    mine,
    other,
    spill,
    stats,
    sent,
    scalar,
    per_edge,
    held,
    y,
    wide,
    norm,
    msg,
    heads_acc,
    grad_edge,
    sems,
    out_sem,
):
    channels, edges = LANES, wigner.shape[2]
    heads = attention_t.shape[0]
    count = stats.shape[1] // 2
    start_weights(places, first[0, 0], mine, other, held, sems)
    edge_copy = pltpu.make_async_copy(part_of(spill_in, EDGE_PART), grad_edge, out_sem.at[1])
    edge_copy.start()
    wide[...] = wigner[...].astype(f32)
    base, rows = ZERO
    acc = None
    wait_weights(places, (0,), mine, held, sems)
    for tiles in pairs(rows):
        right = z[tiles[0] : tiles[-1] + 1].reshape(-1, edges)
        term = half_dot(map_tiles(held, places[0], tiles), right)
        acc = term if acc is None else acc + term
    spread(acc, held, places[0][2], base, y)
    for (base, rows), real, imag in ((ONE, places[1], places[2]), (TWO, places[3], places[4])):
        wait_weights(places, (1, 2) if base == ONE[0] else (3, 4), mine, held, sems)
        acc = None
        for tiles in pairs(rows):
            lo, hi = base + tiles[0], base + tiles[-1] + 1
            plus = z[lo:hi].reshape(-1, edges)
            minus = z[lo + rows : hi + rows].reshape(-1, edges)
            term = half_dot(map_tiles(held, real, tiles), jnp.concatenate([plus, minus], axis=1))
            term = term + half_dot(
                map_tiles(held, imag, tiles), jnp.concatenate([-minus, plus], axis=1)
            )
            acc = term if acc is None else acc + term
        spread(acc[:, :edges], held, real[2], base * channels, y)
        spread(acc[:, edges:], held, real[2], (base + rows) * channels, y)
    value = y[:channels, :]
    scalar[...] = value
    y[...] = y[...].astype(bf16).astype(f32)
    gating = (value / (1.0 + jnp.exp(-value))).astype(bf16)
    logits = half_dot(attention_t[...], gating)
    weight = jnp.where(ids[2:3, :] > 0, jnp.exp(logits), 0.0)
    target = hot_rows(ids[1:2, :], count)
    own_sum = nt_full(weight, target)
    at_edges = full_dot(own_sum, target)
    own_norm = weight / jnp.where(at_edges > 0.0, at_edges, 1.0)
    norm[...] = widen(own_norm, channels)

    def body(start):
        at = pl.ds(start, CHUNK)
        own = norm[at, :]
        total = jnp.zeros((CHUNK, edges), f32)
        for l in range(LMAX + 1):
            for j in COEFS_OF[l]:
                acc = None
                for k in ROWS_OF[l]:
                    term = wide[j, k : k + 1, :] * y[rows_at(k, start), :]
                    acc = term if acc is None else acc + term
                total = total + acc * grad_edge[j, at, :].astype(f32)
                msg[j, at, :] = (acc * own).astype(bf16)
        heads_acc[at, :] = total

    edge_copy.wait()
    chunks(channels, body)
    copy = pltpu.make_async_copy(msg, part_of(spill, MESSAGE_PART), out_sem.at[0])
    copy.start()
    grad_norm = jnp.sum(heads_acc[...].reshape(heads, channels // heads, edges), axis=1)
    own_shared = nt_full(own_norm * grad_norm, target)
    sums = jnp.concatenate([own_sum, own_shared], axis=1)
    stats[...] = sums
    for owner in range(group):
        sent[owner] = sums
    per_edge[:heads, :] = own_norm
    per_edge[heads:, :] = grad_norm
    copy.wait()


def backward_kernel(
    first,
    ids,
    stats,
    every,
    scalar,
    per_edge,
    wigner,
    spill_in,
    attention,
    attention_t,
    spill,
    mine,
    theirs,
    wide,
    norm,
    grad,
    turned,
    grad_conv,
    grad_edge,
    z,
    out_sem,
):
    channels, edges = LANES, wigner.shape[2]
    heads = attention_t.shape[0]
    count = stats.shape[1] // 2
    edge_copy = pltpu.make_async_copy(part_of(spill_in, EDGE_PART), grad_edge, out_sem.at[1])
    edge_copy.start()
    zero_copy = pltpu.make_async_copy(part_of(spill_in, ZERO_PART), z, out_sem.at[2])
    zero_copy.start()
    wide[...] = wigner[...].astype(f32)
    total = jnp.sum(every[:, :, :count], axis=0)
    total = jnp.where(total > 0.0, total, 1.0)
    shares = every[:, :, :count] / total[None]
    shared = jnp.sum(shares * every[:, :, count:], axis=0)
    own_share = stats[:, :count] / total
    target = hot_rows(ids[1:2, :], count)
    normalized = per_edge[:heads, :] * full_dot(own_share, target)
    grad_logit = normalized * (per_edge[heads:, :] - full_dot(shared, target))
    value = scalar[...]
    sigmoid = 1.0 / (1.0 + jnp.exp(-value))
    gating = (value / (1.0 + jnp.exp(-value))).astype(bf16).astype(f32)
    att = nt_full(grad_logit, gating)
    grad_gating = full_dot(attention[...].astype(f32), grad_logit)
    grad_scalar = grad_gating * sigmoid * (1.0 + value * (1.0 - sigmoid))
    norm[...] = widen(normalized, channels)

    def body(start):
        at = pl.ds(start, CHUNK)
        own = norm[at, :]
        for l in range(LMAX + 1):
            fields = [
                (grad_edge[j, at, :].astype(f32) * own).astype(bf16).astype(f32)
                for j in COEFS_OF[l]
            ]
            for k in ROWS_OF[l]:
                acc = None
                for j, field in zip(COEFS_OF[l], fields):
                    term = wide[j, k : k + 1, :] * field
                    acc = term if acc is None else acc + term
                grad[rows_at(k, start), :] = acc

    edge_copy.wait()
    chunks(channels, body)
    grad[:channels, :] = grad[:channels, :] + grad_scalar
    depth = (LMAX + 1) * channels
    parts, share = mine.shape[0], depth // (2 * mine.shape[0])
    grad_conv[...] = grad[...].astype(bf16).reshape(grad_conv.shape)
    copy = pltpu.make_async_copy(grad_conv, part_of(spill, CONV_PART), out_sem.at[0])
    copy.start()
    zero_copy.wait()
    turned[:depth, :] = nt_dot(
        grad_conv[: LMAX + 1].reshape(depth, edges), z[...].reshape(depth, edges)
    )
    turned[depth:, :] = jnp.zeros((turned.shape[0] - depth, depth), f32)
    padded = mine.shape[1]
    tail_row = lax.broadcasted_iota(jnp.int32, (padded, depth), 0)
    one = jnp.concatenate([att[h : h + 1, :] for h in range(LMAX + 1)], axis=1)
    two = [att[h : h + 1, :] for h in range(LMAX + 1, heads)]
    two = jnp.concatenate(two + [jnp.zeros((1, depth - len(two) * channels), f32)], axis=1)

    def store(outs):
        for core in range(2):
            for part in range(parts):
                at = (2 * part + core) * share
                block = turned[at : at + padded, :]
                block = jnp.where(tail_row == share, one, block)
                block = jnp.where(tail_row == share + 1, two, block)
                outs[core][part] = block.astype(bf16)

    @pl.when(first[0, 0] == 0)
    def _():
        store((mine, theirs))

    @pl.when(first[0, 0] != 0)
    def _():
        store((theirs, mine))

    copy.wait()


def scatter_kernel(
    places,
    group,
    own,
    first,
    ids,
    spill,
    wigner,
    mine,
    other,
    spill_out,
    held,
    wide,
    dz,
    gp,
    grad,
    grad_rows,
    grads,
    grad_conv,
    sems,
    out_sem,
):
    channels, edges = LANES, wigner.shape[2]
    count = own * group
    conv_copy = pltpu.make_async_copy(part_of(spill, CONV_PART), grad_conv, out_sem.at[1])
    conv_copy.start()
    start_weights(places, first[0, 0], mine, other, held, sems)
    wide[...] = wigner[...].astype(f32)
    conv_copy.wait()
    grad[...] = grad_conv[...].astype(f32).reshape(grad.shape)
    zs = held.shape[1]
    for base, rows in (ZERO, ONE, (ONE[0] + ONE[1], ONE[1]), TWO, (TWO[0] + TWO[1], TWO[1])):
        size = rows * channels // (2 * zs)
        blocks = []
        for zz in range(zs):
            for xh in range(2):
                at = base * channels + (xh * zs + zz) * size
                blocks.append(grad[at : at + size, :])
        ordered = jnp.concatenate(blocks, axis=0)
        for t in range(rows):
            at = slice(t * channels, (t + 1) * channels)
            to = (base + t) * channels
            grad_rows[:, to : to + channels] = ordered[at, :].T.astype(bf16)
    base, rows = ZERO
    left = grad_rows[:, : rows * channels]
    wait_weights(places, (0,), mine, held, sems)
    for tiles in pairs(rows):
        out = half_dot(left, map_tiles(held, places[0], tiles)).astype(bf16).astype(f32)
        for i, t in enumerate(tiles):
            dz[t] = out[:, i * channels : (i + 1) * channels].T
    for (base, rows), real, imag in ((ONE, places[1], places[2]), (TWO, places[3], places[4])):
        wait_weights(places, (1, 2) if base == ONE[0] else (3, 4), mine, held, sems)
        plus = grad_rows[:, base * channels : (base + rows) * channels]
        minus = grad_rows[:, (base + rows) * channels : (base + 2 * rows) * channels]
        left = jnp.concatenate([plus, minus], axis=0)
        crossed = jnp.concatenate([minus, -plus], axis=0)
        for tiles in pairs(rows):
            out = half_dot(left, map_tiles(held, real, tiles))
            out = out + half_dot(crossed, map_tiles(held, imag, tiles))
            out = out.astype(bf16).astype(f32)
            for i, t in enumerate(tiles):
                at = slice(i * channels, (i + 1) * channels)
                dz[base + t] = out[:edges, at].T
                dz[base + rows + t] = out[edges:, at].T

    def body(start):
        at = pl.ds(start, CHUNK)
        for l in range(LMAX + 1):
            for j in COEFS_OF[l]:
                acc = None
                for k in ROWS_OF[l]:
                    term = wide[j, k : k + 1, :] * dz[k, at, :]
                    acc = term if acc is None else acc + term
                gp[j, at, :] = acc.astype(bf16)

    chunks(channels, body)
    both = (hot_rows(ids[1:2, :], count) + hot_rows(ids[0:1, :], count)).astype(bf16)
    by_owner(both, gp, grads, group, split=True)
    copy = pltpu.make_async_copy(
        grads, part_of(spill_out, (SUM_START, grads.shape[0])), out_sem.at[0]
    )
    copy.start()
    copy.wait()


def node_rows(own):
    return -(-COEF * own // 16) * 16


def one_hot(rows, columns, shift, low, high):
    row = lax.broadcasted_iota(jnp.int32, (rows, columns), 0)
    column = lax.broadcasted_iota(jnp.int32, (rows, columns), 1)
    return ((column == row + shift) & (row >= low) & (row < high)).astype(bf16)


def tail_kernel(used, share, heads, parts, spill, grads, total, att, sems):
    count, depth = parts.shape[0], parts.shape[2]
    group = grads.shape[0]
    inner, skip = depth // group, used % 16
    base, rows = used - skip, grads.shape[1] - (used - skip)
    low_copy = pltpu.make_async_copy(
        spill.at[pl.ds(SUM_START, group)], grads.at[:, pl.ds(0, LANES), :], sems.at[0]
    )
    high_copy = pltpu.make_async_copy(
        spill.at[pl.ds(SUM_START + group, group), pl.ds(0, base + 16 - LANES), :],
        grads.at[:, pl.ds(LANES, base + 16 - LANES), :],
        sems.at[1],
    )
    low_copy.start()
    high_copy.start()
    acc = parts[0].astype(f32)
    for p in range(1, count):
        acc = acc + parts[p].astype(f32)
    total[...] = acc
    for h in range(heads):
        row, at = share + h // (depth // LANES), h % (depth // LANES) * LANES
        att[h : h + 1, :] = total[row : row + 1, at : at + LANES]
    low = att[...].astype(bf16)
    half = LANES // 2
    left = half_dot(low, one_hot(LANES, LANES, half, 0, half)).astype(bf16)
    right = half_dot(low, one_hot(LANES, LANES, 0, half, LANES)).astype(bf16)
    row = lax.broadcasted_iota(jnp.int32, (rows, heads), 0)
    head = lax.broadcasted_iota(jnp.int32, (rows, heads), 1)
    tail = half_dot((row == head + skip).astype(bf16), left)
    tail = tail + half_dot((row == head + skip + heads).astype(bf16), right)
    moved = half_dot(one_hot(rows, total.shape[0], -skip, skip, skip + share), acc.astype(bf16))
    moved = moved.astype(bf16)
    kept = lax.broadcasted_iota(jnp.int32, (rows, LANES), 0) < skip
    low_copy.wait()
    high_copy.wait()
    for g in range(group):
        first = g * inner // LANES * LANES
        last = -(-(g + 1) * inner // LANES) * LANES
        shift = g * inner - first
        place = one_hot(last - first, LANES, -shift, shift, shift + inner)
        piece = half_dot(moved[:, first:last], place) + tail
        before = grads[g, base : base + 16, :].astype(f32)
        if rows > 16:
            before = jnp.concatenate([before, jnp.zeros((rows - 16, LANES), f32)], axis=0)
        grads[g, base:, :] = jnp.where(kept, before, piece).astype(bf16)


def last_kernel(scale, parts, nodes, zero, att, total):
    acc = parts[0].astype(f32)
    for g in range(1, parts.shape[0]):
        acc = acc + parts[g].astype(f32)
    total[...] = acc
    used = nodes.shape[0] * nodes.shape[1]
    heads, half = att.shape[0], LANES // 2
    nodes[...] = acc[:used].astype(bf16).reshape(nodes.shape)
    zero[...] = total[used : used + zero.shape[0], :][:, : zero.shape[1]] * scale
    left = full_dot(
        total[used : used + heads, :], one_hot(LANES, LANES, -half, half, LANES).astype(f32)
    )
    lane = lax.broadcasted_iota(jnp.int32, (heads, LANES), 1)
    right = jnp.where(lane >= half, total[used + heads : used + 2 * heads, :], 0.0)
    att[...] = (left + right) * scale


def sum_kernel(parts, nodes, tail, total):
    acc = parts[0].astype(f32)
    for g in range(1, parts.shape[0]):
        acc = acc + parts[g].astype(f32)
    total[...] = acc
    used = nodes.shape[0] * nodes.shape[1]
    nodes[...] = acc[:used].astype(bf16).reshape(nodes.shape)
    tail[...] = total[used : used + tail.shape[0], :]


def pad_to(block, rows, columns):
    return jnp.pad(block, ((0, rows - block.shape[0]), (0, columns - block.shape[1])))


def whole_lanes(count):
    return -(-count // LANES) * LANES


def gather_weights(shards):
    rows = [w.shape[0] for w in shards]
    columns = [w.shape[1] for w in shards]
    most = -(-max(columns) // 16) * 16
    sets = ((0, 1), (2, 3, 4))
    lanes = whole_lanes(max(sum(rows[i] for i in s) for s in sets))
    starts = [0] * len(shards)
    for half_index, s in enumerate(sets):
        for n, i in enumerate(s):
            starts[i] = half_index * lanes + sum(rows[j] for j in s[:n])
    packed = pl.pallas_call(
        functools.partial(pack_kernel, starts),
        out_shape=jax.ShapeDtypeStruct((most, 2 * lanes), bf16),
        in_specs=[HBM] * len(shards),
        out_specs=VMEM,
        scratch_shapes=[pltpu.VMEM(w.shape[::-1], bf16) for w in shards]
        + [pltpu.VMEM((most, 2 * lanes), f32), pltpu.SemaphoreType.DMA((len(shards),))],
        compiler_params=WHOLE,
    )(*[w.T for w in shards])
    core = lax.axis_index("core")
    near = lax.all_gather(packed, "core")
    sent = lax.dynamic_slice_in_dim(near, core * lanes, lanes, axis=2)
    slabs = gather(sent.reshape(2 * most, lanes), ROW_GROUP)
    group = slabs.shape[0] // 2
    places = [None] * len(shards)
    depth = 0
    for half_index, s in enumerate(sets):
        at = 0
        for i in s:
            tiles = group * rows[i] // LANES
            places[i] = (half_index, at, 4 * columns[i], tiles)
            at += tiles * 4 * columns[i]
        depth = max(depth, at)
    kinds = [[(rows[i], columns[i], starts[i] - n * lanes) for i in s] for n, s in enumerate(sets)]
    tiled = pl.pallas_call(
        functools.partial(slab_kernel, kinds),
        out_shape=jax.ShapeDtypeStruct((depth, LANES), bf16),
        in_specs=[pl.BlockSpec(memory_space=pltpu.SMEM), VMEM],
        out_specs=VMEM,
        compiler_params=SMALL,
    )(core.astype(jnp.int32).reshape(1, 1), slabs)
    return lax.all_gather(tiled, "z"), places, tiled


def on_device(
    embeddings,
    atom_counts,
    edge_counts,
    source,
    target,
    wigner,
    cotangent,
    w_zero,
    w_one_real,
    w_one_imag,
    w_two_real,
    w_two_imag,
    attention,
):
    half, places, tiled = gather_weights((w_zero, w_one_real, w_one_imag, w_two_real, w_two_imag))
    row_count = embeddings.shape[1]
    harmonics = embeddings.shape[2]
    channels = embeddings.shape[3]
    width = harmonics * channels
    edge_rows = source.shape[1]
    head_count = attention.shape[1]
    group = lax.axis_size(GRAPH)
    all_nodes = row_count * group
    rotation = jnp.transpose(wigner[0], (1, 0, 2))
    in_use = (lax.iota(jnp.int32, edge_rows) < edge_counts[0, 0]).astype(jnp.int32)
    ids = jnp.stack([source[0], target[0], in_use] + [jnp.zeros_like(in_use)] * 5)
    attention_t = attention.T
    core = lax.axis_index("core")
    first = core.astype(jnp.int32).reshape(1, 1)
    own_first = lax.axis_index(GRAPH) * row_count
    present = ((own_first + lax.iota(jnp.int32, row_count)) < atom_counts[0])[:, None]
    cot_rows = jnp.where(present[:, :, None], cotangent[0], 0.0).astype(bf16)
    own_rows = jnp.stack([embeddings[0], cot_rows])
    own_rows = jnp.transpose(own_rows, (2, 0, 1, 3)).reshape(-1, channels)
    own_rows = pad_to(own_rows, -(-own_rows.shape[0] // 16) * 16, channels)
    own_rows, tiled = lax.optimization_barrier((own_rows, tiled))
    nodes = gather(own_rows, GRAPH)
    half, nodes = lax.optimization_barrier((half, nodes))
    other = lax.ppermute(half, "core", [(0, 1), (1, 0)])

    smem = pl.BlockSpec(memory_space=pltpu.SMEM)
    field = (channels, edge_rows)
    wide = pltpu.VMEM(rotation.shape, f32)
    spill_shape = jax.ShapeDtypeStruct((SPILL,) + field, bf16)
    out_copy = pltpu.SemaphoreType.DMA((1,))
    two_copies = pltpu.SemaphoreType.DMA((2,))
    edge_field = pltpu.VMEM((COEF,) + field, bf16)
    z, spill = pl.pallas_call(
        functools.partial(rotate_kernel, row_count),
        out_shape=(
            jax.ShapeDtypeStruct((REDUCED,) + field, bf16),
            spill_shape,
        ),
        in_specs=[VMEM] * 3,
        out_specs=[VMEM, HBM],
        scratch_shapes=[
            pltpu.VMEM((COEF,) + field, f32),
            wide,
            edge_field,
            two_copies,
        ],
        compiler_params=LARGE,
    )(ids, nodes, rotation)
    held = pltpu.VMEM((2,) + half.shape, bf16)
    copies = pltpu.SemaphoreType.DMA((len(places),))

    span = node_rows(row_count)
    sums = (head_count, 2 * all_nodes)
    spill, stats, sent, scalar, per_edge = pl.pallas_call(
        functools.partial(forward_kernel, places, group),
        out_shape=(
            spill_shape,
            jax.ShapeDtypeStruct(sums, f32),
            jax.ShapeDtypeStruct((group,) + sums, f32),
            jax.ShapeDtypeStruct(field, f32),
            jax.ShapeDtypeStruct((2 * head_count, edge_rows), f32),
        ),
        in_specs=[smem] + [VMEM] * 3 + [HBM, VMEM] + [HBM] * 2,
        out_specs=[HBM] + [VMEM] * 4,
        scratch_shapes=[
            held,
            pltpu.VMEM((REDUCED * channels, edge_rows), f32),
            wide,
            pltpu.VMEM(field, f32),
            pltpu.VMEM((COEF,) + field, bf16),
            pltpu.VMEM(field, f32),
            edge_field,
            copies,
            two_copies,
        ],
        input_output_aliases={4: 0},
        compiler_params=LARGE,
    )(first, ids, z, rotation, spill, attention_t, half, other)
    every = exchange(sent, GRAPH)

    columns = lax.axis_size(COLUMN_GROUP)
    depth = channels * (LMAX + 1)
    share = depth // (2 * columns)
    padded = -(-(share + 2) // 16) * 16
    partial = jax.ShapeDtypeStruct((columns, padded, depth), bf16)
    spill, mine, theirs = pl.pallas_call(
        backward_kernel,
        out_shape=(
            spill_shape,
            partial,
            partial,
        ),
        in_specs=[smem] + [VMEM] * 6 + [HBM] + [VMEM] * 2,
        out_specs=[HBM] + [VMEM] * 2,
        scratch_shapes=[
            wide,
            pltpu.VMEM(field, f32),
            pltpu.VMEM((REDUCED * channels, edge_rows), f32),
            pltpu.VMEM((depth + padded, depth), f32),
            pltpu.VMEM((REDUCED,) + field, bf16),
            edge_field,
            pltpu.VMEM((LMAX + 1,) + field, bf16),
            pltpu.SemaphoreType.DMA((3,)),
        ],
        input_output_aliases={7: 0},
        compiler_params=LARGE,
    )(first, ids, stats, every, scalar, per_edge, rotation, spill, attention, attention_t)

    theirs = lax.ppermute(theirs, "core", [(0, 1), (1, 0)])
    message_sums = pl.pallas_call(
        message_kernel,
        out_shape=jax.ShapeDtypeStruct((group, span, channels), bf16),
        in_specs=[VMEM] * 3 + [HBM],
        out_specs=VMEM,
        scratch_shapes=[edge_field, out_copy],
        compiler_params=LARGE,
    )(ids, stats, every, spill)
    theirs, message_sums, spill = lax.optimization_barrier((theirs, message_sums, spill))
    mine = (mine.astype(f32) + theirs.astype(f32)).astype(bf16)
    zero_parts = exchange(mine, COLUMN_GROUP)
    message_sums = message_sums.reshape(group // 2, 2 * span, channels)
    near_sums = lax.psum_scatter(message_sums, "y", scatter_dimension=0, tiled=True)
    near_sums = near_sums.reshape(2, span, channels)
    side = lax.axis_index("xl")
    kept = lax.dynamic_index_in_dim(near_sums, side, keepdims=False)
    passed = lax.dynamic_index_in_dim(near_sums, 1 - side, keepdims=False)
    passed = lax.ppermute(passed, "xl", [(0, 1), (1, 0)])
    summed = kept.astype(f32) + passed.astype(f32)
    used = harmonics * row_count
    inner = depth // group
    lanes = whole_lanes(inner)
    beside = lanes - inner >= channels // 2 and lanes == channels and share >= 2 * head_count
    tail_rows = share if beside else share * lanes // LANES + head_count
    spill = pl.pallas_call(
        functools.partial(scatter_kernel, places, group, row_count),
        out_shape=spill_shape,
        in_specs=[smem, VMEM, HBM, VMEM] + [HBM] * 2,
        out_specs=HBM,
        scratch_shapes=[
            held,
            wide,
            pltpu.VMEM((REDUCED,) + field, f32),
            pltpu.VMEM((COEF,) + field, bf16),
            pltpu.VMEM((REDUCED * channels, edge_rows), f32),
            pltpu.VMEM((edge_rows, REDUCED * channels), bf16),
            pltpu.VMEM((2 * group, channels, channels), bf16),
            pltpu.VMEM((REDUCED,) + field, bf16),
            copies,
            two_copies,
        ],
        input_output_aliases={2: 0},
        compiler_params=LARGE,
    )(first, ids, spill, rotation, half, other)
    sums_shape = (group, -(-(used + tail_rows) // 16) * 16, channels)
    nodes_shape = jax.ShapeDtypeStruct((harmonics, row_count, channels), bf16)
    batch_scale = 1.0 / (2 * columns)
    if beside:
        grad_sums = pl.pallas_call(
            functools.partial(tail_kernel, used, share, head_count),
            out_shape=jax.ShapeDtypeStruct(sums_shape, bf16),
            in_specs=[VMEM, HBM],
            out_specs=VMEM,
            scratch_shapes=[
                pltpu.VMEM((padded, depth), f32),
                pltpu.VMEM((head_count, channels), f32),
                two_copies,
            ],
            compiler_params=SMALL,
        )(zero_parts, spill)
        last = exchange(grad_sums, GRAPH)
        grad_nodes, grad_zero, grad_att = pl.pallas_call(
            functools.partial(last_kernel, batch_scale),
            out_shape=(
                nodes_shape,
                jax.ShapeDtypeStruct((share, inner), f32),
                jax.ShapeDtypeStruct((head_count, channels), f32),
            ),
            in_specs=[VMEM],
            out_specs=[VMEM] * 3,
            scratch_shapes=[pltpu.VMEM(last.shape[1:], f32)],
            compiler_params=SMALL,
        )(last)
        grad_zero, grad_att = grad_zero.T, grad_att.T
    else:
        zero_sum = jnp.sum(zero_parts.astype(f32), axis=0)
        att = zero_sum[share : share + 2].reshape(-1)[: head_count * channels]
        zero_send = jnp.transpose(zero_sum[:share].reshape(share, group, inner), (1, 0, 2))
        zero_send = jnp.pad(zero_send, ((0, 0), (0, 0), (0, lanes - inner)))
        zero_send = zero_send.reshape(group, share * lanes // LANES, LANES)
        att = jnp.broadcast_to(
            att.reshape(1, head_count, channels), (group, head_count, channels)
        )
        last_rows = jnp.concatenate([zero_send, att], axis=1).astype(bf16)
        grad_sums = spill[SUM_START : SUM_START + 2 * group].reshape(2, group, channels, channels)
        grad_sums = jnp.transpose(grad_sums, (1, 0, 2, 3)).reshape(group, 2 * channels, channels)
        rest = jnp.zeros(sums_shape, bf16)
        grad_sums = lax.dynamic_update_slice(rest, grad_sums[:, :used], (0, 0, 0))
        grad_sums = lax.dynamic_update_slice(grad_sums, last_rows, (0, used, 0))
        last = exchange(grad_sums, GRAPH)
        grad_nodes, tail = pl.pallas_call(
            sum_kernel,
            out_shape=(nodes_shape, jax.ShapeDtypeStruct((tail_rows, channels), f32)),
            in_specs=[VMEM],
            out_specs=[VMEM] * 2,
            scratch_shapes=[pltpu.VMEM(last.shape[1:], f32)],
            compiler_params=SMALL,
        )(last)
        tail = tail * batch_scale
        zero_rows = share * lanes // LANES
        grad_zero = tail[:zero_rows].reshape(share, lanes)[:, :inner].T
        grad_att = tail[zero_rows:].T
    update = summed[:used].reshape(harmonics, row_count, channels)
    update = jnp.transpose(jnp.where(present[None], update, 0.0).astype(bf16), (1, 0, 2))
    grad_nodes = jnp.transpose(grad_nodes, (1, 0, 2))

    shape = (1, row_count, harmonics, channels)
    return (update.reshape(shape), grad_nodes.reshape(shape), grad_zero, grad_att)


def solution(mesh):
    columns, group = mesh.shape["dp"], mesh.shape["graph"]
    devices = mesh.devices.reshape(2, columns // 4, 2, group // 2, 2)
    fine = Mesh(devices, DP + GRAPH)
    in_specs = (
        P(DP, GRAPH, None, None),
        P(DP),
        P(DP, GRAPH),
        P(DP, GRAPH),
        P(DP, GRAPH),
        P(DP, None, None, GRAPH),
        P(DP, GRAPH, None, None),
        P(GRAPH, DP),
        P(GRAPH, DP),
        P(GRAPH, DP),
        P(GRAPH, DP),
        P(GRAPH, DP),
        P(),
    )
    out_specs = (P(DP, GRAPH, None, None), P(DP, GRAPH, None, None), P(GRAPH, DP), P())
    return jax.shard_map(
        on_device, mesh=fine, in_specs=in_specs, out_specs=out_specs, check_vma=False
    )
```

```python
import functools

import jax
import jax.numpy as jnp
from jax import lax
from jax.experimental import pallas as pl
from jax.experimental.pallas import tpu as pltpu
from jax.sharding import Mesh, PartitionSpec as P

LMAX = 6
LANES = 128
DP = ("xh", "z", "core")
COLUMN_GROUP = ("xh", "z")
ROW_GROUP = ("xh", "y", "xl")
GRAPH = ("y", "xl")
precise = lax.Precision.HIGHEST
f32 = jnp.float32
bf16 = jnp.bfloat16


def half_dot(left, right):
    return jnp.dot(left, right, preferred_element_type=f32)


def full_dot(left, right):
    return jnp.dot(left, right, precision=precise, preferred_element_type=f32)


def gather(block, axes):
    count = lax.axis_size(axes)
    copies = jnp.broadcast_to(block[None], (count,) + block.shape)
    return lax.all_to_all(copies, axes, split_axis=0, concat_axis=0, tiled=True)


def exchange(blocks, axes):
    return lax.all_to_all(blocks, axes, split_axis=0, concat_axis=0, tiled=True)


ROW_DEGREE = (
    list(range(LMAX + 1)) + list(range(1, LMAX + 1)) * 2 + list(range(2, LMAX + 1)) * 2
)
ROWS_OF = [[k for k, d in enumerate(ROW_DEGREE) if d == l] for l in range(LMAX + 1)]
COEFS_OF = [list(range(l * l, (l + 1) * (l + 1))) for l in range(LMAX + 1)]
REDUCED = len(ROW_DEGREE)
COEF = (LMAX + 1) ** 2
ZERO = (0, LMAX + 1)
ONE = (LMAX + 1, LMAX)
TWO = (3 * LMAX + 1, LMAX - 1)
CHUNK = 32
VMEM = pl.BlockSpec(memory_space=pltpu.VMEM)
HBM = pl.BlockSpec(memory_space=pltpu.HBM)
SMALL = pltpu.CompilerParams(vmem_limit_bytes=28 * 1024 * 1024)
LARGE = pltpu.CompilerParams(vmem_limit_bytes=48 * 1024 * 1024)
WHOLE = pltpu.CompilerParams(vmem_limit_bytes=60 * 1024 * 1024)
EDGE_PART = (0, COEF)
MESSAGE_PART = (COEF, COEF)
CONV_PART = (2 * COEF, REDUCED)
ZERO_PART = (2 * COEF + REDUCED, LMAX + 1)
SUM_START = 2 * COEF + REDUCED + LMAX + 1
SPILL = 600
MAP_SLOTS = 7


def nt_dot(left, right):
    return lax.dot_general(left, right, (((1,), (1,)), ((), ())), preferred_element_type=f32)


def nt_full(left, right):
    return lax.dot_general(
        left, right, (((1,), (1,)), ((), ())), precision=precise, preferred_element_type=f32
    )


def hot_rows(ids, count):
    rows = lax.broadcasted_iota(jnp.int32, (count, ids.shape[1]), 0)
    return (rows == ids).astype(f32)


def widen(values, channels):
    heads, edges = values.shape
    wide = jnp.broadcast_to(values[:, None, :], (heads, channels // heads, edges))
    return wide.reshape(channels, edges)


def part_of(spill, part):
    return spill.at[pl.ds(part[0], part[1])]


def chunks(channels, body):
    def step(i, carry):
        body(pl.multiple_of(i * CHUNK, CHUNK))
        return carry

    lax.fori_loop(0, channels // CHUNK, step, 0)


def rows_at(k, start):
    return pl.ds(pl.multiple_of(k * LANES + start, CHUNK), CHUNK)


def start_weights(places, first, mine, other, held, sems):
    def go(halves):
        for i, (half, at, rows, tiles) in enumerate(places):
            span = pl.ds(at, tiles * rows)
            pltpu.make_async_copy(
                halves[half].at[:, span, :], held.at[half, :, span, :], sems.at[i]
            ).start()

    if first is None:
        return go((mine, other))

    @pl.when(first == 0)
    def _():
        go((mine, other))

    @pl.when(first != 0)
    def _():
        go((other, mine))


def wait_weights(places, which, mine, held, sems):
    for i in which:
        half, at, rows, tiles = places[i]
        span = pl.ds(at, tiles * rows)
        pltpu.make_async_copy(mine.at[:, span, :], held.at[half, :, span, :], sems.at[i]).wait()


def map_tiles(held, place, tiles):
    half, at, rows, _ = place
    parts = []
    for t in tiles:
        part = held[half, :, at + t * rows : at + (t + 1) * rows, :]
        parts.append(part.reshape(-1, LANES))
    return parts[0] if len(parts) == 1 else jnp.concatenate(parts, axis=1)


def pairs(count):
    return [tuple(range(i, min(i + 2, count))) for i in range(0, count, 2)]


def spread(blocks, held, rows, base, out):
    zs = held.shape[1]
    size = rows // 2
    for z in range(zs):
        for xh in range(2):
            to = base + (xh * zs + z) * size
            at = (z * 2 + xh) * size
            out[to : to + size, :] = blocks[at : at + size, :]


def by_owner(target, turned, out, group, scale=None, split=False):
    channels = turned.shape[1]
    own = target.shape[0] // group
    per = 16 // own
    for first in range(0, COEF, per):
        parts = []
        for j in range(first, first + per):
            if j < COEF:
                part = nt_dot(target, turned[j])
                part = part if scale is None else part * scale
            else:
                part = jnp.zeros((target.shape[0], channels), f32)
            parts.append(part.reshape(group, 1, own, channels))
        block = jnp.concatenate(parts, axis=1).reshape(group, 16, channels)
        at = first * own
        if split:
            half, at = at // LANES * group, at % LANES
            out[half : half + group, at : at + 16, :] = block.astype(bf16)
        else:
            out[:, at : at + 16, :] = block.astype(bf16)


def pack_kernel(places, *refs):
    count = len(places)
    shards, out = refs[:count], refs[count]
    held, acc, sems = refs[count + 1 : -2], refs[-2], refs[-1]
    copies = [pltpu.make_async_copy(shards[i], held[i], sems.at[i]) for i in range(count)]
    for copy in copies:
        copy.start()
    acc[...] = jnp.zeros_like(acc)
    for copy, shard, at in zip(copies, held, places):
        columns, rows = shard.shape
        lane = lax.broadcasted_iota(jnp.int32, (rows, acc.shape[1]), 1)
        row = lax.broadcasted_iota(jnp.int32, (rows, acc.shape[1]), 0)
        place = (lane == row + at).astype(bf16)
        copy.wait()
        acc[:columns, :] += half_dot(shard[...], place)
    out[...] = acc[...].astype(bf16)


def slab_kernel(sets, first, slabs, out):
    group, most, lanes = slabs.shape[0] // 2, slabs.shape[1] // 2, slabs.shape[2]
    blocks = [jnp.concatenate([slabs[g], slabs[group + g]], axis=0) for g in range(group)]

    def rolled(which):
        wide = [block.astype(f32) for block in blocks]
        lane = lax.broadcasted_iota(jnp.int32, wide[0].shape, 1)
        to = 0
        for rows, columns, at in which:
            size = 4 * columns
            row = lax.broadcasted_iota(jnp.int32, (size, 4 * most), 0)
            column = lax.broadcasted_iota(jnp.int32, (size, 4 * most), 1)
            chosen = (column == row // columns * most + row % columns).astype(bf16)
            tiles = [None] * (group * rows // LANES)
            for g in range(group):
                t, off = divmod(g * rows, LANES)
                shift = (off - at) % LANES
                moved = pltpu.roll(wide[g], shift, 1) if shift else wide[g]
                tiles[t] = moved if tiles[t] is None else jnp.where(lane >= off, moved, tiles[t])
                if off + rows > LANES:
                    tiles[t + 1] = moved
            for t in range(0, len(tiles), 2):
                pair = jnp.concatenate([tile.astype(bf16) for tile in tiles[t : t + 2]], axis=1)
                pair = half_dot(chosen, pair).astype(bf16)
                for i in range(len(tiles[t : t + 2])):
                    out[to : to + size, :] = pair[:, i * LANES : (i + 1) * LANES]
                    to += size
        if to < out.shape[0]:
            out[to:, :] = jnp.zeros((out.shape[0] - to, LANES), bf16)

    def lay(which):
        if lanes == LANES:
            return rolled(which)
        to = 0
        for rows, columns, at in which:
            size = 4 * columns
            row = lax.broadcasted_iota(jnp.int32, (size, 4 * most), 0)
            lane = lax.broadcasted_iota(jnp.int32, (size, 4 * most), 1)
            kept = row // columns * most + row % columns
            chosen = (lane == kept).astype(bf16)
            source = lax.broadcasted_iota(jnp.int32, (lanes, LANES), 0)
            place = lax.broadcasted_iota(jnp.int32, (lanes, LANES), 1)
            for t in range(group * rows // LANES):
                acc = None
                for g in range(group):
                    if g * rows >= (t + 1) * LANES or (g + 1) * rows <= t * LANES:
                        continue
                    shift = g * rows - t * LANES - at
                    hit = (place == source + shift) & (source >= at) & (source < at + rows)
                    term = half_dot(blocks[g], hit.astype(bf16))
                    acc = term if acc is None else acc + term
                tile = half_dot(chosen, acc.astype(bf16))
                out[to : to + size, :] = tile.astype(bf16)
                to += size
        if to < out.shape[0]:
            out[to:, :] = jnp.zeros((out.shape[0] - to, LANES), bf16)

    @pl.when(first[0, 0] == 0)
    def _():
        lay(sets[0])

    @pl.when(first[0, 0] != 0)
    def _():
        lay(sets[1])


def message_kernel(ids, stats, every, spill, out, msg, sem):
    copy = pltpu.make_async_copy(part_of(spill, MESSAGE_PART), msg, sem.at[0])
    copy.start()
    group = out.shape[0]
    count = stats.shape[1] // 2
    total = jnp.sum(every[:, :, :count], axis=0)
    share = stats[:, :count] / jnp.where(total > 0.0, total, 1.0)
    scale = widen(share, LANES).T
    copy.wait()
    by_owner(hot_rows(ids[1:2, :], count).astype(bf16), msg, out, group, scale)


def rotate_kernel(
    own, ids, nodes, wigner, half, z, spill, maps, paired, wide, grad_edge, out_sem
):
    group, edges = nodes.shape[0], wigner.shape[2]
    channels = LANES
    per = 16 // (2 * own)
    count = own * group
    half_copy = pltpu.make_async_copy(half, maps.at[2], out_sem.at[2])
    half_copy.start()
    target = hot_rows(ids[1:2, :], count)
    both = (target + hot_rows(ids[0:1, :], count)).astype(bf16)
    target = target.astype(bf16)
    wide[...] = wigner[...].astype(f32)
    for first in range(0, COEF, per):
        rows = nodes[:, first * 2 * own : first * 2 * own + 16, :].astype(f32)
        rows = rows.reshape(group, 2 * per, own, channels)
        for j in range(first, min(first + per, COEF)):
            at = 2 * (j - first)
            here = rows[:, at].reshape(count, channels).T.astype(bf16)
            paired[j] = half_dot(here, both).astype(bf16).astype(f32)
            here = rows[:, at + 1].reshape(count, channels).T.astype(bf16)
            grad_edge[j] = half_dot(here, target).astype(bf16)
    copy = pltpu.make_async_copy(grad_edge, part_of(spill, EDGE_PART), out_sem.at[0])
    copy.start()
    for l in range(LMAX + 1):
        for k in ROWS_OF[l]:
            acc = None
            for j in COEFS_OF[l]:
                term = wide[j, k : k + 1, :] * paired[j]
                acc = term if acc is None else acc + term
            z[k] = acc.astype(bf16)
    zero_copy = pltpu.make_async_copy(
        z.at[pl.ds(0, LMAX + 1)], part_of(spill, ZERO_PART), out_sem.at[1]
    )
    zero_copy.start()
    copy.wait()
    zero_copy.wait()
    half_copy.wait()


def forward_kernel(
    places,
    group,
    first,
    ids,
    z,
    wigner,
    spill_in,
    attention_t,
    maps_in,
    other,
    spill,
    maps,
    stats,
    sent,
    scalar,
    per_edge,
    held,
    y,
    wide,
    norm,
    msg,
    heads_acc,
    grad_edge,
    sems,
    out_sem,
):
    channels, edges = LANES, wigner.shape[2]
    heads = attention_t.shape[0]
    count = stats.shape[1] // 2
    mine = maps_in.at[2]
    start_weights(places, first[0, 0], mine, other, held, sems)
    edge_copy = pltpu.make_async_copy(part_of(spill_in, EDGE_PART), grad_edge, out_sem.at[1])
    edge_copy.start()
    wide[...] = wigner[...].astype(f32)
    base, rows = ZERO
    acc = None
    wait_weights(places, (0,), mine, held, sems)
    for tiles in pairs(rows):
        right = z[tiles[0] : tiles[-1] + 1].reshape(-1, edges)
        term = half_dot(map_tiles(held, places[0], tiles), right)
        acc = term if acc is None else acc + term
    spread(acc, held, places[0][2], base, y)
    for (base, rows), real, imag in ((ONE, places[1], places[2]), (TWO, places[3], places[4])):
        wait_weights(places, (1, 2) if base == ONE[0] else (3, 4), mine, held, sems)
        acc = None
        for tiles in pairs(rows):
            lo, hi = base + tiles[0], base + tiles[-1] + 1
            plus = z[lo:hi].reshape(-1, edges)
            minus = z[lo + rows : hi + rows].reshape(-1, edges)
            term = half_dot(map_tiles(held, real, tiles), jnp.concatenate([plus, minus], axis=1))
            term = term + half_dot(
                map_tiles(held, imag, tiles), jnp.concatenate([-minus, plus], axis=1)
            )
            acc = term if acc is None else acc + term
        spread(acc[:, :edges], held, real[2], base * channels, y)
        spread(acc[:, edges:], held, real[2], (base + rows) * channels, y)
    maps_copy = pltpu.make_async_copy(held, maps.at[pl.ds(0, 2)], out_sem.at[2])
    maps_copy.start()
    value = y[:channels, :]
    scalar[...] = value
    y[...] = y[...].astype(bf16).astype(f32)
    gating = (value / (1.0 + jnp.exp(-value))).astype(bf16)
    logits = half_dot(attention_t[...], gating)
    weight = jnp.where(ids[2:3, :] > 0, jnp.exp(logits), 0.0)
    target = hot_rows(ids[1:2, :], count)
    own_sum = nt_full(weight, target)
    at_edges = full_dot(own_sum, target)
    own_norm = weight / jnp.where(at_edges > 0.0, at_edges, 1.0)
    norm[...] = widen(own_norm, channels)

    def body(start):
        at = pl.ds(start, CHUNK)
        own = norm[at, :]
        total = jnp.zeros((CHUNK, edges), f32)
        for l in range(LMAX + 1):
            for j in COEFS_OF[l]:
                acc = None
                for k in ROWS_OF[l]:
                    term = wide[j, k : k + 1, :] * y[rows_at(k, start), :]
                    acc = term if acc is None else acc + term
                total = total + acc * grad_edge[j, at, :].astype(f32)
                msg[j, at, :] = (acc * own).astype(bf16)
        heads_acc[at, :] = total

    edge_copy.wait()
    chunks(channels, body)
    copy = pltpu.make_async_copy(msg, part_of(spill, MESSAGE_PART), out_sem.at[0])
    copy.start()
    grad_norm = jnp.sum(heads_acc[...].reshape(heads, channels // heads, edges), axis=1)
    own_shared = nt_full(own_norm * grad_norm, target)
    sums = jnp.concatenate([own_sum, own_shared], axis=1)
    stats[...] = sums
    for owner in range(group):
        sent[owner] = sums
    per_edge[:heads, :] = own_norm
    per_edge[heads:, :] = grad_norm
    copy.wait()
    maps_copy.wait()


def backward_kernel(
    first,
    ids,
    stats,
    every,
    scalar,
    per_edge,
    wigner,
    spill_in,
    attention,
    attention_t,
    spill,
    mine,
    theirs,
    wide,
    norm,
    grad,
    turned,
    grad_conv,
    grad_edge,
    z,
    out_sem,
):
    channels, edges = LANES, wigner.shape[2]
    heads = attention_t.shape[0]
    count = stats.shape[1] // 2
    edge_copy = pltpu.make_async_copy(part_of(spill_in, EDGE_PART), grad_edge, out_sem.at[1])
    edge_copy.start()
    zero_copy = pltpu.make_async_copy(part_of(spill_in, ZERO_PART), z, out_sem.at[2])
    zero_copy.start()
    wide[...] = wigner[...].astype(f32)
    total = jnp.sum(every[:, :, :count], axis=0)
    total = jnp.where(total > 0.0, total, 1.0)
    shares = every[:, :, :count] / total[None]
    shared = jnp.sum(shares * every[:, :, count:], axis=0)
    own_share = stats[:, :count] / total
    target = hot_rows(ids[1:2, :], count)
    normalized = per_edge[:heads, :] * full_dot(own_share, target)
    grad_logit = normalized * (per_edge[heads:, :] - full_dot(shared, target))
    value = scalar[...]
    sigmoid = 1.0 / (1.0 + jnp.exp(-value))
    gating = (value / (1.0 + jnp.exp(-value))).astype(bf16).astype(f32)
    att = nt_full(grad_logit, gating)
    grad_gating = full_dot(attention[...].astype(f32), grad_logit)
    grad_scalar = grad_gating * sigmoid * (1.0 + value * (1.0 - sigmoid))
    norm[...] = widen(normalized, channels)

    def body(start):
        at = pl.ds(start, CHUNK)
        own = norm[at, :]
        for l in range(LMAX + 1):
            fields = [
                (grad_edge[j, at, :].astype(f32) * own).astype(bf16).astype(f32)
                for j in COEFS_OF[l]
            ]
            for k in ROWS_OF[l]:
                acc = None
                for j, field in zip(COEFS_OF[l], fields):
                    term = wide[j, k : k + 1, :] * field
                    acc = term if acc is None else acc + term
                grad[rows_at(k, start), :] = acc

    edge_copy.wait()
    chunks(channels, body)
    grad[:channels, :] = grad[:channels, :] + grad_scalar
    depth = (LMAX + 1) * channels
    parts, share = mine.shape[0], depth // (2 * mine.shape[0])
    grad_conv[...] = grad[...].astype(bf16).reshape(grad_conv.shape)
    copy = pltpu.make_async_copy(grad_conv, part_of(spill, CONV_PART), out_sem.at[0])
    copy.start()
    zero_copy.wait()
    turned[:depth, :] = nt_dot(
        grad_conv[: LMAX + 1].reshape(depth, edges), z[...].reshape(depth, edges)
    )
    turned[depth:, :] = jnp.zeros((turned.shape[0] - depth, depth), f32)
    padded = mine.shape[1]
    tail_row = lax.broadcasted_iota(jnp.int32, (padded, depth), 0)
    one = jnp.concatenate([att[h : h + 1, :] for h in range(LMAX + 1)], axis=1)
    two = [att[h : h + 1, :] for h in range(LMAX + 1, heads)]
    two = jnp.concatenate(two + [jnp.zeros((1, depth - len(two) * channels), f32)], axis=1)

    def store(outs):
        for core in range(2):
            for part in range(parts):
                at = (2 * part + core) * share
                block = turned[at : at + padded, :]
                block = jnp.where(tail_row == share, one, block)
                block = jnp.where(tail_row == share + 1, two, block)
                outs[core][part] = block.astype(bf16)

    @pl.when(first[0, 0] == 0)
    def _():
        store((mine, theirs))

    @pl.when(first[0, 0] != 0)
    def _():
        store((theirs, mine))

    copy.wait()


def scatter_kernel(
    places,
    group,
    own,
    ids,
    spill,
    wigner,
    maps,
    spill_out,
    held,
    wide,
    dz,
    gp,
    grad,
    grad_rows,
    grads,
    grad_conv,
    sems,
    out_sem,
):
    channels, edges = LANES, wigner.shape[2]
    count = own * group
    conv_copy = pltpu.make_async_copy(part_of(spill, CONV_PART), grad_conv, out_sem.at[1])
    conv_copy.start()
    mine = maps.at[0]
    start_weights(places, None, mine, maps.at[1], held, sems)
    wide[...] = wigner[...].astype(f32)
    conv_copy.wait()
    grad[...] = grad_conv[...].astype(f32).reshape(grad.shape)
    zs = held.shape[1]
    for base, rows in (ZERO, ONE, (ONE[0] + ONE[1], ONE[1]), TWO, (TWO[0] + TWO[1], TWO[1])):
        size = rows * channels // (2 * zs)
        blocks = []
        for zz in range(zs):
            for xh in range(2):
                at = base * channels + (xh * zs + zz) * size
                blocks.append(grad[at : at + size, :])
        ordered = jnp.concatenate(blocks, axis=0)
        for t in range(rows):
            at = slice(t * channels, (t + 1) * channels)
            to = (base + t) * channels
            grad_rows[:, to : to + channels] = ordered[at, :].T.astype(bf16)
    base, rows = ZERO
    left = grad_rows[:, : rows * channels]
    wait_weights(places, (0,), mine, held, sems)
    for tiles in pairs(rows):
        out = half_dot(left, map_tiles(held, places[0], tiles)).astype(bf16).astype(f32)
        for i, t in enumerate(tiles):
            dz[t] = out[:, i * channels : (i + 1) * channels].T
    for (base, rows), real, imag in ((ONE, places[1], places[2]), (TWO, places[3], places[4])):
        wait_weights(places, (1, 2) if base == ONE[0] else (3, 4), mine, held, sems)
        plus = grad_rows[:, base * channels : (base + rows) * channels]
        minus = grad_rows[:, (base + rows) * channels : (base + 2 * rows) * channels]
        left = jnp.concatenate([plus, minus], axis=0)
        crossed = jnp.concatenate([minus, -plus], axis=0)
        for tiles in pairs(rows):
            out = half_dot(left, map_tiles(held, real, tiles))
            out = out + half_dot(crossed, map_tiles(held, imag, tiles))
            out = out.astype(bf16).astype(f32)
            for i, t in enumerate(tiles):
                at = slice(i * channels, (i + 1) * channels)
                dz[base + t] = out[:edges, at].T
                dz[base + rows + t] = out[edges:, at].T

    def body(start):
        at = pl.ds(start, CHUNK)
        for l in range(LMAX + 1):
            for j in COEFS_OF[l]:
                acc = None
                for k in ROWS_OF[l]:
                    term = wide[j, k : k + 1, :] * dz[k, at, :]
                    acc = term if acc is None else acc + term
                gp[j, at, :] = acc.astype(bf16)

    chunks(channels, body)
    both = (hot_rows(ids[1:2, :], count) + hot_rows(ids[0:1, :], count)).astype(bf16)
    by_owner(both, gp, grads, group, split=True)
    copy = pltpu.make_async_copy(
        grads, part_of(spill_out, (SUM_START, grads.shape[0])), out_sem.at[0]
    )
    copy.start()
    copy.wait()


def node_rows(own):
    return -(-COEF * own // 16) * 16


def one_hot(rows, columns, shift, low, high):
    row = lax.broadcasted_iota(jnp.int32, (rows, columns), 0)
    column = lax.broadcasted_iota(jnp.int32, (rows, columns), 1)
    return ((column == row + shift) & (row >= low) & (row < high)).astype(bf16)


def tail_kernel(used, share, heads, parts, spill, grads, total, att, sems):
    count, depth = parts.shape[0], parts.shape[2]
    group = grads.shape[0]
    inner, skip = depth // group, used % 16
    base, rows = used - skip, grads.shape[1] - (used - skip)
    low_copy = pltpu.make_async_copy(
        spill.at[pl.ds(SUM_START, group)], grads.at[:, pl.ds(0, LANES), :], sems.at[0]
    )
    high_copy = pltpu.make_async_copy(
        spill.at[pl.ds(SUM_START + group, group), pl.ds(0, base + 16 - LANES), :],
        grads.at[:, pl.ds(LANES, base + 16 - LANES), :],
        sems.at[1],
    )
    low_copy.start()
    high_copy.start()
    acc = parts[0].astype(f32)
    for p in range(1, count):
        acc = acc + parts[p].astype(f32)
    total[...] = acc
    for h in range(heads):
        row, at = share + h // (depth // LANES), h % (depth // LANES) * LANES
        att[h : h + 1, :] = total[row : row + 1, at : at + LANES]
    low = att[...].astype(bf16)
    half = LANES // 2
    left = half_dot(low, one_hot(LANES, LANES, half, 0, half)).astype(bf16)
    right = half_dot(low, one_hot(LANES, LANES, 0, half, LANES)).astype(bf16)
    row = lax.broadcasted_iota(jnp.int32, (rows, heads), 0)
    head = lax.broadcasted_iota(jnp.int32, (rows, heads), 1)
    tail = half_dot((row == head + skip).astype(bf16), left)
    tail = tail + half_dot((row == head + skip + heads).astype(bf16), right)
    moved = half_dot(one_hot(rows, total.shape[0], -skip, skip, skip + share), acc.astype(bf16))
    moved = moved.astype(bf16)
    kept = lax.broadcasted_iota(jnp.int32, (rows, LANES), 0) < skip
    low_copy.wait()
    high_copy.wait()
    for g in range(group):
        first = g * inner // LANES * LANES
        last = -(-(g + 1) * inner // LANES) * LANES
        shift = g * inner - first
        place = one_hot(last - first, LANES, -shift, shift, shift + inner)
        piece = half_dot(moved[:, first:last], place) + tail
        before = grads[g, base : base + 16, :].astype(f32)
        if rows > 16:
            before = jnp.concatenate([before, jnp.zeros((rows - 16, LANES), f32)], axis=0)
        grads[g, base:, :] = jnp.where(kept, before, piece).astype(bf16)


def last_kernel(scale, parts, nodes, zero, att, total):
    acc = parts[0].astype(f32)
    for g in range(1, parts.shape[0]):
        acc = acc + parts[g].astype(f32)
    total[...] = acc
    used = nodes.shape[0] * nodes.shape[1]
    heads, half = att.shape[0], LANES // 2
    nodes[...] = acc[:used].astype(bf16).reshape(nodes.shape)
    zero[...] = total[used : used + zero.shape[0], :][:, : zero.shape[1]] * scale
    left = full_dot(
        total[used : used + heads, :], one_hot(LANES, LANES, -half, half, LANES).astype(f32)
    )
    lane = lax.broadcasted_iota(jnp.int32, (heads, LANES), 1)
    right = jnp.where(lane >= half, total[used + heads : used + 2 * heads, :], 0.0)
    att[...] = (left + right) * scale


def sum_kernel(parts, nodes, tail, total):
    acc = parts[0].astype(f32)
    for g in range(1, parts.shape[0]):
        acc = acc + parts[g].astype(f32)
    total[...] = acc
    used = nodes.shape[0] * nodes.shape[1]
    nodes[...] = acc[:used].astype(bf16).reshape(nodes.shape)
    tail[...] = total[used : used + tail.shape[0], :]


def pad_to(block, rows, columns):
    return jnp.pad(block, ((0, rows - block.shape[0]), (0, columns - block.shape[1])))


def whole_lanes(count):
    return -(-count // LANES) * LANES


def gather_weights(shards):
    rows = [w.shape[0] for w in shards]
    columns = [w.shape[1] for w in shards]
    most = -(-max(columns) // 16) * 16
    sets = ((0, 1), (2, 3, 4))
    lanes = whole_lanes(max(sum(rows[i] for i in s) for s in sets))
    starts = [0] * len(shards)
    for half_index, s in enumerate(sets):
        for n, i in enumerate(s):
            starts[i] = half_index * lanes + sum(rows[j] for j in s[:n])
    packed = pl.pallas_call(
        functools.partial(pack_kernel, starts),
        out_shape=jax.ShapeDtypeStruct((most, 2 * lanes), bf16),
        in_specs=[HBM] * len(shards),
        out_specs=VMEM,
        scratch_shapes=[pltpu.VMEM(w.shape[::-1], bf16) for w in shards]
        + [pltpu.VMEM((most, 2 * lanes), f32), pltpu.SemaphoreType.DMA((len(shards),))],
        compiler_params=WHOLE,
    )(*[w.T for w in shards])
    core = lax.axis_index("core")
    near = lax.all_gather(packed, "core")
    sent = lax.dynamic_slice_in_dim(near, core * lanes, lanes, axis=2)
    slabs = gather(sent.reshape(2 * most, lanes), ROW_GROUP)
    group = slabs.shape[0] // 2
    places = [None] * len(shards)
    depth = 0
    for half_index, s in enumerate(sets):
        at = 0
        for i in s:
            tiles = group * rows[i] // LANES
            places[i] = (half_index, at, 4 * columns[i], tiles)
            at += tiles * 4 * columns[i]
        depth = max(depth, at)
    kinds = [[(rows[i], columns[i], starts[i] - n * lanes) for i in s] for n, s in enumerate(sets)]
    tiled = pl.pallas_call(
        functools.partial(slab_kernel, kinds),
        out_shape=jax.ShapeDtypeStruct((depth, LANES), bf16),
        in_specs=[pl.BlockSpec(memory_space=pltpu.SMEM), VMEM],
        out_specs=VMEM,
        compiler_params=SMALL,
    )(core.astype(jnp.int32).reshape(1, 1), slabs)
    return lax.all_gather(tiled, "z"), places, tiled


def on_device(
    embeddings,
    atom_counts,
    edge_counts,
    source,
    target,
    wigner,
    cotangent,
    w_zero,
    w_one_real,
    w_one_imag,
    w_two_real,
    w_two_imag,
    attention,
):
    half, places, tiled = gather_weights((w_zero, w_one_real, w_one_imag, w_two_real, w_two_imag))
    row_count = embeddings.shape[1]
    harmonics = embeddings.shape[2]
    channels = embeddings.shape[3]
    width = harmonics * channels
    edge_rows = source.shape[1]
    head_count = attention.shape[1]
    group = lax.axis_size(GRAPH)
    all_nodes = row_count * group
    rotation = jnp.transpose(wigner[0], (1, 0, 2))
    in_use = (lax.iota(jnp.int32, edge_rows) < edge_counts[0, 0]).astype(jnp.int32)
    ids = jnp.stack([source[0], target[0], in_use] + [jnp.zeros_like(in_use)] * 5)
    attention_t = attention.T
    core = lax.axis_index("core")
    first = core.astype(jnp.int32).reshape(1, 1)
    own_first = lax.axis_index(GRAPH) * row_count
    present = ((own_first + lax.iota(jnp.int32, row_count)) < atom_counts[0])[:, None]
    cot_rows = jnp.where(present[:, :, None], cotangent[0], 0.0).astype(bf16)
    own_rows = jnp.stack([embeddings[0], cot_rows])
    own_rows = jnp.transpose(own_rows, (2, 0, 1, 3)).reshape(-1, channels)
    own_rows = pad_to(own_rows, -(-own_rows.shape[0] // 16) * 16, channels)
    own_rows, tiled = lax.optimization_barrier((own_rows, tiled))
    nodes = gather(own_rows, GRAPH)
    half, nodes = lax.optimization_barrier((half, nodes))
    other = lax.ppermute(half, "core", [(0, 1), (1, 0)])

    smem = pl.BlockSpec(memory_space=pltpu.SMEM)
    field = (channels, edge_rows)
    wide = pltpu.VMEM(rotation.shape, f32)
    maps_shape = jax.ShapeDtypeStruct((MAP_SLOTS,) + half.shape, bf16)
    spill_shape = jax.ShapeDtypeStruct((SPILL,) + field, bf16)
    out_copy = pltpu.SemaphoreType.DMA((1,))
    two_copies = pltpu.SemaphoreType.DMA((2,))
    edge_field = pltpu.VMEM((COEF,) + field, bf16)
    z, spill, maps = pl.pallas_call(
        functools.partial(rotate_kernel, row_count),
        out_shape=(
            jax.ShapeDtypeStruct((REDUCED,) + field, bf16),
            spill_shape,
            maps_shape,
        ),
        in_specs=[VMEM] * 3 + [HBM],
        out_specs=[VMEM, HBM, HBM],
        scratch_shapes=[
            pltpu.VMEM((COEF,) + field, f32),
            wide,
            edge_field,
            pltpu.SemaphoreType.DMA((3,)),
        ],
        compiler_params=LARGE,
    )(ids, nodes, rotation, half)
    held = pltpu.VMEM((2,) + half.shape, bf16)
    copies = pltpu.SemaphoreType.DMA((len(places),))

    span = node_rows(row_count)
    sums = (head_count, 2 * all_nodes)
    spill, maps, stats, sent, scalar, per_edge = pl.pallas_call(
        functools.partial(forward_kernel, places, group),
        out_shape=(
            spill_shape,
            maps_shape,
            jax.ShapeDtypeStruct(sums, f32),
            jax.ShapeDtypeStruct((group,) + sums, f32),
            jax.ShapeDtypeStruct(field, f32),
            jax.ShapeDtypeStruct((2 * head_count, edge_rows), f32),
        ),
        in_specs=[smem] + [VMEM] * 3 + [HBM, VMEM] + [HBM] * 2,
        out_specs=[HBM] * 2 + [VMEM] * 4,
        scratch_shapes=[
            held,
            pltpu.VMEM((REDUCED * channels, edge_rows), f32),
            wide,
            pltpu.VMEM(field, f32),
            pltpu.VMEM((COEF,) + field, bf16),
            pltpu.VMEM(field, f32),
            edge_field,
            copies,
            pltpu.SemaphoreType.DMA((3,)),
        ],
        input_output_aliases={4: 0, 6: 1},
        compiler_params=LARGE,
    )(first, ids, z, rotation, spill, attention_t, maps, other)
    every = exchange(sent, GRAPH)

    columns = lax.axis_size(COLUMN_GROUP)
    depth = channels * (LMAX + 1)
    share = depth // (2 * columns)
    padded = -(-(share + 2) // 16) * 16
    partial = jax.ShapeDtypeStruct((columns, padded, depth), bf16)
    spill, mine, theirs = pl.pallas_call(
        backward_kernel,
        out_shape=(
            spill_shape,
            partial,
            partial,
        ),
        in_specs=[smem] + [VMEM] * 6 + [HBM] + [VMEM] * 2,
        out_specs=[HBM] + [VMEM] * 2,
        scratch_shapes=[
            wide,
            pltpu.VMEM(field, f32),
            pltpu.VMEM((REDUCED * channels, edge_rows), f32),
            pltpu.VMEM((depth + padded, depth), f32),
            pltpu.VMEM((REDUCED,) + field, bf16),
            edge_field,
            pltpu.VMEM((LMAX + 1,) + field, bf16),
            pltpu.SemaphoreType.DMA((3,)),
        ],
        input_output_aliases={7: 0},
        compiler_params=LARGE,
    )(first, ids, stats, every, scalar, per_edge, rotation, spill, attention, attention_t)

    theirs = lax.ppermute(theirs, "core", [(0, 1), (1, 0)])
    mine = (mine.astype(f32) + theirs.astype(f32)).astype(bf16)
    mine, spill = lax.optimization_barrier((mine, spill))
    zero_parts = exchange(mine, COLUMN_GROUP)
    message_sums = pl.pallas_call(
        message_kernel,
        out_shape=jax.ShapeDtypeStruct((group, span, channels), bf16),
        in_specs=[VMEM] * 3 + [HBM],
        out_specs=VMEM,
        scratch_shapes=[edge_field, out_copy],
        compiler_params=LARGE,
    )(ids, stats, every, spill)
    message_sums, spill = lax.optimization_barrier((message_sums, spill))
    message_sums = message_sums.reshape(group // 2, 2 * span, channels)
    near_sums = lax.psum_scatter(message_sums, "y", scatter_dimension=0, tiled=True)
    near_sums = near_sums.reshape(2, span, channels)
    side = lax.axis_index("xl")
    kept = lax.dynamic_index_in_dim(near_sums, side, keepdims=False)
    passed = lax.dynamic_index_in_dim(near_sums, 1 - side, keepdims=False)
    passed = lax.ppermute(passed, "xl", [(0, 1), (1, 0)])
    summed = kept.astype(f32) + passed.astype(f32)
    used = harmonics * row_count
    inner = depth // group
    lanes = whole_lanes(inner)
    beside = lanes - inner >= channels // 2 and lanes == channels and share >= 2 * head_count
    tail_rows = share if beside else share * lanes // LANES + head_count
    spill = pl.pallas_call(
        functools.partial(scatter_kernel, places, group, row_count),
        out_shape=spill_shape,
        in_specs=[VMEM, HBM, VMEM, HBM],
        out_specs=HBM,
        scratch_shapes=[
            held,
            wide,
            pltpu.VMEM((REDUCED,) + field, f32),
            pltpu.VMEM((COEF,) + field, bf16),
            pltpu.VMEM((REDUCED * channels, edge_rows), f32),
            pltpu.VMEM((edge_rows, REDUCED * channels), bf16),
            pltpu.VMEM((2 * group, channels, channels), bf16),
            pltpu.VMEM((REDUCED,) + field, bf16),
            copies,
            two_copies,
        ],
        input_output_aliases={1: 0},
        compiler_params=LARGE,
    )(ids, spill, rotation, maps)
    sums_shape = (group, -(-(used + tail_rows) // 16) * 16, channels)
    nodes_shape = jax.ShapeDtypeStruct((harmonics, row_count, channels), bf16)
    batch_scale = 1.0 / (2 * columns)
    if beside:
        grad_sums = pl.pallas_call(
            functools.partial(tail_kernel, used, share, head_count),
            out_shape=jax.ShapeDtypeStruct(sums_shape, bf16),
            in_specs=[VMEM, HBM],
            out_specs=VMEM,
            scratch_shapes=[
                pltpu.VMEM((padded, depth), f32),
                pltpu.VMEM((head_count, channels), f32),
                two_copies,
            ],
            compiler_params=LARGE,
        )(zero_parts, spill)
        last = exchange(grad_sums, GRAPH)
        grad_nodes, grad_zero, grad_att = pl.pallas_call(
            functools.partial(last_kernel, batch_scale),
            out_shape=(
                nodes_shape,
                jax.ShapeDtypeStruct((share, inner), f32),
                jax.ShapeDtypeStruct((head_count, channels), f32),
            ),
            in_specs=[VMEM],
            out_specs=[VMEM] * 3,
            scratch_shapes=[pltpu.VMEM(last.shape[1:], f32)],
            compiler_params=SMALL,
        )(last)
        grad_zero, grad_att = grad_zero.T, grad_att.T
    else:
        zero_sum = jnp.sum(zero_parts.astype(f32), axis=0)
        att = zero_sum[share : share + 2].reshape(-1)[: head_count * channels]
        zero_send = jnp.transpose(zero_sum[:share].reshape(share, group, inner), (1, 0, 2))
        zero_send = jnp.pad(zero_send, ((0, 0), (0, 0), (0, lanes - inner)))
        zero_send = zero_send.reshape(group, share * lanes // LANES, LANES)
        att = jnp.broadcast_to(
            att.reshape(1, head_count, channels), (group, head_count, channels)
        )
        last_rows = jnp.concatenate([zero_send, att], axis=1).astype(bf16)
        grad_sums = spill[SUM_START : SUM_START + 2 * group].reshape(2, group, channels, channels)
        grad_sums = jnp.transpose(grad_sums, (1, 0, 2, 3)).reshape(group, 2 * channels, channels)
        rest = jnp.zeros(sums_shape, bf16)
        grad_sums = lax.dynamic_update_slice(rest, grad_sums[:, :used], (0, 0, 0))
        grad_sums = lax.dynamic_update_slice(grad_sums, last_rows, (0, used, 0))
        last = exchange(grad_sums, GRAPH)
        grad_nodes, tail = pl.pallas_call(
            sum_kernel,
            out_shape=(nodes_shape, jax.ShapeDtypeStruct((tail_rows, channels), f32)),
            in_specs=[VMEM],
            out_specs=[VMEM] * 2,
            scratch_shapes=[pltpu.VMEM(last.shape[1:], f32)],
            compiler_params=SMALL,
        )(last)
        tail = tail * batch_scale
        zero_rows = share * lanes // LANES
        grad_zero = tail[:zero_rows].reshape(share, lanes)[:, :inner].T
        grad_att = tail[zero_rows:].T
    update = summed[:used].reshape(harmonics, row_count, channels)
    update = jnp.transpose(jnp.where(present[None], update, 0.0).astype(bf16), (1, 0, 2))
    grad_nodes = jnp.transpose(grad_nodes, (1, 0, 2))

    shape = (1, row_count, harmonics, channels)
    return (update.reshape(shape), grad_nodes.reshape(shape), grad_zero, grad_att)


def solution(mesh):
    columns, group = mesh.shape["dp"], mesh.shape["graph"]
    devices = mesh.devices.reshape(2, columns // 4, 2, group // 2, 2)
    fine = Mesh(devices, DP + GRAPH)
    in_specs = (
        P(DP, GRAPH, None, None),
        P(DP),
        P(DP, GRAPH),
        P(DP, GRAPH),
        P(DP, GRAPH),
        P(DP, None, None, GRAPH),
        P(DP, GRAPH, None, None),
        P(GRAPH, DP),
        P(GRAPH, DP),
        P(GRAPH, DP),
        P(GRAPH, DP),
        P(GRAPH, DP),
        P(),
    )
    out_specs = (P(DP, GRAPH, None, None), P(DP, GRAPH, None, None), P(GRAPH, DP), P())
    return jax.shard_map(
        on_device, mesh=fine, in_specs=in_specs, out_specs=out_specs, check_vma=False
    )
```

```python
import functools

import jax
import jax.numpy as jnp
from jax import lax
from jax.experimental import pallas as pl
from jax.experimental.pallas import tpu as pltpu
from jax.sharding import Mesh, PartitionSpec as P

LMAX = 6
LANES = 128
DP = ("xh", "z", "core")
COLUMN_GROUP = ("xh", "z")
ROW_GROUP = ("xh", "y", "xl")
GRAPH = ("y", "xl")
precise = lax.Precision.HIGHEST
f32 = jnp.float32
bf16 = jnp.bfloat16


def half_dot(left, right):
    return jnp.dot(left, right, preferred_element_type=f32)


def full_dot(left, right):
    return jnp.dot(left, right, precision=precise, preferred_element_type=f32)


def gather(block, axes):
    count = lax.axis_size(axes)
    copies = jnp.broadcast_to(block[None], (count,) + block.shape)
    return lax.all_to_all(copies, axes, split_axis=0, concat_axis=0, tiled=True)


def exchange(blocks, axes):
    return lax.all_to_all(blocks, axes, split_axis=0, concat_axis=0, tiled=True)


ROW_DEGREE = (
    list(range(LMAX + 1)) + list(range(1, LMAX + 1)) * 2 + list(range(2, LMAX + 1)) * 2
)
ROWS_OF = [[k for k, d in enumerate(ROW_DEGREE) if d == l] for l in range(LMAX + 1)]
COEFS_OF = [list(range(l * l, (l + 1) * (l + 1))) for l in range(LMAX + 1)]
REDUCED = len(ROW_DEGREE)
COEF = (LMAX + 1) ** 2
ZERO = (0, LMAX + 1)
ONE = (LMAX + 1, LMAX)
TWO = (3 * LMAX + 1, LMAX - 1)
CHUNK = 32
VMEM = pl.BlockSpec(memory_space=pltpu.VMEM)
HBM = pl.BlockSpec(memory_space=pltpu.HBM)
SMALL = pltpu.CompilerParams(vmem_limit_bytes=28 * 1024 * 1024)
LARGE = pltpu.CompilerParams(vmem_limit_bytes=48 * 1024 * 1024)
WHOLE = pltpu.CompilerParams(vmem_limit_bytes=60 * 1024 * 1024)
EDGE_PART = (0, COEF)
MESSAGE_PART = (COEF, COEF)
CONV_PART = (2 * COEF, REDUCED)
ZERO_PART = (2 * COEF + REDUCED, LMAX + 1)
SUM_START = 2 * COEF + REDUCED + LMAX + 1
SPILL = 600
MAP_SLOTS = 7


def nt_dot(left, right):
    return lax.dot_general(left, right, (((1,), (1,)), ((), ())), preferred_element_type=f32)


def nt_full(left, right):
    return lax.dot_general(
        left, right, (((1,), (1,)), ((), ())), precision=precise, preferred_element_type=f32
    )


def in_terms(values):
    parts, rest = [], values
    for _ in range(3):
        low = rest.astype(bf16).astype(f32)
        parts.append(low)
        rest = rest - low
    return jnp.concatenate(parts, axis=0).astype(bf16)


def of_terms(stacked):
    rows = stacked.shape[0] // 3
    return stacked[:rows] + stacked[rows : 2 * rows] + stacked[2 * rows :]


def hot_rows(ids, count):
    rows = lax.broadcasted_iota(jnp.int32, (count, ids.shape[1]), 0)
    return (rows == ids).astype(f32)


def widen(values, channels):
    heads, edges = values.shape
    wide = jnp.broadcast_to(values[:, None, :], (heads, channels // heads, edges))
    return wide.reshape(channels, edges)


def part_of(spill, part):
    return spill.at[pl.ds(part[0], part[1])]


def chunks(channels, body):
    def step(i, carry):
        body(pl.multiple_of(i * CHUNK, CHUNK))
        return carry

    lax.fori_loop(0, channels // CHUNK, step, 0)


def rows_at(k, start):
    return pl.ds(pl.multiple_of(k * LANES + start, CHUNK), CHUNK)


def start_weights(places, first, mine, other, held, sems):
    def go(halves):
        for i, (half, at, rows, tiles) in enumerate(places):
            span = pl.ds(at, tiles * rows)
            pltpu.make_async_copy(
                halves[half].at[:, span, :], held.at[half, :, span, :], sems.at[i]
            ).start()

    if first is None:
        return go((mine, other))

    @pl.when(first == 0)
    def _():
        go((mine, other))

    @pl.when(first != 0)
    def _():
        go((other, mine))


def wait_weights(places, which, mine, held, sems):
    for i in which:
        half, at, rows, tiles = places[i]
        span = pl.ds(at, tiles * rows)
        pltpu.make_async_copy(mine.at[:, span, :], held.at[half, :, span, :], sems.at[i]).wait()


def map_tiles(held, place, tiles):
    half, at, rows, _ = place
    parts = []
    for t in tiles:
        part = held[half, :, at + t * rows : at + (t + 1) * rows, :]
        parts.append(part.reshape(-1, LANES))
    return parts[0] if len(parts) == 1 else jnp.concatenate(parts, axis=1)


def pairs(count):
    return [tuple(range(i, min(i + 2, count))) for i in range(0, count, 2)]


def spread(blocks, held, rows, base, out):
    zs = held.shape[1]
    size = rows // 2
    for z in range(zs):
        for xh in range(2):
            to = base + (xh * zs + z) * size
            at = (z * 2 + xh) * size
            out[to : to + size, :] = blocks[at : at + size, :]


def by_owner(target, turned, out, group, scale=None, split=False):
    channels = turned.shape[1]
    own = target.shape[0] // group
    per = 16 // own
    for first in range(0, COEF, per):
        parts = []
        for j in range(first, first + per):
            if j < COEF:
                part = nt_dot(target, turned[j])
                part = part if scale is None else part * scale
            else:
                part = jnp.zeros((target.shape[0], channels), f32)
            parts.append(part.reshape(group, 1, own, channels))
        block = jnp.concatenate(parts, axis=1).reshape(group, 16, channels)
        at = first * own
        if split:
            half, at = at // LANES * group, at % LANES
            out[half : half + group, at : at + 16, :] = block.astype(bf16)
        else:
            out[:, at : at + 16, :] = block.astype(bf16)


def pack_kernel(places, *refs):
    count = len(places)
    shards, out = refs[:count], refs[count]
    held, acc, sems = refs[count + 1 : -2], refs[-2], refs[-1]
    copies = [pltpu.make_async_copy(shards[i], held[i], sems.at[i]) for i in range(count)]
    for copy in copies:
        copy.start()
    acc[...] = jnp.zeros_like(acc)
    for copy, shard, at in zip(copies, held, places):
        columns, rows = shard.shape
        lane = lax.broadcasted_iota(jnp.int32, (rows, acc.shape[1]), 1)
        row = lax.broadcasted_iota(jnp.int32, (rows, acc.shape[1]), 0)
        place = (lane == row + at).astype(bf16)
        copy.wait()
        acc[:columns, :] += half_dot(shard[...], place)
    out[...] = acc[...].astype(bf16)


def slab_kernel(sets, first, slabs, out):
    group, most, lanes = slabs.shape[0] // 2, slabs.shape[1] // 2, slabs.shape[2]
    blocks = [jnp.concatenate([slabs[g], slabs[group + g]], axis=0) for g in range(group)]

    def rolled(which):
        wide = [block.astype(f32) for block in blocks]
        lane = lax.broadcasted_iota(jnp.int32, wide[0].shape, 1)
        to = 0
        for rows, columns, at in which:
            size = 4 * columns
            row = lax.broadcasted_iota(jnp.int32, (size, 4 * most), 0)
            column = lax.broadcasted_iota(jnp.int32, (size, 4 * most), 1)
            chosen = (column == row // columns * most + row % columns).astype(bf16)
            tiles = [None] * (group * rows // LANES)
            for g in range(group):
                t, off = divmod(g * rows, LANES)
                shift = (off - at) % LANES
                moved = pltpu.roll(wide[g], shift, 1) if shift else wide[g]
                tiles[t] = moved if tiles[t] is None else jnp.where(lane >= off, moved, tiles[t])
                if off + rows > LANES:
                    tiles[t + 1] = moved
            for t in range(0, len(tiles), 2):
                pair = jnp.concatenate([tile.astype(bf16) for tile in tiles[t : t + 2]], axis=1)
                pair = half_dot(chosen, pair).astype(bf16)
                for i in range(len(tiles[t : t + 2])):
                    out[to : to + size, :] = pair[:, i * LANES : (i + 1) * LANES]
                    to += size
        if to < out.shape[0]:
            out[to:, :] = jnp.zeros((out.shape[0] - to, LANES), bf16)

    def lay(which):
        if lanes == LANES:
            return rolled(which)
        to = 0
        for rows, columns, at in which:
            size = 4 * columns
            row = lax.broadcasted_iota(jnp.int32, (size, 4 * most), 0)
            lane = lax.broadcasted_iota(jnp.int32, (size, 4 * most), 1)
            kept = row // columns * most + row % columns
            chosen = (lane == kept).astype(bf16)
            source = lax.broadcasted_iota(jnp.int32, (lanes, LANES), 0)
            place = lax.broadcasted_iota(jnp.int32, (lanes, LANES), 1)
            for t in range(group * rows // LANES):
                acc = None
                for g in range(group):
                    if g * rows >= (t + 1) * LANES or (g + 1) * rows <= t * LANES:
                        continue
                    shift = g * rows - t * LANES - at
                    hit = (place == source + shift) & (source >= at) & (source < at + rows)
                    term = half_dot(blocks[g], hit.astype(bf16))
                    acc = term if acc is None else acc + term
                tile = half_dot(chosen, acc.astype(bf16))
                out[to : to + size, :] = tile.astype(bf16)
                to += size
        if to < out.shape[0]:
            out[to:, :] = jnp.zeros((out.shape[0] - to, LANES), bf16)

    @pl.when(first[0, 0] == 0)
    def _():
        lay(sets[0])

    @pl.when(first[0, 0] != 0)
    def _():
        lay(sets[1])


def message_kernel(ids, stats, every, spill, out, msg, sem):
    copy = pltpu.make_async_copy(part_of(spill, MESSAGE_PART), msg, sem.at[0])
    copy.start()
    group = out.shape[0]
    count = stats.shape[1] // 2
    total = jnp.sum(every[:, :, :count], axis=0)
    share = stats[:, :count] / jnp.where(total > 0.0, total, 1.0)
    scale = widen(share, LANES).T
    copy.wait()
    by_owner(hot_rows(ids[1:2, :], count).astype(bf16), msg, out, group, scale)


def rotate_kernel(
    own, ids, nodes, wigner, half, z, spill, maps, paired, wide, grad_edge, out_sem
):
    group, edges = nodes.shape[0], wigner.shape[2]
    channels = LANES
    per = 16 // (2 * own)
    count = own * group
    half_copy = pltpu.make_async_copy(half, maps.at[2], out_sem.at[2])
    half_copy.start()
    target = hot_rows(ids[1:2, :], count)
    both = (target + hot_rows(ids[0:1, :], count)).astype(bf16)
    target = target.astype(bf16)
    wide[...] = wigner[...].astype(f32)
    for first in range(0, COEF, per):
        rows = nodes[:, first * 2 * own : first * 2 * own + 16, :].astype(f32)
        rows = rows.reshape(group, 2 * per, own, channels)
        for j in range(first, min(first + per, COEF)):
            at = 2 * (j - first)
            here = rows[:, at].reshape(count, channels).T.astype(bf16)
            paired[j] = half_dot(here, both).astype(bf16).astype(f32)
            here = rows[:, at + 1].reshape(count, channels).T.astype(bf16)
            grad_edge[j] = half_dot(here, target).astype(bf16)
    copy = pltpu.make_async_copy(grad_edge, part_of(spill, EDGE_PART), out_sem.at[0])
    copy.start()
    for l in range(LMAX + 1):
        for k in ROWS_OF[l]:
            acc = None
            for j in COEFS_OF[l]:
                term = wide[j, k : k + 1, :] * paired[j]
                acc = term if acc is None else acc + term
            z[k] = acc.astype(bf16)
    zero_copy = pltpu.make_async_copy(
        z.at[pl.ds(0, LMAX + 1)], part_of(spill, ZERO_PART), out_sem.at[1]
    )
    zero_copy.start()
    copy.wait()
    zero_copy.wait()
    half_copy.wait()


def forward_kernel(
    places,
    group,
    first,
    ids,
    z,
    wigner,
    spill_in,
    attention_t,
    maps_in,
    other,
    spill,
    maps,
    stats,
    sent,
    scalar,
    per_edge,
    held,
    y,
    wide,
    norm,
    msg,
    heads_acc,
    grad_edge,
    sems,
    out_sem,
):
    channels, edges = LANES, wigner.shape[2]
    heads = attention_t.shape[0]
    count = stats.shape[1] // 2
    mine = maps_in.at[2]
    start_weights(places, first[0, 0], mine, other, held, sems)
    edge_copy = pltpu.make_async_copy(part_of(spill_in, EDGE_PART), grad_edge, out_sem.at[1])
    edge_copy.start()
    wide[...] = wigner[...].astype(f32)
    base, rows = ZERO
    acc = None
    wait_weights(places, (0,), mine, held, sems)
    for tiles in pairs(rows):
        right = z[tiles[0] : tiles[-1] + 1].reshape(-1, edges)
        term = half_dot(map_tiles(held, places[0], tiles), right)
        acc = term if acc is None else acc + term
    spread(acc, held, places[0][2], base, y)
    for (base, rows), real, imag in ((ONE, places[1], places[2]), (TWO, places[3], places[4])):
        wait_weights(places, (1, 2) if base == ONE[0] else (3, 4), mine, held, sems)
        acc = None
        for tiles in pairs(rows):
            lo, hi = base + tiles[0], base + tiles[-1] + 1
            plus = z[lo:hi].reshape(-1, edges)
            minus = z[lo + rows : hi + rows].reshape(-1, edges)
            term = half_dot(map_tiles(held, real, tiles), jnp.concatenate([plus, minus], axis=1))
            term = term + half_dot(
                map_tiles(held, imag, tiles), jnp.concatenate([-minus, plus], axis=1)
            )
            acc = term if acc is None else acc + term
        spread(acc[:, :edges], held, real[2], base * channels, y)
        spread(acc[:, edges:], held, real[2], (base + rows) * channels, y)
    maps_copy = pltpu.make_async_copy(held, maps.at[pl.ds(0, 2)], out_sem.at[2])
    maps_copy.start()
    value = y[:channels, :]
    scalar[...] = value
    y[...] = y[...].astype(bf16).astype(f32)
    gating = (value / (1.0 + jnp.exp(-value))).astype(bf16)
    logits = half_dot(attention_t[...], gating)
    weight = jnp.where(ids[2:3, :] > 0, jnp.exp(logits), 0.0)
    target = hot_rows(ids[1:2, :], count).astype(bf16)
    own_sum = of_terms(nt_dot(in_terms(weight), target))
    at_edges = of_terms(half_dot(in_terms(own_sum), target))
    own_norm = weight / jnp.where(at_edges > 0.0, at_edges, 1.0)
    norm[...] = widen(own_norm, channels)

    def body(start):
        at = pl.ds(start, CHUNK)
        own = norm[at, :]
        total = jnp.zeros((CHUNK, edges), f32)
        for l in range(LMAX + 1):
            fields = [y[rows_at(k, start), :] for k in ROWS_OF[l]]
            for j in COEFS_OF[l]:
                acc = None
                for k, field in zip(ROWS_OF[l], fields):
                    term = wide[j, k : k + 1, :] * field
                    acc = term if acc is None else acc + term
                total = total + acc * grad_edge[j, at, :].astype(f32)
                msg[j, at, :] = (acc * own).astype(bf16)
        heads_acc[at, :] = total

    edge_copy.wait()
    chunks(channels, body)
    copy = pltpu.make_async_copy(msg, part_of(spill, MESSAGE_PART), out_sem.at[0])
    copy.start()
    grad_norm = jnp.sum(heads_acc[...].reshape(heads, channels // heads, edges), axis=1)
    own_shared = of_terms(nt_dot(in_terms(own_norm * grad_norm), target))
    sums = jnp.concatenate([own_sum, own_shared], axis=1)
    stats[...] = sums
    for owner in range(group):
        sent[owner] = sums
    per_edge[:heads, :] = own_norm
    per_edge[heads:, :] = grad_norm
    copy.wait()
    maps_copy.wait()


def backward_kernel(
    first,
    ids,
    stats,
    every,
    scalar,
    per_edge,
    wigner,
    spill_in,
    attention,
    attention_t,
    spill,
    mine,
    theirs,
    wide,
    norm,
    grad,
    turned,
    grad_conv,
    grad_edge,
    z,
    out_sem,
):
    channels, edges = LANES, wigner.shape[2]
    heads = attention_t.shape[0]
    count = stats.shape[1] // 2
    edge_copy = pltpu.make_async_copy(part_of(spill_in, EDGE_PART), grad_edge, out_sem.at[1])
    edge_copy.start()
    zero_copy = pltpu.make_async_copy(part_of(spill_in, ZERO_PART), z, out_sem.at[2])
    zero_copy.start()
    wide[...] = wigner[...].astype(f32)
    total = jnp.sum(every[:, :, :count], axis=0)
    total = jnp.where(total > 0.0, total, 1.0)
    shares = every[:, :, :count] / total[None]
    shared = jnp.sum(shares * every[:, :, count:], axis=0)
    own_share = stats[:, :count] / total
    target = hot_rows(ids[1:2, :], count).astype(bf16)
    at_edges = jnp.concatenate([own_share, shared], axis=0)
    at_edges = of_terms(half_dot(in_terms(at_edges), target))
    normalized = per_edge[:heads, :] * at_edges[:heads]
    grad_logit = normalized * (per_edge[heads:, :] - at_edges[heads:])
    value = scalar[...]
    sigmoid = 1.0 / (1.0 + jnp.exp(-value))
    gating = (value / (1.0 + jnp.exp(-value))).astype(bf16)
    logit_terms = in_terms(grad_logit)
    att = of_terms(nt_dot(logit_terms, gating))
    grad_gating = half_dot(attention[...], logit_terms)
    grad_scalar = grad_gating * sigmoid * (1.0 + value * (1.0 - sigmoid))
    norm[...] = widen(normalized, channels)

    def body(start):
        at = pl.ds(start, CHUNK)
        own = norm[at, :]
        for l in range(LMAX + 1):
            fields = [
                (grad_edge[j, at, :].astype(f32) * own).astype(bf16).astype(f32)
                for j in COEFS_OF[l]
            ]
            for k in ROWS_OF[l]:
                acc = None
                for j, field in zip(COEFS_OF[l], fields):
                    term = wide[j, k : k + 1, :] * field
                    acc = term if acc is None else acc + term
                grad[rows_at(k, start), :] = acc

    edge_copy.wait()
    chunks(channels, body)
    grad[:channels, :] = grad[:channels, :] + grad_scalar
    depth = (LMAX + 1) * channels
    parts, share = mine.shape[0], depth // (2 * mine.shape[0])
    grad_conv[...] = grad[...].astype(bf16).reshape(grad_conv.shape)
    copy = pltpu.make_async_copy(grad_conv, part_of(spill, CONV_PART), out_sem.at[0])
    copy.start()
    zero_copy.wait()
    turned[:depth, :] = nt_dot(
        grad_conv[: LMAX + 1].reshape(depth, edges), z[...].reshape(depth, edges)
    )
    turned[depth:, :] = jnp.zeros((turned.shape[0] - depth, depth), f32)
    padded = mine.shape[1]
    tail_row = lax.broadcasted_iota(jnp.int32, (padded, depth), 0)
    one = jnp.concatenate([att[h : h + 1, :] for h in range(LMAX + 1)], axis=1)
    two = [att[h : h + 1, :] for h in range(LMAX + 1, heads)]
    two = jnp.concatenate(two + [jnp.zeros((1, depth - len(two) * channels), f32)], axis=1)

    def store(outs):
        for core in range(2):
            for part in range(parts):
                at = (2 * part + core) * share
                block = turned[at : at + padded, :]
                block = jnp.where(tail_row == share, one, block)
                block = jnp.where(tail_row == share + 1, two, block)
                outs[core][part] = block.astype(bf16)

    @pl.when(first[0, 0] == 0)
    def _():
        store((mine, theirs))

    @pl.when(first[0, 0] != 0)
    def _():
        store((theirs, mine))

    copy.wait()


def scatter_kernel(
    places,
    group,
    own,
    ids,
    spill,
    wigner,
    maps,
    spill_out,
    held,
    wide,
    dz,
    gp,
    grad,
    grad_rows,
    grads,
    grad_conv,
    sems,
    out_sem,
):
    channels, edges = LANES, wigner.shape[2]
    count = own * group
    conv_copy = pltpu.make_async_copy(part_of(spill, CONV_PART), grad_conv, out_sem.at[1])
    conv_copy.start()
    mine = maps.at[0]
    start_weights(places, None, mine, maps.at[1], held, sems)
    wide[...] = wigner[...].astype(f32)
    conv_copy.wait()
    grad[...] = grad_conv[...].astype(f32).reshape(grad.shape)
    zs = held.shape[1]
    for base, rows in (ZERO, ONE, (ONE[0] + ONE[1], ONE[1]), TWO, (TWO[0] + TWO[1], TWO[1])):
        size = rows * channels // (2 * zs)
        blocks = []
        for zz in range(zs):
            for xh in range(2):
                at = base * channels + (xh * zs + zz) * size
                blocks.append(grad[at : at + size, :])
        ordered = jnp.concatenate(blocks, axis=0)
        for t in range(rows):
            at = slice(t * channels, (t + 1) * channels)
            to = (base + t) * channels
            grad_rows[:, to : to + channels] = ordered[at, :].T.astype(bf16)
    base, rows = ZERO
    left = grad_rows[:, : rows * channels]
    wait_weights(places, (0,), mine, held, sems)
    for tiles in pairs(rows):
        out = half_dot(left, map_tiles(held, places[0], tiles)).astype(bf16).astype(f32)
        for i, t in enumerate(tiles):
            dz[t] = out[:, i * channels : (i + 1) * channels].T
    for (base, rows), real, imag in ((ONE, places[1], places[2]), (TWO, places[3], places[4])):
        wait_weights(places, (1, 2) if base == ONE[0] else (3, 4), mine, held, sems)
        plus = grad_rows[:, base * channels : (base + rows) * channels]
        minus = grad_rows[:, (base + rows) * channels : (base + 2 * rows) * channels]
        left = jnp.concatenate([plus, minus], axis=0)
        crossed = jnp.concatenate([minus, -plus], axis=0)
        for tiles in pairs(rows):
            out = half_dot(left, map_tiles(held, real, tiles))
            out = out + half_dot(crossed, map_tiles(held, imag, tiles))
            out = out.astype(bf16).astype(f32)
            for i, t in enumerate(tiles):
                at = slice(i * channels, (i + 1) * channels)
                dz[base + t] = out[:edges, at].T
                dz[base + rows + t] = out[edges:, at].T

    def body(start):
        at = pl.ds(start, CHUNK)
        for l in range(LMAX + 1):
            fields = [dz[k, at, :] for k in ROWS_OF[l]]
            for j in COEFS_OF[l]:
                acc = None
                for k, field in zip(ROWS_OF[l], fields):
                    term = wide[j, k : k + 1, :] * field
                    acc = term if acc is None else acc + term
                gp[j, at, :] = acc.astype(bf16)

    chunks(channels, body)
    both = (hot_rows(ids[1:2, :], count) + hot_rows(ids[0:1, :], count)).astype(bf16)
    by_owner(both, gp, grads, group, split=True)
    copy = pltpu.make_async_copy(
        grads, part_of(spill_out, (SUM_START, grads.shape[0])), out_sem.at[0]
    )
    copy.start()
    copy.wait()


def node_rows(own):
    return -(-COEF * own // 16) * 16


def one_hot(rows, columns, shift, low, high):
    row = lax.broadcasted_iota(jnp.int32, (rows, columns), 0)
    column = lax.broadcasted_iota(jnp.int32, (rows, columns), 1)
    return ((column == row + shift) & (row >= low) & (row < high)).astype(bf16)


def tail_kernel(used, share, heads, parts, spill, grads, total, att, sems):
    count, depth = parts.shape[0], parts.shape[2]
    group = grads.shape[0]
    inner, skip = depth // group, used % 16
    base, rows = used - skip, grads.shape[1] - (used - skip)
    low_copy = pltpu.make_async_copy(
        spill.at[pl.ds(SUM_START, group)], grads.at[:, pl.ds(0, LANES), :], sems.at[0]
    )
    high_copy = pltpu.make_async_copy(
        spill.at[pl.ds(SUM_START + group, group), pl.ds(0, base + 16 - LANES), :],
        grads.at[:, pl.ds(LANES, base + 16 - LANES), :],
        sems.at[1],
    )
    low_copy.start()
    high_copy.start()
    acc = parts[0].astype(f32)
    for p in range(1, count):
        acc = acc + parts[p].astype(f32)
    total[...] = acc
    for h in range(heads):
        row, at = share + h // (depth // LANES), h % (depth // LANES) * LANES
        att[h : h + 1, :] = total[row : row + 1, at : at + LANES]
    low = att[...].astype(bf16)
    half = LANES // 2
    left = half_dot(low, one_hot(LANES, LANES, half, 0, half)).astype(bf16)
    right = half_dot(low, one_hot(LANES, LANES, 0, half, LANES)).astype(bf16)
    row = lax.broadcasted_iota(jnp.int32, (rows, heads), 0)
    head = lax.broadcasted_iota(jnp.int32, (rows, heads), 1)
    tail = half_dot((row == head + skip).astype(bf16), left)
    tail = tail + half_dot((row == head + skip + heads).astype(bf16), right)
    moved = half_dot(one_hot(rows, total.shape[0], -skip, skip, skip + share), acc.astype(bf16))
    moved = moved.astype(bf16)
    kept = lax.broadcasted_iota(jnp.int32, (rows, LANES), 0) < skip
    low_copy.wait()
    high_copy.wait()
    for g in range(group):
        first = g * inner // LANES * LANES
        last = -(-(g + 1) * inner // LANES) * LANES
        shift = g * inner - first
        place = one_hot(last - first, LANES, -shift, shift, shift + inner)
        piece = half_dot(moved[:, first:last], place) + tail
        before = grads[g, base : base + 16, :].astype(f32)
        if rows > 16:
            before = jnp.concatenate([before, jnp.zeros((rows - 16, LANES), f32)], axis=0)
        grads[g, base:, :] = jnp.where(kept, before, piece).astype(bf16)


def last_kernel(scale, parts, nodes, zero, att, total):
    acc = parts[0].astype(f32)
    for g in range(1, parts.shape[0]):
        acc = acc + parts[g].astype(f32)
    total[...] = acc
    used = nodes.shape[0] * nodes.shape[1]
    heads, half = att.shape[0], LANES // 2
    nodes[...] = acc[:used].astype(bf16).reshape(nodes.shape)
    zero[...] = total[used : used + zero.shape[0], :][:, : zero.shape[1]] * scale
    left = full_dot(
        total[used : used + heads, :], one_hot(LANES, LANES, -half, half, LANES).astype(f32)
    )
    lane = lax.broadcasted_iota(jnp.int32, (heads, LANES), 1)
    right = jnp.where(lane >= half, total[used + heads : used + 2 * heads, :], 0.0)
    att[...] = (left + right) * scale


def sum_kernel(parts, nodes, tail, total):
    acc = parts[0].astype(f32)
    for g in range(1, parts.shape[0]):
        acc = acc + parts[g].astype(f32)
    total[...] = acc
    used = nodes.shape[0] * nodes.shape[1]
    nodes[...] = acc[:used].astype(bf16).reshape(nodes.shape)
    tail[...] = total[used : used + tail.shape[0], :]


def pad_to(block, rows, columns):
    return jnp.pad(block, ((0, rows - block.shape[0]), (0, columns - block.shape[1])))


def whole_lanes(count):
    return -(-count // LANES) * LANES


def gather_weights(shards):
    rows = [w.shape[0] for w in shards]
    columns = [w.shape[1] for w in shards]
    most = -(-max(columns) // 16) * 16
    sets = ((0, 1), (2, 3, 4))
    lanes = whole_lanes(max(sum(rows[i] for i in s) for s in sets))
    starts = [0] * len(shards)
    for half_index, s in enumerate(sets):
        for n, i in enumerate(s):
            starts[i] = half_index * lanes + sum(rows[j] for j in s[:n])
    packed = pl.pallas_call(
        functools.partial(pack_kernel, starts),
        out_shape=jax.ShapeDtypeStruct((most, 2 * lanes), bf16),
        in_specs=[HBM] * len(shards),
        out_specs=VMEM,
        scratch_shapes=[pltpu.VMEM(w.shape[::-1], bf16) for w in shards]
        + [pltpu.VMEM((most, 2 * lanes), f32), pltpu.SemaphoreType.DMA((len(shards),))],
        compiler_params=WHOLE,
    )(*[w.T for w in shards])
    core = lax.axis_index("core")
    near = lax.all_gather(packed, "core")
    sent = lax.dynamic_slice_in_dim(near, core * lanes, lanes, axis=2)
    slabs = gather(sent.reshape(2 * most, lanes), ROW_GROUP)
    group = slabs.shape[0] // 2
    places = [None] * len(shards)
    depth = 0
    for half_index, s in enumerate(sets):
        at = 0
        for i in s:
            tiles = group * rows[i] // LANES
            places[i] = (half_index, at, 4 * columns[i], tiles)
            at += tiles * 4 * columns[i]
        depth = max(depth, at)
    kinds = [[(rows[i], columns[i], starts[i] - n * lanes) for i in s] for n, s in enumerate(sets)]
    tiled = pl.pallas_call(
        functools.partial(slab_kernel, kinds),
        out_shape=jax.ShapeDtypeStruct((depth, LANES), bf16),
        in_specs=[pl.BlockSpec(memory_space=pltpu.SMEM), VMEM],
        out_specs=VMEM,
        compiler_params=SMALL,
    )(core.astype(jnp.int32).reshape(1, 1), slabs)
    return lax.all_gather(tiled, "z"), places, tiled


def on_device(
    embeddings,
    atom_counts,
    edge_counts,
    source,
    target,
    wigner,
    cotangent,
    w_zero,
    w_one_real,
    w_one_imag,
    w_two_real,
    w_two_imag,
    attention,
):
    half, places, tiled = gather_weights((w_zero, w_one_real, w_one_imag, w_two_real, w_two_imag))
    row_count = embeddings.shape[1]
    harmonics = embeddings.shape[2]
    channels = embeddings.shape[3]
    width = harmonics * channels
    edge_rows = source.shape[1]
    head_count = attention.shape[1]
    group = lax.axis_size(GRAPH)
    all_nodes = row_count * group
    rotation = jnp.transpose(wigner[0], (1, 0, 2))
    in_use = (lax.iota(jnp.int32, edge_rows) < edge_counts[0, 0]).astype(jnp.int32)
    ids = jnp.stack([source[0], target[0], in_use] + [jnp.zeros_like(in_use)] * 5)
    attention_t = attention.T
    core = lax.axis_index("core")
    first = core.astype(jnp.int32).reshape(1, 1)
    own_first = lax.axis_index(GRAPH) * row_count
    present = ((own_first + lax.iota(jnp.int32, row_count)) < atom_counts[0])[:, None]
    cot_rows = jnp.where(present[:, :, None], cotangent[0], 0.0).astype(bf16)
    own_rows = jnp.stack([embeddings[0], cot_rows])
    own_rows = jnp.transpose(own_rows, (2, 0, 1, 3)).reshape(-1, channels)
    own_rows = pad_to(own_rows, -(-own_rows.shape[0] // 16) * 16, channels)
    own_rows, tiled = lax.optimization_barrier((own_rows, tiled))
    nodes = gather(own_rows, GRAPH)
    half, nodes = lax.optimization_barrier((half, nodes))
    other = lax.ppermute(half, "core", [(0, 1), (1, 0)])

    smem = pl.BlockSpec(memory_space=pltpu.SMEM)
    field = (channels, edge_rows)
    wide = pltpu.VMEM(rotation.shape, f32)
    maps_shape = jax.ShapeDtypeStruct((MAP_SLOTS,) + half.shape, bf16)
    spill_shape = jax.ShapeDtypeStruct((SPILL,) + field, bf16)
    out_copy = pltpu.SemaphoreType.DMA((1,))
    two_copies = pltpu.SemaphoreType.DMA((2,))
    edge_field = pltpu.VMEM((COEF,) + field, bf16)
    z, spill, maps = pl.pallas_call(
        functools.partial(rotate_kernel, row_count),
        out_shape=(
            jax.ShapeDtypeStruct((REDUCED,) + field, bf16),
            spill_shape,
            maps_shape,
        ),
        in_specs=[VMEM] * 3 + [HBM],
        out_specs=[VMEM, HBM, HBM],
        scratch_shapes=[
            pltpu.VMEM((COEF,) + field, f32),
            wide,
            edge_field,
            pltpu.SemaphoreType.DMA((3,)),
        ],
        compiler_params=LARGE,
    )(ids, nodes, rotation, half)
    held = pltpu.VMEM((2,) + half.shape, bf16)
    copies = pltpu.SemaphoreType.DMA((len(places),))

    span = node_rows(row_count)
    sums = (head_count, 2 * all_nodes)
    spill, maps, stats, sent, scalar, per_edge = pl.pallas_call(
        functools.partial(forward_kernel, places, group),
        out_shape=(
            spill_shape,
            maps_shape,
            jax.ShapeDtypeStruct(sums, f32),
            jax.ShapeDtypeStruct((group,) + sums, f32),
            jax.ShapeDtypeStruct(field, f32),
            jax.ShapeDtypeStruct((2 * head_count, edge_rows), f32),
        ),
        in_specs=[smem] + [VMEM] * 3 + [HBM, VMEM] + [HBM] * 2,
        out_specs=[HBM] * 2 + [VMEM] * 4,
        scratch_shapes=[
            held,
            pltpu.VMEM((REDUCED * channels, edge_rows), f32),
            wide,
            pltpu.VMEM(field, f32),
            pltpu.VMEM((COEF,) + field, bf16),
            pltpu.VMEM(field, f32),
            edge_field,
            copies,
            pltpu.SemaphoreType.DMA((3,)),
        ],
        input_output_aliases={4: 0, 6: 1},
        compiler_params=LARGE,
    )(first, ids, z, rotation, spill, attention_t, maps, other)
    every = exchange(sent, GRAPH)

    columns = lax.axis_size(COLUMN_GROUP)
    depth = channels * (LMAX + 1)
    share = depth // (2 * columns)
    padded = -(-(share + 2) // 16) * 16
    partial = jax.ShapeDtypeStruct((columns, padded, depth), bf16)
    spill, mine, theirs = pl.pallas_call(
        backward_kernel,
        out_shape=(
            spill_shape,
            partial,
            partial,
        ),
        in_specs=[smem] + [VMEM] * 6 + [HBM] + [VMEM] * 2,
        out_specs=[HBM] + [VMEM] * 2,
        scratch_shapes=[
            wide,
            pltpu.VMEM(field, f32),
            pltpu.VMEM((REDUCED * channels, edge_rows), f32),
            pltpu.VMEM((depth + padded, depth), f32),
            pltpu.VMEM((REDUCED,) + field, bf16),
            edge_field,
            pltpu.VMEM((LMAX + 1,) + field, bf16),
            pltpu.SemaphoreType.DMA((3,)),
        ],
        input_output_aliases={7: 0},
        compiler_params=LARGE,
    )(first, ids, stats, every, scalar, per_edge, rotation, spill, jnp.tile(attention, (1, 3)), attention_t)

    theirs = lax.ppermute(theirs, "core", [(0, 1), (1, 0)])
    mine = (mine.astype(f32) + theirs.astype(f32)).astype(bf16)
    mine, spill = lax.optimization_barrier((mine, spill))
    zero_parts = exchange(mine, COLUMN_GROUP)
    message_sums = pl.pallas_call(
        message_kernel,
        out_shape=jax.ShapeDtypeStruct((group, span, channels), bf16),
        in_specs=[VMEM] * 3 + [HBM],
        out_specs=VMEM,
        scratch_shapes=[edge_field, out_copy],
        compiler_params=LARGE,
    )(ids, stats, every, spill)
    message_sums, spill = lax.optimization_barrier((message_sums, spill))
    message_sums = message_sums.reshape(group // 2, 2 * span, channels)
    near_sums = lax.psum_scatter(message_sums, "y", scatter_dimension=0, tiled=True)
    near_sums = near_sums.reshape(2, span, channels)
    side = lax.axis_index("xl")
    kept = lax.dynamic_index_in_dim(near_sums, side, keepdims=False)
    passed = lax.dynamic_index_in_dim(near_sums, 1 - side, keepdims=False)
    passed = lax.ppermute(passed, "xl", [(0, 1), (1, 0)])
    summed = kept.astype(f32) + passed.astype(f32)
    used = harmonics * row_count
    inner = depth // group
    lanes = whole_lanes(inner)
    beside = lanes - inner >= channels // 2 and lanes == channels and share >= 2 * head_count
    tail_rows = share if beside else share * lanes // LANES + head_count
    spill = pl.pallas_call(
        functools.partial(scatter_kernel, places, group, row_count),
        out_shape=spill_shape,
        in_specs=[VMEM, HBM, VMEM, HBM],
        out_specs=HBM,
        scratch_shapes=[
            held,
            wide,
            pltpu.VMEM((REDUCED,) + field, f32),
            pltpu.VMEM((COEF,) + field, bf16),
            pltpu.VMEM((REDUCED * channels, edge_rows), f32),
            pltpu.VMEM((edge_rows, REDUCED * channels), bf16),
            pltpu.VMEM((2 * group, channels, channels), bf16),
            pltpu.VMEM((REDUCED,) + field, bf16),
            copies,
            two_copies,
        ],
        input_output_aliases={1: 0},
        compiler_params=LARGE,
    )(ids, spill, rotation, maps)
    sums_shape = (group, -(-(used + tail_rows) // 16) * 16, channels)
    nodes_shape = jax.ShapeDtypeStruct((harmonics, row_count, channels), bf16)
    batch_scale = 1.0 / (2 * columns)
    if beside:
        grad_sums = pl.pallas_call(
            functools.partial(tail_kernel, used, share, head_count),
            out_shape=jax.ShapeDtypeStruct(sums_shape, bf16),
            in_specs=[VMEM, HBM],
            out_specs=VMEM,
            scratch_shapes=[
                pltpu.VMEM((padded, depth), f32),
                pltpu.VMEM((head_count, channels), f32),
                two_copies,
            ],
            compiler_params=LARGE,
        )(zero_parts, spill)
        last = exchange(grad_sums, GRAPH)
        grad_nodes, grad_zero, grad_att = pl.pallas_call(
            functools.partial(last_kernel, batch_scale),
            out_shape=(
                nodes_shape,
                jax.ShapeDtypeStruct((share, inner), f32),
                jax.ShapeDtypeStruct((head_count, channels), f32),
            ),
            in_specs=[VMEM],
            out_specs=[VMEM] * 3,
            scratch_shapes=[pltpu.VMEM(last.shape[1:], f32)],
            compiler_params=SMALL,
        )(last)
        grad_zero, grad_att = grad_zero.T, grad_att.T
    else:
        zero_sum = jnp.sum(zero_parts.astype(f32), axis=0)
        att = zero_sum[share : share + 2].reshape(-1)[: head_count * channels]
        zero_send = jnp.transpose(zero_sum[:share].reshape(share, group, inner), (1, 0, 2))
        zero_send = jnp.pad(zero_send, ((0, 0), (0, 0), (0, lanes - inner)))
        zero_send = zero_send.reshape(group, share * lanes // LANES, LANES)
        att = jnp.broadcast_to(
            att.reshape(1, head_count, channels), (group, head_count, channels)
        )
        last_rows = jnp.concatenate([zero_send, att], axis=1).astype(bf16)
        grad_sums = spill[SUM_START : SUM_START + 2 * group].reshape(2, group, channels, channels)
        grad_sums = jnp.transpose(grad_sums, (1, 0, 2, 3)).reshape(group, 2 * channels, channels)
        rest = jnp.zeros(sums_shape, bf16)
        grad_sums = lax.dynamic_update_slice(rest, grad_sums[:, :used], (0, 0, 0))
        grad_sums = lax.dynamic_update_slice(grad_sums, last_rows, (0, used, 0))
        last = exchange(grad_sums, GRAPH)
        grad_nodes, tail = pl.pallas_call(
            sum_kernel,
            out_shape=(nodes_shape, jax.ShapeDtypeStruct((tail_rows, channels), f32)),
            in_specs=[VMEM],
            out_specs=[VMEM] * 2,
            scratch_shapes=[pltpu.VMEM(last.shape[1:], f32)],
            compiler_params=SMALL,
        )(last)
        tail = tail * batch_scale
        zero_rows = share * lanes // LANES
        grad_zero = tail[:zero_rows].reshape(share, lanes)[:, :inner].T
        grad_att = tail[zero_rows:].T
    update = summed[:used].reshape(harmonics, row_count, channels)
    update = jnp.transpose(jnp.where(present[None], update, 0.0).astype(bf16), (1, 0, 2))
    grad_nodes = jnp.transpose(grad_nodes, (1, 0, 2))

    shape = (1, row_count, harmonics, channels)
    return (update.reshape(shape), grad_nodes.reshape(shape), grad_zero, grad_att)


def solution(mesh):
    columns, group = mesh.shape["dp"], mesh.shape["graph"]
    devices = mesh.devices.reshape(2, columns // 4, 2, group // 2, 2)
    fine = Mesh(devices, DP + GRAPH)
    in_specs = (
        P(DP, GRAPH, None, None),
        P(DP),
        P(DP, GRAPH),
        P(DP, GRAPH),
        P(DP, GRAPH),
        P(DP, None, None, GRAPH),
        P(DP, GRAPH, None, None),
        P(GRAPH, DP),
        P(GRAPH, DP),
        P(GRAPH, DP),
        P(GRAPH, DP),
        P(GRAPH, DP),
        P(),
    )
    out_specs = (P(DP, GRAPH, None, None), P(DP, GRAPH, None, None), P(GRAPH, DP), P())
    return jax.shard_map(
        on_device, mesh=fine, in_specs=in_specs, out_specs=out_specs, check_vma=False
    )
```

```python
import functools

import jax
import jax.numpy as jnp
from jax import lax
from jax.experimental import pallas as pl
from jax.experimental.pallas import tpu as pltpu
from jax.sharding import Mesh, PartitionSpec as P

LMAX = 6
LANES = 128
DP = ("xh", "z", "core")
COLUMN_GROUP = ("xh", "z")
ROW_GROUP = ("xh", "y", "xl")
GRAPH = ("y", "xl")
precise = lax.Precision.HIGHEST
f32 = jnp.float32
bf16 = jnp.bfloat16


def half_dot(left, right):
    return jnp.dot(left, right, preferred_element_type=f32)


def full_dot(left, right):
    return jnp.dot(left, right, precision=precise, preferred_element_type=f32)


def gather(block, axes):
    count = lax.axis_size(axes)
    copies = jnp.broadcast_to(block[None], (count,) + block.shape)
    return lax.all_to_all(copies, axes, split_axis=0, concat_axis=0, tiled=True)


def exchange(blocks, axes):
    return lax.all_to_all(blocks, axes, split_axis=0, concat_axis=0, tiled=True)


ROW_DEGREE = (
    list(range(LMAX + 1)) + list(range(1, LMAX + 1)) * 2 + list(range(2, LMAX + 1)) * 2
)
ROWS_OF = [[k for k, d in enumerate(ROW_DEGREE) if d == l] for l in range(LMAX + 1)]
COEFS_OF = [list(range(l * l, (l + 1) * (l + 1))) for l in range(LMAX + 1)]
REDUCED = len(ROW_DEGREE)
COEF = (LMAX + 1) ** 2
ZERO = (0, LMAX + 1)
ONE = (LMAX + 1, LMAX)
TWO = (3 * LMAX + 1, LMAX - 1)
CHUNK = 32
VMEM = pl.BlockSpec(memory_space=pltpu.VMEM)
HBM = pl.BlockSpec(memory_space=pltpu.HBM)
SMALL = pltpu.CompilerParams(vmem_limit_bytes=28 * 1024 * 1024)
LARGE = pltpu.CompilerParams(vmem_limit_bytes=48 * 1024 * 1024)
WHOLE = pltpu.CompilerParams(vmem_limit_bytes=60 * 1024 * 1024)
EDGE_PART = (0, COEF)
MESSAGE_PART = (COEF, COEF)
CONV_PART = (2 * COEF, REDUCED)
ZERO_PART = (2 * COEF + REDUCED, LMAX + 1)
SUM_START = 2 * COEF + REDUCED + LMAX + 1
SPILL = 600
MAP_SLOTS = 7


def nt_dot(left, right):
    return lax.dot_general(left, right, (((1,), (1,)), ((), ())), preferred_element_type=f32)


def nt_full(left, right):
    return lax.dot_general(
        left, right, (((1,), (1,)), ((), ())), precision=precise, preferred_element_type=f32
    )


def in_terms(values):
    parts, rest = [], values
    for _ in range(3):
        low = rest.astype(bf16).astype(f32)
        parts.append(low)
        rest = rest - low
    return jnp.concatenate(parts, axis=0).astype(bf16)


def of_terms(stacked):
    rows = stacked.shape[0] // 3
    return stacked[:rows] + stacked[rows : 2 * rows] + stacked[2 * rows :]


def hot_rows(ids, count):
    rows = lax.broadcasted_iota(jnp.int32, (count, ids.shape[1]), 0)
    return (rows == ids).astype(f32)


def widen(values, channels):
    heads, edges = values.shape
    wide = jnp.broadcast_to(values[:, None, :], (heads, channels // heads, edges))
    return wide.reshape(channels, edges)


def part_of(spill, part):
    return spill.at[pl.ds(part[0], part[1])]


def chunks(channels, body):
    def step(i, carry):
        body(pl.multiple_of(i * CHUNK, CHUNK))
        return carry

    lax.fori_loop(0, channels // CHUNK, step, 0)


def rows_at(k, start):
    return pl.ds(pl.multiple_of(k * LANES + start, CHUNK), CHUNK)


def start_weights(places, first, mine, other, held, sems):
    def go(halves):
        for i, (half, at, rows, tiles) in enumerate(places):
            span = pl.ds(at, tiles * rows)
            pltpu.make_async_copy(
                halves[half].at[:, span, :], held.at[half, :, span, :], sems.at[i]
            ).start()

    @pl.when(first == 0)
    def _():
        go((mine, other))

    @pl.when(first != 0)
    def _():
        go((other, mine))


def wait_weights(places, which, mine, held, sems):
    for i in which:
        half, at, rows, tiles = places[i]
        span = pl.ds(at, tiles * rows)
        pltpu.make_async_copy(mine.at[:, span, :], held.at[half, :, span, :], sems.at[i]).wait()


def map_tiles(held, place, tiles):
    half, at, rows, _ = place
    parts = []
    for t in tiles:
        part = held[half, :, at + t * rows : at + (t + 1) * rows, :]
        parts.append(part.reshape(-1, LANES))
    return parts[0] if len(parts) == 1 else jnp.concatenate(parts, axis=1)


def pairs(count):
    return [tuple(range(i, min(i + 2, count))) for i in range(0, count, 2)]


def spread(blocks, held, rows, base, out):
    zs = held.shape[1]
    size = rows // 2
    for z in range(zs):
        for xh in range(2):
            to = base + (xh * zs + z) * size
            at = (z * 2 + xh) * size
            out[to : to + size, :] = blocks[at : at + size, :]


def by_owner(target, turned, out, group, scale=None, split=False):
    channels = turned.shape[1]
    own = target.shape[0] // group
    per = 16 // own
    for first in range(0, COEF, per):
        parts = []
        for j in range(first, first + per):
            if j < COEF:
                part = nt_dot(target, turned[j])
                part = part if scale is None else part * scale
            else:
                part = jnp.zeros((target.shape[0], channels), f32)
            parts.append(part.reshape(group, 1, own, channels))
        block = jnp.concatenate(parts, axis=1).reshape(group, 16, channels)
        at = first * own
        if split:
            half, at = at // LANES * group, at % LANES
            out[half : half + group, at : at + 16, :] = block.astype(bf16)
        else:
            out[:, at : at + 16, :] = block.astype(bf16)


def pack_kernel(places, *refs):
    count = len(places)
    shards, out = refs[:count], refs[count]
    held, acc, sems = refs[count + 1 : -2], refs[-2], refs[-1]
    copies = [pltpu.make_async_copy(shards[i], held[i], sems.at[i]) for i in range(count)]
    for copy in copies:
        copy.start()
    acc[...] = jnp.zeros_like(acc)
    for copy, shard, at in zip(copies, held, places):
        columns, rows = shard.shape
        lane = lax.broadcasted_iota(jnp.int32, (rows, acc.shape[1]), 1)
        row = lax.broadcasted_iota(jnp.int32, (rows, acc.shape[1]), 0)
        place = (lane == row + at).astype(bf16)
        copy.wait()
        acc[:columns, :] += half_dot(shard[...], place)
    out[...] = acc[...].astype(bf16)


def slab_kernel(sets, fold, first, slabs, out):
    group, lanes = slabs.shape[0] // 2, slabs.shape[2] // fold
    most = slabs.shape[1] * fold // 2

    def unfolded(i):
        return [slabs[i][:, q * lanes : (q + 1) * lanes] for q in range(fold)]

    blocks = [jnp.concatenate(unfolded(g) + unfolded(group + g), axis=0) for g in range(group)]

    def rolled(which):
        wide = [block.astype(f32) for block in blocks]
        lane = lax.broadcasted_iota(jnp.int32, wide[0].shape, 1)
        to = 0
        for rows, columns, at in which:
            size = 4 * columns
            row = lax.broadcasted_iota(jnp.int32, (size, 4 * most), 0)
            column = lax.broadcasted_iota(jnp.int32, (size, 4 * most), 1)
            chosen = (column == row // columns * most + row % columns).astype(bf16)
            tiles = [None] * (group * rows // LANES)
            for g in range(group):
                t, off = divmod(g * rows, LANES)
                shift = (off - at) % LANES
                moved = pltpu.roll(wide[g], shift, 1) if shift else wide[g]
                tiles[t] = moved if tiles[t] is None else jnp.where(lane >= off, moved, tiles[t])
                if off + rows > LANES:
                    tiles[t + 1] = moved
            for t in range(0, len(tiles), 2):
                pair = jnp.concatenate([tile.astype(bf16) for tile in tiles[t : t + 2]], axis=1)
                pair = half_dot(chosen, pair).astype(bf16)
                for i in range(len(tiles[t : t + 2])):
                    out[to : to + size, :] = pair[:, i * LANES : (i + 1) * LANES]
                    to += size
        if to < out.shape[0]:
            out[to:, :] = jnp.zeros((out.shape[0] - to, LANES), bf16)

    def lay(which):
        if lanes == LANES:
            return rolled(which)
        to = 0
        for rows, columns, at in which:
            size = 4 * columns
            row = lax.broadcasted_iota(jnp.int32, (size, 4 * most), 0)
            lane = lax.broadcasted_iota(jnp.int32, (size, 4 * most), 1)
            kept = row // columns * most + row % columns
            chosen = (lane == kept).astype(bf16)
            source = lax.broadcasted_iota(jnp.int32, (lanes, LANES), 0)
            place = lax.broadcasted_iota(jnp.int32, (lanes, LANES), 1)
            for t in range(group * rows // LANES):
                acc = None
                for g in range(group):
                    if g * rows >= (t + 1) * LANES or (g + 1) * rows <= t * LANES:
                        continue
                    shift = g * rows - t * LANES - at
                    hit = (place == source + shift) & (source >= at) & (source < at + rows)
                    term = half_dot(blocks[g], hit.astype(bf16))
                    acc = term if acc is None else acc + term
                tile = half_dot(chosen, acc.astype(bf16))
                out[to : to + size, :] = tile.astype(bf16)
                to += size
        if to < out.shape[0]:
            out[to:, :] = jnp.zeros((out.shape[0] - to, LANES), bf16)

    @pl.when(first[0, 0] == 0)
    def _():
        lay(sets[0])

    @pl.when(first[0, 0] != 0)
    def _():
        lay(sets[1])


def message_kernel(ids, stats, every, spill, out, msg, sem):
    copy = pltpu.make_async_copy(part_of(spill, MESSAGE_PART), msg, sem.at[0])
    copy.start()
    group = out.shape[0]
    count = stats.shape[1] // 2
    total = jnp.sum(every[:, :, :count], axis=0)
    share = stats[:, :count] / jnp.where(total > 0.0, total, 1.0)
    scale = widen(share, LANES).T
    copy.wait()
    by_owner(hot_rows(ids[1:2, :], count).astype(bf16), msg, out, group, scale)


def rotate_kernel(
    own, ids, nodes, wigner, half, z, spill, maps, paired, wide, grad_edge, out_sem
):
    group, edges = nodes.shape[0], wigner.shape[2]
    channels = LANES
    per = 16 // (2 * own)
    count = own * group
    half_copy = pltpu.make_async_copy(half, maps.at[2], out_sem.at[2])
    half_copy.start()
    target = hot_rows(ids[1:2, :], count)
    both = (target + hot_rows(ids[0:1, :], count)).astype(bf16)
    target = target.astype(bf16)
    wide[...] = wigner[...].astype(f32)
    for first in range(0, COEF, per):
        rows = nodes[:, first * 2 * own : first * 2 * own + 16, :].astype(f32)
        rows = rows.reshape(group, 2 * per, own, channels)
        for j in range(first, min(first + per, COEF)):
            at = 2 * (j - first)
            here = rows[:, at].reshape(count, channels).T.astype(bf16)
            paired[j] = half_dot(here, both).astype(bf16).astype(f32)
            here = rows[:, at + 1].reshape(count, channels).T.astype(bf16)
            grad_edge[j] = half_dot(here, target).astype(bf16)
    copy = pltpu.make_async_copy(grad_edge, part_of(spill, EDGE_PART), out_sem.at[0])
    copy.start()
    for l in range(LMAX + 1):
        for k in ROWS_OF[l]:
            acc = None
            for j in COEFS_OF[l]:
                term = wide[j, k : k + 1, :] * paired[j]
                acc = term if acc is None else acc + term
            z[k] = acc.astype(bf16)
    zero_copy = pltpu.make_async_copy(
        z.at[pl.ds(0, LMAX + 1)], part_of(spill, ZERO_PART), out_sem.at[1]
    )
    zero_copy.start()
    copy.wait()
    zero_copy.wait()
    half_copy.wait()


def forward_kernel(
    places,
    group,
    first,
    ids,
    z,
    wigner,
    spill_in,
    attention_t,
    maps_in,
    other,
    spill,
    maps,
    stats,
    sent,
    scalar,
    per_edge,
    held,
    y,
    wide,
    norm,
    msg,
    heads_acc,
    grad_edge,
    sems,
    out_sem,
):
    channels, edges = LANES, wigner.shape[2]
    heads = attention_t.shape[0]
    count = stats.shape[1] // 2
    mine = maps_in.at[2]
    start_weights(places, first[0, 0], mine, other, held, sems)
    edge_copy = pltpu.make_async_copy(part_of(spill_in, EDGE_PART), grad_edge, out_sem.at[1])
    edge_copy.start()
    wide[...] = wigner[...].astype(f32)
    base, rows = ZERO
    acc = None
    wait_weights(places, (0,), mine, held, sems)
    for tiles in pairs(rows):
        right = z[tiles[0] : tiles[-1] + 1].reshape(-1, edges)
        term = half_dot(map_tiles(held, places[0], tiles), right)
        acc = term if acc is None else acc + term
    spread(acc, held, places[0][2], base, y)
    for (base, rows), real, imag in ((ONE, places[1], places[2]), (TWO, places[3], places[4])):
        wait_weights(places, (1, 2) if base == ONE[0] else (3, 4), mine, held, sems)
        acc = None
        for tiles in pairs(rows):
            lo, hi = base + tiles[0], base + tiles[-1] + 1
            plus = z[lo:hi].reshape(-1, edges)
            minus = z[lo + rows : hi + rows].reshape(-1, edges)
            term = half_dot(map_tiles(held, real, tiles), jnp.concatenate([plus, minus], axis=1))
            term = term + half_dot(
                map_tiles(held, imag, tiles), jnp.concatenate([-minus, plus], axis=1)
            )
            acc = term if acc is None else acc + term
        spread(acc[:, :edges], held, real[2], base * channels, y)
        spread(acc[:, edges:], held, real[2], (base + rows) * channels, y)
    maps_copy = pltpu.make_async_copy(other, maps.at[1], out_sem.at[2])
    maps_copy.start()
    value = y[:channels, :]
    scalar[...] = value
    y[...] = y[...].astype(bf16).astype(f32)
    gating = (value / (1.0 + jnp.exp(-value))).astype(bf16)
    logits = half_dot(attention_t[...], gating)
    weight = jnp.where(ids[2:3, :] > 0, jnp.exp(logits), 0.0)
    target = hot_rows(ids[1:2, :], count).astype(bf16)
    own_sum = of_terms(nt_dot(in_terms(weight), target))
    at_edges = of_terms(half_dot(in_terms(own_sum), target))
    own_norm = weight / jnp.where(at_edges > 0.0, at_edges, 1.0)
    norm[...] = widen(own_norm, channels)

    def body(start):
        at = pl.ds(start, CHUNK)
        own = norm[at, :]
        total = jnp.zeros((CHUNK, edges), f32)
        for l in range(LMAX + 1):
            fields = [y[rows_at(k, start), :] for k in ROWS_OF[l]]
            for j in COEFS_OF[l]:
                acc = None
                for k, field in zip(ROWS_OF[l], fields):
                    term = wide[j, k : k + 1, :] * field
                    acc = term if acc is None else acc + term
                total = total + acc * grad_edge[j, at, :].astype(f32)
                msg[j, at, :] = (acc * own).astype(bf16)
        heads_acc[at, :] = total

    edge_copy.wait()
    chunks(channels, body)
    copy = pltpu.make_async_copy(msg, part_of(spill, MESSAGE_PART), out_sem.at[0])
    copy.start()
    grad_norm = jnp.sum(heads_acc[...].reshape(heads, channels // heads, edges), axis=1)
    own_shared = of_terms(nt_dot(in_terms(own_norm * grad_norm), target))
    sums = jnp.concatenate([own_sum, own_shared], axis=1)
    stats[...] = sums
    for owner in range(group):
        sent[owner] = sums
    per_edge[:heads, :] = own_norm
    per_edge[heads:, :] = grad_norm
    copy.wait()
    maps_copy.wait()


def backward_kernel(
    first,
    ids,
    stats,
    every,
    scalar,
    per_edge,
    wigner,
    spill_in,
    attention,
    attention_t,
    spill,
    mine,
    theirs,
    wide,
    norm,
    grad,
    turned,
    grad_conv,
    grad_edge,
    z,
    out_sem,
):
    channels, edges = LANES, wigner.shape[2]
    heads = attention_t.shape[0]
    count = stats.shape[1] // 2
    edge_copy = pltpu.make_async_copy(part_of(spill_in, EDGE_PART), grad_edge, out_sem.at[1])
    edge_copy.start()
    zero_copy = pltpu.make_async_copy(part_of(spill_in, ZERO_PART), z, out_sem.at[2])
    zero_copy.start()
    wide[...] = wigner[...].astype(f32)
    total = jnp.sum(every[:, :, :count], axis=0)
    total = jnp.where(total > 0.0, total, 1.0)
    shares = every[:, :, :count] / total[None]
    shared = jnp.sum(shares * every[:, :, count:], axis=0)
    own_share = stats[:, :count] / total
    target = hot_rows(ids[1:2, :], count).astype(bf16)
    at_edges = jnp.concatenate([own_share, shared], axis=0)
    at_edges = of_terms(half_dot(in_terms(at_edges), target))
    normalized = per_edge[:heads, :] * at_edges[:heads]
    grad_logit = normalized * (per_edge[heads:, :] - at_edges[heads:])
    value = scalar[...]
    sigmoid = 1.0 / (1.0 + jnp.exp(-value))
    gating = (value / (1.0 + jnp.exp(-value))).astype(bf16)
    logit_terms = in_terms(grad_logit)
    att = of_terms(nt_dot(logit_terms, gating))
    grad_gating = half_dot(attention[...], logit_terms)
    grad_scalar = grad_gating * sigmoid * (1.0 + value * (1.0 - sigmoid))
    norm[...] = widen(normalized, channels)

    def body(start):
        at = pl.ds(start, CHUNK)
        own = norm[at, :]
        for l in range(LMAX + 1):
            fields = [
                (grad_edge[j, at, :].astype(f32) * own).astype(bf16).astype(f32)
                for j in COEFS_OF[l]
            ]
            for k in ROWS_OF[l]:
                acc = None
                for j, field in zip(COEFS_OF[l], fields):
                    term = wide[j, k : k + 1, :] * field
                    acc = term if acc is None else acc + term
                grad[rows_at(k, start), :] = acc

    edge_copy.wait()
    chunks(channels, body)
    grad[:channels, :] = grad[:channels, :] + grad_scalar
    depth = (LMAX + 1) * channels
    parts, share = mine.shape[0], depth // (2 * mine.shape[0])
    grad_conv[...] = grad[...].astype(bf16).reshape(grad_conv.shape)
    copy = pltpu.make_async_copy(grad_conv, part_of(spill, CONV_PART), out_sem.at[0])
    copy.start()
    zero_copy.wait()
    turned[:depth, :] = nt_dot(
        grad_conv[: LMAX + 1].reshape(depth, edges), z[...].reshape(depth, edges)
    )
    turned[depth:, :] = jnp.zeros((turned.shape[0] - depth, depth), f32)
    padded = mine.shape[1]
    tail_row = lax.broadcasted_iota(jnp.int32, (padded, depth), 0)
    one = jnp.concatenate([att[h : h + 1, :] for h in range(LMAX + 1)], axis=1)
    two = [att[h : h + 1, :] for h in range(LMAX + 1, heads)]
    two = jnp.concatenate(two + [jnp.zeros((1, depth - len(two) * channels), f32)], axis=1)

    def store(outs):
        for core in range(2):
            for part in range(parts):
                at = (2 * part + core) * share
                block = turned[at : at + padded, :]
                block = jnp.where(tail_row == share, one, block)
                block = jnp.where(tail_row == share + 1, two, block)
                outs[core][part] = block.astype(bf16)

    @pl.when(first[0, 0] == 0)
    def _():
        store((mine, theirs))

    @pl.when(first[0, 0] != 0)
    def _():
        store((theirs, mine))

    copy.wait()


def scatter_kernel(
    places,
    group,
    own,
    first,
    ids,
    spill,
    wigner,
    maps,
    spill_out,
    held,
    wide,
    dz,
    gp,
    grad,
    grad_rows,
    grads,
    grad_conv,
    sems,
    out_sem,
):
    channels, edges = LANES, wigner.shape[2]
    count = own * group
    conv_copy = pltpu.make_async_copy(part_of(spill, CONV_PART), grad_conv, out_sem.at[1])
    conv_copy.start()
    mine = maps.at[2]
    start_weights(places, first[0, 0], mine, maps.at[1], held, sems)
    wide[...] = wigner[...].astype(f32)
    conv_copy.wait()
    grad[...] = grad_conv[...].astype(f32).reshape(grad.shape)
    zs = held.shape[1]
    for base, rows in (ZERO, ONE, (ONE[0] + ONE[1], ONE[1]), TWO, (TWO[0] + TWO[1], TWO[1])):
        size = rows * channels // (2 * zs)
        blocks = []
        for zz in range(zs):
            for xh in range(2):
                at = base * channels + (xh * zs + zz) * size
                blocks.append(grad[at : at + size, :])
        ordered = jnp.concatenate(blocks, axis=0)
        for t in range(rows):
            at = slice(t * channels, (t + 1) * channels)
            to = (base + t) * channels
            grad_rows[:, to : to + channels] = ordered[at, :].T.astype(bf16)
    base, rows = ZERO
    left = grad_rows[:, : rows * channels]
    wait_weights(places, (0,), mine, held, sems)
    for tiles in pairs(rows):
        out = half_dot(left, map_tiles(held, places[0], tiles)).astype(bf16).astype(f32)
        for i, t in enumerate(tiles):
            dz[t] = out[:, i * channels : (i + 1) * channels].T
    for (base, rows), real, imag in ((ONE, places[1], places[2]), (TWO, places[3], places[4])):
        wait_weights(places, (1, 2) if base == ONE[0] else (3, 4), mine, held, sems)
        plus = grad_rows[:, base * channels : (base + rows) * channels]
        minus = grad_rows[:, (base + rows) * channels : (base + 2 * rows) * channels]
        left = jnp.concatenate([plus, minus], axis=0)
        crossed = jnp.concatenate([minus, -plus], axis=0)
        for tiles in pairs(rows):
            out = half_dot(left, map_tiles(held, real, tiles))
            out = out + half_dot(crossed, map_tiles(held, imag, tiles))
            out = out.astype(bf16).astype(f32)
            for i, t in enumerate(tiles):
                at = slice(i * channels, (i + 1) * channels)
                dz[base + t] = out[:edges, at].T
                dz[base + rows + t] = out[edges:, at].T

    def body(start):
        at = pl.ds(start, CHUNK)
        for l in range(LMAX + 1):
            fields = [dz[k, at, :] for k in ROWS_OF[l]]
            for j in COEFS_OF[l]:
                acc = None
                for k, field in zip(ROWS_OF[l], fields):
                    term = wide[j, k : k + 1, :] * field
                    acc = term if acc is None else acc + term
                gp[j, at, :] = acc.astype(bf16)

    chunks(channels, body)
    both = (hot_rows(ids[1:2, :], count) + hot_rows(ids[0:1, :], count)).astype(bf16)
    by_owner(both, gp, grads, group, split=True)
    copy = pltpu.make_async_copy(
        grads, part_of(spill_out, (SUM_START, grads.shape[0])), out_sem.at[0]
    )
    copy.start()
    copy.wait()


def node_rows(own):
    return -(-COEF * own // 16) * 16


def one_hot(rows, columns, shift, low, high):
    row = lax.broadcasted_iota(jnp.int32, (rows, columns), 0)
    column = lax.broadcasted_iota(jnp.int32, (rows, columns), 1)
    return ((column == row + shift) & (row >= low) & (row < high)).astype(bf16)


def tail_kernel(used, share, heads, parts, spill, grads, total, att, sems):
    count, depth = parts.shape[0], parts.shape[2]
    group = grads.shape[0]
    inner, skip = depth // group, used % 16
    base, rows = used - skip, grads.shape[1] - (used - skip)
    low_copy = pltpu.make_async_copy(
        spill.at[pl.ds(SUM_START, group)], grads.at[:, pl.ds(0, LANES), :], sems.at[0]
    )
    high_copy = pltpu.make_async_copy(
        spill.at[pl.ds(SUM_START + group, group), pl.ds(0, base + 16 - LANES), :],
        grads.at[:, pl.ds(LANES, base + 16 - LANES), :],
        sems.at[1],
    )
    low_copy.start()
    high_copy.start()
    acc = parts[0].astype(f32)
    for p in range(1, count):
        acc = acc + parts[p].astype(f32)
    total[...] = acc
    for h in range(heads):
        row, at = share + h // (depth // LANES), h % (depth // LANES) * LANES
        att[h : h + 1, :] = total[row : row + 1, at : at + LANES]
    low = att[...].astype(bf16)
    half = LANES // 2
    left = half_dot(low, one_hot(LANES, LANES, half, 0, half)).astype(bf16)
    right = half_dot(low, one_hot(LANES, LANES, 0, half, LANES)).astype(bf16)
    row = lax.broadcasted_iota(jnp.int32, (rows, heads), 0)
    head = lax.broadcasted_iota(jnp.int32, (rows, heads), 1)
    tail = half_dot((row == head + skip).astype(bf16), left)
    tail = tail + half_dot((row == head + skip + heads).astype(bf16), right)
    moved = half_dot(one_hot(rows, total.shape[0], -skip, skip, skip + share), acc.astype(bf16))
    moved = moved.astype(bf16)
    kept = lax.broadcasted_iota(jnp.int32, (rows, LANES), 0) < skip
    low_copy.wait()
    high_copy.wait()
    for g in range(group):
        first = g * inner // LANES * LANES
        last = -(-(g + 1) * inner // LANES) * LANES
        shift = g * inner - first
        place = one_hot(last - first, LANES, -shift, shift, shift + inner)
        piece = half_dot(moved[:, first:last], place) + tail
        before = grads[g, base : base + 16, :].astype(f32)
        if rows > 16:
            before = jnp.concatenate([before, jnp.zeros((rows - 16, LANES), f32)], axis=0)
        grads[g, base:, :] = jnp.where(kept, before, piece).astype(bf16)


def last_kernel(scale, parts, nodes, zero, att, total):
    acc = parts[0].astype(f32)
    for g in range(1, parts.shape[0]):
        acc = acc + parts[g].astype(f32)
    total[...] = acc
    used = nodes.shape[0] * nodes.shape[1]
    heads, half = att.shape[0], LANES // 2
    nodes[...] = acc[:used].astype(bf16).reshape(nodes.shape)
    zero[...] = total[used : used + zero.shape[0], :][:, : zero.shape[1]] * scale
    left = full_dot(
        total[used : used + heads, :], one_hot(LANES, LANES, -half, half, LANES).astype(f32)
    )
    lane = lax.broadcasted_iota(jnp.int32, (heads, LANES), 1)
    right = jnp.where(lane >= half, total[used + heads : used + 2 * heads, :], 0.0)
    att[...] = (left + right) * scale


def sum_kernel(parts, nodes, tail, total):
    acc = parts[0].astype(f32)
    for g in range(1, parts.shape[0]):
        acc = acc + parts[g].astype(f32)
    total[...] = acc
    used = nodes.shape[0] * nodes.shape[1]
    nodes[...] = acc[:used].astype(bf16).reshape(nodes.shape)
    tail[...] = total[used : used + tail.shape[0], :]


def pad_to(block, rows, columns):
    return jnp.pad(block, ((0, rows - block.shape[0]), (0, columns - block.shape[1])))


def whole_lanes(count):
    return -(-count // LANES) * LANES


def gather_weights(shards):
    rows = [w.shape[0] for w in shards]
    columns = [w.shape[1] for w in shards]
    most = -(-max(columns) // 16) * 16
    sets = ((0, 1), (2, 3, 4))
    lanes = whole_lanes(max(sum(rows[i] for i in s) for s in sets))
    starts = [0] * len(shards)
    for half_index, s in enumerate(sets):
        for n, i in enumerate(s):
            starts[i] = half_index * lanes + sum(rows[j] for j in s[:n])
    packed = pl.pallas_call(
        functools.partial(pack_kernel, starts),
        out_shape=jax.ShapeDtypeStruct((most, 2 * lanes), bf16),
        in_specs=[HBM] * len(shards),
        out_specs=VMEM,
        scratch_shapes=[pltpu.VMEM(w.shape[::-1], bf16) for w in shards]
        + [pltpu.VMEM((most, 2 * lanes), f32), pltpu.SemaphoreType.DMA((len(shards),))],
        compiler_params=WHOLE,
    )(*[w.T for w in shards])
    core = lax.axis_index("core")
    near = lax.all_gather(packed, "core")
    sent = lax.dynamic_slice_in_dim(near, core * lanes, lanes, axis=2)
    fold = 4 if lanes == LANES else 1
    sent = jnp.transpose(sent.reshape(fold, 2 * most // fold, lanes), (1, 0, 2))
    slabs = gather(sent.reshape(2 * most // fold, fold * lanes), ROW_GROUP)
    group = slabs.shape[0] // 2
    places = [None] * len(shards)
    depth = 0
    for half_index, s in enumerate(sets):
        at = 0
        for i in s:
            tiles = group * rows[i] // LANES
            places[i] = (half_index, at, 4 * columns[i], tiles)
            at += tiles * 4 * columns[i]
        depth = max(depth, at)
    kinds = [[(rows[i], columns[i], starts[i] - n * lanes) for i in s] for n, s in enumerate(sets)]
    tiled = pl.pallas_call(
        functools.partial(slab_kernel, kinds, fold),
        out_shape=jax.ShapeDtypeStruct((depth, LANES), bf16),
        in_specs=[pl.BlockSpec(memory_space=pltpu.SMEM), VMEM],
        out_specs=VMEM,
        compiler_params=SMALL,
    )(core.astype(jnp.int32).reshape(1, 1), slabs)
    return lax.all_gather(tiled, "z"), places, tiled


def on_device(
    embeddings,
    atom_counts,
    edge_counts,
    source,
    target,
    wigner,
    cotangent,
    w_zero,
    w_one_real,
    w_one_imag,
    w_two_real,
    w_two_imag,
    attention,
):
    half, places, tiled = gather_weights((w_zero, w_one_real, w_one_imag, w_two_real, w_two_imag))
    row_count = embeddings.shape[1]
    harmonics = embeddings.shape[2]
    channels = embeddings.shape[3]
    width = harmonics * channels
    edge_rows = source.shape[1]
    head_count = attention.shape[1]
    group = lax.axis_size(GRAPH)
    all_nodes = row_count * group
    rotation = jnp.transpose(wigner[0], (1, 0, 2))
    in_use = (lax.iota(jnp.int32, edge_rows) < edge_counts[0, 0]).astype(jnp.int32)
    ids = jnp.stack([source[0], target[0], in_use] + [jnp.zeros_like(in_use)] * 5)
    attention_t = attention.T
    core = lax.axis_index("core")
    first = core.astype(jnp.int32).reshape(1, 1)
    own_first = lax.axis_index(GRAPH) * row_count
    present = ((own_first + lax.iota(jnp.int32, row_count)) < atom_counts[0])[:, None]
    cot_rows = jnp.where(present[:, :, None], cotangent[0], 0.0).astype(bf16)
    own_rows = jnp.stack([embeddings[0], cot_rows])
    own_rows = jnp.transpose(own_rows, (2, 0, 1, 3)).reshape(-1, channels)
    own_rows = pad_to(own_rows, -(-own_rows.shape[0] // 16) * 16, channels)
    own_rows, tiled = lax.optimization_barrier((own_rows, tiled))
    nodes = gather(own_rows, GRAPH)
    half, nodes = lax.optimization_barrier((half, nodes))
    other = lax.ppermute(half, "core", [(0, 1), (1, 0)])

    smem = pl.BlockSpec(memory_space=pltpu.SMEM)
    field = (channels, edge_rows)
    wide = pltpu.VMEM(rotation.shape, f32)
    maps_shape = jax.ShapeDtypeStruct((MAP_SLOTS,) + half.shape, bf16)
    spill_shape = jax.ShapeDtypeStruct((SPILL,) + field, bf16)
    out_copy = pltpu.SemaphoreType.DMA((1,))
    two_copies = pltpu.SemaphoreType.DMA((2,))
    edge_field = pltpu.VMEM((COEF,) + field, bf16)
    z, spill, maps = pl.pallas_call(
        functools.partial(rotate_kernel, row_count),
        out_shape=(
            jax.ShapeDtypeStruct((REDUCED,) + field, bf16),
            spill_shape,
            maps_shape,
        ),
        in_specs=[VMEM] * 3 + [HBM],
        out_specs=[VMEM, HBM, HBM],
        scratch_shapes=[
            pltpu.VMEM((COEF,) + field, f32),
            wide,
            edge_field,
            pltpu.SemaphoreType.DMA((3,)),
        ],
        compiler_params=LARGE,
    )(ids, nodes, rotation, half)
    held = pltpu.VMEM((2,) + half.shape, bf16)
    copies = pltpu.SemaphoreType.DMA((len(places),))

    span = node_rows(row_count)
    sums = (head_count, 2 * all_nodes)
    spill, maps, stats, sent, scalar, per_edge = pl.pallas_call(
        functools.partial(forward_kernel, places, group),
        out_shape=(
            spill_shape,
            maps_shape,
            jax.ShapeDtypeStruct(sums, f32),
            jax.ShapeDtypeStruct((group,) + sums, f32),
            jax.ShapeDtypeStruct(field, f32),
            jax.ShapeDtypeStruct((2 * head_count, edge_rows), f32),
        ),
        in_specs=[smem] + [VMEM] * 3 + [HBM, VMEM] + [HBM] * 2,
        out_specs=[HBM] * 2 + [VMEM] * 4,
        scratch_shapes=[
            held,
            pltpu.VMEM((REDUCED * channels, edge_rows), f32),
            wide,
            pltpu.VMEM(field, f32),
            pltpu.VMEM((COEF,) + field, bf16),
            pltpu.VMEM(field, f32),
            edge_field,
            copies,
            pltpu.SemaphoreType.DMA((3,)),
        ],
        input_output_aliases={4: 0, 6: 1},
        compiler_params=LARGE,
    )(first, ids, z, rotation, spill, attention_t, maps, other)
    every = exchange(sent, GRAPH)

    columns = lax.axis_size(COLUMN_GROUP)
    depth = channels * (LMAX + 1)
    share = depth // (2 * columns)
    padded = -(-(share + 2) // 16) * 16
    partial = jax.ShapeDtypeStruct((columns, padded, depth), bf16)
    spill, mine, theirs = pl.pallas_call(
        backward_kernel,
        out_shape=(
            spill_shape,
            partial,
            partial,
        ),
        in_specs=[smem] + [VMEM] * 6 + [HBM] + [VMEM] * 2,
        out_specs=[HBM] + [VMEM] * 2,
        scratch_shapes=[
            wide,
            pltpu.VMEM(field, f32),
            pltpu.VMEM((REDUCED * channels, edge_rows), f32),
            pltpu.VMEM((depth + padded, depth), f32),
            pltpu.VMEM((REDUCED,) + field, bf16),
            edge_field,
            pltpu.VMEM((LMAX + 1,) + field, bf16),
            pltpu.SemaphoreType.DMA((3,)),
        ],
        input_output_aliases={7: 0},
        compiler_params=LARGE,
    )(first, ids, stats, every, scalar, per_edge, rotation, spill, jnp.tile(attention, (1, 3)), attention_t)

    theirs = lax.ppermute(theirs, "core", [(0, 1), (1, 0)])
    mine = (mine.astype(f32) + theirs.astype(f32)).astype(bf16)
    mine, spill = lax.optimization_barrier((mine, spill))
    zero_parts = exchange(mine, COLUMN_GROUP)
    message_sums = pl.pallas_call(
        message_kernel,
        out_shape=jax.ShapeDtypeStruct((group, span, channels), bf16),
        in_specs=[VMEM] * 3 + [HBM],
        out_specs=VMEM,
        scratch_shapes=[edge_field, out_copy],
        compiler_params=LARGE,
    )(ids, stats, every, spill)
    message_sums, spill = lax.optimization_barrier((message_sums, spill))
    message_sums = message_sums.reshape(group // 2, 2 * span, channels)
    near_sums = lax.psum_scatter(message_sums, "y", scatter_dimension=0, tiled=True)
    near_sums = near_sums.reshape(2, span, channels)
    side = lax.axis_index("xl")
    kept = lax.dynamic_index_in_dim(near_sums, side, keepdims=False)
    passed = lax.dynamic_index_in_dim(near_sums, 1 - side, keepdims=False)
    passed = lax.ppermute(passed, "xl", [(0, 1), (1, 0)])
    summed = kept.astype(f32) + passed.astype(f32)
    used = harmonics * row_count
    inner = depth // group
    lanes = whole_lanes(inner)
    beside = lanes - inner >= channels // 2 and lanes == channels and share >= 2 * head_count
    tail_rows = share if beside else share * lanes // LANES + head_count
    spill = pl.pallas_call(
        functools.partial(scatter_kernel, places, group, row_count),
        out_shape=spill_shape,
        in_specs=[smem, VMEM, HBM, VMEM, HBM],
        out_specs=HBM,
        scratch_shapes=[
            held,
            wide,
            pltpu.VMEM((REDUCED,) + field, f32),
            pltpu.VMEM((COEF,) + field, bf16),
            pltpu.VMEM((REDUCED * channels, edge_rows), f32),
            pltpu.VMEM((edge_rows, REDUCED * channels), bf16),
            pltpu.VMEM((2 * group, channels, channels), bf16),
            pltpu.VMEM((REDUCED,) + field, bf16),
            copies,
            two_copies,
        ],
        input_output_aliases={2: 0},
        compiler_params=LARGE,
    )(first, ids, spill, rotation, maps)
    sums_shape = (group, -(-(used + tail_rows) // 16) * 16, channels)
    nodes_shape = jax.ShapeDtypeStruct((harmonics, row_count, channels), bf16)
    batch_scale = 1.0 / (2 * columns)
    if beside:
        grad_sums = pl.pallas_call(
            functools.partial(tail_kernel, used, share, head_count),
            out_shape=jax.ShapeDtypeStruct(sums_shape, bf16),
            in_specs=[VMEM, HBM],
            out_specs=VMEM,
            scratch_shapes=[
                pltpu.VMEM((padded, depth), f32),
                pltpu.VMEM((head_count, channels), f32),
                two_copies,
            ],
            compiler_params=LARGE,
        )(zero_parts, spill)
        last = exchange(grad_sums, GRAPH)
        grad_nodes, grad_zero, grad_att = pl.pallas_call(
            functools.partial(last_kernel, batch_scale),
            out_shape=(
                nodes_shape,
                jax.ShapeDtypeStruct((share, inner), f32),
                jax.ShapeDtypeStruct((head_count, channels), f32),
            ),
            in_specs=[VMEM],
            out_specs=[VMEM] * 3,
            scratch_shapes=[pltpu.VMEM(last.shape[1:], f32)],
            compiler_params=SMALL,
        )(last)
        grad_zero, grad_att = grad_zero.T, grad_att.T
    else:
        zero_sum = jnp.sum(zero_parts.astype(f32), axis=0)
        att = zero_sum[share : share + 2].reshape(-1)[: head_count * channels]
        zero_send = jnp.transpose(zero_sum[:share].reshape(share, group, inner), (1, 0, 2))
        zero_send = jnp.pad(zero_send, ((0, 0), (0, 0), (0, lanes - inner)))
        zero_send = zero_send.reshape(group, share * lanes // LANES, LANES)
        att = jnp.broadcast_to(
            att.reshape(1, head_count, channels), (group, head_count, channels)
        )
        last_rows = jnp.concatenate([zero_send, att], axis=1).astype(bf16)
        grad_sums = spill[SUM_START : SUM_START + 2 * group].reshape(2, group, channels, channels)
        grad_sums = jnp.transpose(grad_sums, (1, 0, 2, 3)).reshape(group, 2 * channels, channels)
        rest = jnp.zeros(sums_shape, bf16)
        grad_sums = lax.dynamic_update_slice(rest, grad_sums[:, :used], (0, 0, 0))
        grad_sums = lax.dynamic_update_slice(grad_sums, last_rows, (0, used, 0))
        last = exchange(grad_sums, GRAPH)
        grad_nodes, tail = pl.pallas_call(
            sum_kernel,
            out_shape=(nodes_shape, jax.ShapeDtypeStruct((tail_rows, channels), f32)),
            in_specs=[VMEM],
            out_specs=[VMEM] * 2,
            scratch_shapes=[pltpu.VMEM(last.shape[1:], f32)],
            compiler_params=SMALL,
        )(last)
        tail = tail * batch_scale
        zero_rows = share * lanes // LANES
        grad_zero = tail[:zero_rows].reshape(share, lanes)[:, :inner].T
        grad_att = tail[zero_rows:].T
    update = summed[:used].reshape(harmonics, row_count, channels)
    update = jnp.transpose(jnp.where(present[None], update, 0.0).astype(bf16), (1, 0, 2))
    grad_nodes = jnp.transpose(grad_nodes, (1, 0, 2))

    shape = (1, row_count, harmonics, channels)
    return (update.reshape(shape), grad_nodes.reshape(shape), grad_zero, grad_att)


def solution(mesh):
    columns, group = mesh.shape["dp"], mesh.shape["graph"]
    devices = mesh.devices.reshape(2, columns // 4, 2, group // 2, 2)
    fine = Mesh(devices, DP + GRAPH)
    in_specs = (
        P(DP, GRAPH, None, None),
        P(DP),
        P(DP, GRAPH),
        P(DP, GRAPH),
        P(DP, GRAPH),
        P(DP, None, None, GRAPH),
        P(DP, GRAPH, None, None),
        P(GRAPH, DP),
        P(GRAPH, DP),
        P(GRAPH, DP),
        P(GRAPH, DP),
        P(GRAPH, DP),
        P(),
    )
    out_specs = (P(DP, GRAPH, None, None), P(DP, GRAPH, None, None), P(GRAPH, DP), P())
    return jax.shard_map(
        on_device, mesh=fine, in_specs=in_specs, out_specs=out_specs, check_vma=False
    )
```
